256 devices in a mesh: frame: 32 (over z, x_lo, core), head: 8 (over x_hi, y).
Axes of the slice: x: 4 (x_hi: 2, x_lo: 2; x = x_hi * 2 + x_lo), y: 4, z: 8, core: 2. Of those that a mesh axis runs over, the one named last changes fastest.
Arguments:
- query: bfloat16 [4096, 3072], P('frame', 'head'), may hold values from -7 to 7
- key: bfloat16 [4096, 3072], P('frame', 'head'), may hold values from -6 to 6
- value: bfloat16 [4096, 3072], P('frame', 'head'), may hold values from -6 to 6
- out_weight: bfloat16 [3072, 6144], P('head'), may hold values from -0.109375 to 0.109375
- gate_table: float32 [16, 6144], P(None, 'head'), may hold values from -4 to 4
- grad_out: bfloat16 [4096, 6144], P('frame', 'head'), may hold values from -6 to 6
- span_ids: int32 [4096], P('frame'), may hold values from 0 to 63, never falling along the last dimension, each value on 1 to 256 neighbouring positions
- span_mask: int32 [64, 64], replicated, may hold values from 0 to 1, as said below
- span_step: int32 [64], replicated, may hold values from 0 to 15
Outputs:
- d_query: bfloat16 [4096, 3072], P('frame', 'head')
- d_key: bfloat16 [4096, 3072], P('frame', 'head')
- d_value: bfloat16 [4096, 3072], P('frame', 'head')
- d_gate: float32 [16, 6144], P(None, 'head')
The draws below stay inside these ranges and needn't reach their ends.
Inputs may be any that keep to these rules, and one draw needn't show every extreme that they name: `span_ids`: never falling along the tokens; every span holds 1 to 256 consecutive tokens, one exactly 256. `span_mask`: 1 on the diagonal, 0 above it.
All inputs are finite; a program needn't handle non-finite values.
Results may differ from the reference program's by a relative error of at most 0.025.
Values may be sent and summed in bfloat16 or wider, within the bound.
No kernel may reach another device: no remote copies, remote signals or barrier semaphores. Data moves between devices by JAX's collectives and lax.ppermute only.
A program may use at most 64 MiB of HBM per device.

```python
import math
import jax
import jax.numpy as jnp
import numpy as np
from jax import lax

D = 6144
HEADS = 24
HDIM = 128
STEPS = 16
TOK_DEV = 128
TOKENS = 4096
F = 3072
SPANS = 64


def draw_query(key, part):
    key = jax.random.fold_in(key, 1)
    base = jnp.clip(jax.random.normal(key, (TOKENS, F), jnp.float32), -6.0, 6.0)
    return base.astype(jnp.bfloat16)


def draw_key(key, part):
    key = jax.random.fold_in(key, 2)
    base = jnp.clip(jax.random.normal(key, (TOKENS, F), jnp.float32), -6.0, 6.0)
    return base.astype(jnp.bfloat16)


def draw_span_mask(key, part):
    key = jax.random.fold_in(key, 5)
    earlier = jax.random.randint(key, (SPANS, SPANS), 0, 4) > 0
    rows_at = jnp.arange(SPANS)[:, None]
    cols_at = jnp.arange(SPANS)[None, :]
    return jnp.where(rows_at == cols_at, 1, jnp.where((cols_at < rows_at) & earlier, 1, 0)).astype(jnp.int32)


def with_ends(entries, key, least, high):
    longest = entries.shape.index(max(entries.shape))
    spots = []
    for shift in (0, 1):
        where = [jax.random.randint(jax.random.fold_in(key, axis), (), 0, length) for axis, length in enumerate(entries.shape)]
        where[longest] = (where[longest] + shift) % entries.shape[longest]
        spots.append(tuple(where))
    return entries.at[spots[0]].set(least).at[spots[1]].set(high)


def levels(stream_key, shape, shards, least, high):
    def one(dim, blocks):
        draws = jax.random.uniform(jax.random.fold_in(jax.random.fold_in(stream_key, 6), dim), (blocks,), jnp.float32, least / len(shards), high / len(shards))
        return jnp.repeat(jnp.exp(draws), shape[dim] // blocks).reshape((-1,) + (1,) * (len(shape) - dim - 1))

    factor_of = one(*shards[0])
    for cut in shards[1:]:
        factor_of = factor_of * one(*cut)
    return factor_of


def profile(amount, total, bound, slope):
    portions = [(1 << 20) // math.isqrt(rank ** slope) + 1 for rank in range(2, amount + 1)]
    surplus, counts = total - bound - (amount - 1), [1] * (amount - 1)
    while surplus > 0:
        free = [i for i in range(amount - 1) if counts[i] < bound]
        mass, budget = sum([portions[i] for i in free]), surplus
        for i in free:
            more = min(bound - counts[i], max(1, budget * portions[i] // mass), surplus)
            counts[i] = counts[i] + more
            surplus = surplus - more
    return np.array([bound] + counts)


def ragged(rng, number_of, total, limit, lean):
    if number_of == 2:
        one = jax.random.randint(rng, (), max(1, total - limit), min(limit, total - 1) + 1)
        return jnp.stack([one, total - one])
    lengths = jnp.asarray(profile(number_of, total, limit, lean), jnp.int32)
    pairs = (number_of - 1) // 2
    source_of, taker = lengths[1:1 + 2 * pairs:2], lengths[2:2 + 2 * pairs:2]
    room = jnp.minimum(source_of - 1, limit - taker)
    passed = jax.random.randint(jax.random.fold_in(rng, 1), (pairs,), 0, 1 << 20) % (room + 1)
    lengths = lengths.at[1:1 + 2 * pairs:2].set(source_of - passed).at[2:2 + 2 * pairs:2].set(taker + passed)
    return lengths[jax.random.permutation(jax.random.fold_in(rng, 2), number_of)]


def noise(key, shape, width, limit, cuts=(), held_as=jnp.bfloat16):
    values = width * jax.random.normal(key, shape, jnp.float32)
    if cuts:
        values = values * levels(key, shape, cuts, -0.22, 0.18)
    return jnp.clip(values, -limit, limit).astype(held_as)


def setup_inputs(seed: int = 0) -> dict:
    streams_of = jax.random.split(jax.random.key(seed), 10)
    query = draw_query(jax.random.fold_in(streams_of[9], 71), 0)
    key = draw_key(jax.random.fold_in(streams_of[9], 71), 0)
    value = noise(streams_of[2], (TOKENS, F), 1.0, 6.0, ((0, 32), (1, 8)))
    out_weight = noise(streams_of[3], (F, D), F ** -0.5, 0.109375, ((0, 8),))
    gate_table = noise(streams_of[4], (STEPS, D), 1.0, 4.0, ((1, 8),), jnp.float32)
    grad_out = noise(streams_of[5], (TOKENS, D), 1.0, 6.0, ((0, 32), (1, 8)))
    span_ids = jnp.searchsorted(jnp.cumsum(ragged(streams_of[6], SPANS, TOKENS, 2 * TOK_DEV, 2)), jnp.arange(TOKENS), side="right").astype(jnp.int32)
    span_mask = draw_span_mask(jax.random.fold_in(streams_of[9], 71), 0)
    span_step = with_ends(jax.random.randint(streams_of[8], (SPANS,), 0, STEPS), jax.random.fold_in(streams_of[8], 1), 0, STEPS - 1).astype(jnp.int32)
    return dict(query=query, key=key, value=value, out_weight=out_weight, gate_table=gate_table, grad_out=grad_out, span_ids=span_ids, span_mask=span_mask, span_step=span_step)


NEG_FILL = -1.0e30


def reference(query, key, value, out_weight, gate_table, grad_out, span_ids, span_mask, span_step):
    scale = HDIM ** -0.5
    allowed = span_mask[span_ids][:, span_ids] == 1

    def split_heads(array):
        return array.reshape(TOKENS, HEADS, HDIM).transpose(1, 0, 2)

    def forward_head(operands):
        q_head, k_head, v_head = operands
        scores = jnp.dot(q_head, k_head.T, preferred_element_type=jnp.float32) * scale
        scores = jnp.where(allowed, scores, NEG_FILL)
        top = jnp.max(scores, axis=1)
        lse = top + jnp.log(jnp.sum(jnp.exp(scores - top[:, None]), axis=1))
        weights = jnp.exp(scores - lse[:, None]).astype(jnp.bfloat16)
        attn = jnp.dot(weights, v_head, preferred_element_type=jnp.float32).astype(jnp.bfloat16)
        return attn, lse

    q_heads = split_heads(query)
    k_heads = split_heads(key)
    v_heads = split_heads(value)
    attn, lse = lax.map(forward_head, (q_heads, k_heads, v_heads))
    attn_rows = attn.transpose(1, 0, 2).reshape(TOKENS, F)
    proj = jnp.dot(attn_rows, out_weight, preferred_element_type=jnp.float32)
    tok_step = span_step[span_ids]
    gate_tok = gate_table[tok_step]
    d_gate = jax.ops.segment_sum(grad_out.astype(jnp.float32) * proj, tok_step, num_segments=STEPS)
    d_proj = (grad_out.astype(jnp.float32) * gate_tok).astype(jnp.bfloat16)
    d_attn = jnp.dot(d_proj, out_weight.T, preferred_element_type=jnp.float32).astype(jnp.bfloat16)
    delta = (d_attn.astype(jnp.float32) * attn_rows.astype(jnp.float32)).reshape(TOKENS, HEADS, HDIM)
    delta = jnp.sum(delta, axis=2).T
    d_heads = split_heads(d_attn)

    def backward_head(operands):
        q_head, k_head, v_head, d_head, lse_head, delta_head = operands
        scores = jnp.dot(q_head, k_head.T, preferred_element_type=jnp.float32) * scale
        scores = jnp.where(allowed, scores, NEG_FILL)
        probs = jnp.exp(scores - lse_head[:, None])
        dprob = jnp.dot(d_head, v_head.T, preferred_element_type=jnp.float32)
        dscore = (probs * (dprob - delta_head[:, None])).astype(jnp.bfloat16)
        grad_q = (jnp.dot(dscore, k_head, preferred_element_type=jnp.float32) * scale).astype(jnp.bfloat16)
        grad_k = (jnp.dot(dscore.T, q_head, preferred_element_type=jnp.float32) * scale).astype(jnp.bfloat16)
        grad_v = jnp.dot(probs.astype(jnp.bfloat16).T, d_head, preferred_element_type=jnp.float32).astype(jnp.bfloat16)
        return grad_q, grad_k, grad_v

    grad_q, grad_k, grad_v = lax.map(backward_head, (q_heads, k_heads, v_heads, d_heads, lse, delta))

    def join_heads(array):
        return array.transpose(1, 0, 2).reshape(TOKENS, F)

    return join_heads(grad_q), join_heads(grad_k), join_heads(grad_v), d_gate
```

```python
import math

import jax
import jax.numpy as jnp
from jax import lax
from jax.experimental import pallas as pl
from jax.experimental.pallas import tpu as pltpu
from jax.sharding import Mesh, PartitionSpec as P

HDIM = 128
BIG = 1e30
SCALE = HDIM ** (-0.5)
LOG2E = math.log2(math.e)
C2 = SCALE * LOG2E
FRAME = ("z", "xl", "core")
HEAD = ("xh", "y")
FRAME_C = ("xl", "core")
NT = (((1,), (1,)), ((), ()))
NN = (((1,), (0,)), ((), ()))
F32 = jnp.float32
BF16 = jnp.bfloat16
VMEM_LIMIT = 48 * 1024 * 1024


def dot(a, b, dims):
    return lax.dot_general(a, b, dims, preferred_element_type=F32)


def swap(block, axes, count, by):
    return lax.ppermute(block, axes, [(i, i ^ by) for i in range(count)])


def call(kernel, out_shape, scratch=(), flops=0, nbytes=0, smem=0):
    def run(*args):
        specs = [pl.BlockSpec(memory_space=pltpu.SMEM)] * smem
        specs += [pl.BlockSpec(memory_space=pltpu.VMEM)] * (len(args) - smem)
        return pl.pallas_call(
            kernel,
            out_shape=out_shape,
            in_specs=specs,
            out_specs=jax.tree.map(lambda _: pl.BlockSpec(memory_space=pltpu.VMEM), out_shape),
            scratch_shapes=list(scratch),
            compiler_params=pltpu.CompilerParams(vmem_limit_bytes=VMEM_LIMIT),
            cost_estimate=pl.CostEstimate(flops=flops, bytes_accessed=nbytes, transcendentals=0),
        )(*args)

    return run


def shape(rows, cols, dtype=BF16):
    return jax.ShapeDtypeStruct((rows, cols), dtype)


def prep_kernel(key, value, query, grad, gate, ids, mask, step, kv, bias, tok_step, sent):
    rows, width = key.shape
    spans = mask.shape[0]
    levels = gate.shape[0]
    hot_t = (lax.broadcasted_iota(jnp.int32, (rows, rows), 0) == ids[...]).astype(F32)
    hot = hot_t.T.astype(BF16)
    kv[:, :width] = key[...]
    kv[:, width : 2 * width] = value[...]
    kv[:, 2 * width :] = hot
    table = jnp.where(mask[...] == 1, 0.0, -BIG).astype(BF16)
    bias[...] = jnp.zeros_like(bias)
    bias[:, :spans] = dot(hot[:, :spans], table, NN).astype(BF16)
    step_t = (lax.broadcasted_iota(jnp.int32, (levels, spans), 0) == step[...]).astype(BF16)
    tok_step[...] = dot(hot[:, :spans], step_t, NT).astype(BF16)
    sent[:rows, :] = grad[...]
    sent[rows:, :] = gate[...].astype(BF16)


def dattn_kernel(me, *refs):
    blocks = refs[:8]
    tok_step, weight, query, bias, out, w_vmem, sems = refs[8:]
    rows, width = query.shape
    cols = blocks[0].shape[1]
    copies = []
    for e in range(8):
        at = pl.multiple_of((me[0] ^ e) * cols, cols)
        copy = pltpu.make_async_copy(weight.at[:, pl.ds(at, cols)], w_vmem.at[e], sems.at[e])
        copy.start()
        copies.append(copy)
    acc = jnp.zeros((rows, width), F32)
    for e in range(8):
        gate_tok = dot(tok_step[...], blocks[e][rows:, :], NN)
        d_proj = (blocks[e][:rows, :].astype(F32) * gate_tok).astype(BF16)
        copies[e].wait()
        acc += dot(d_proj, w_vmem[e], NT)
    out[:, :width] = query[...]
    out[:, width : 2 * width] = acc.astype(BF16)
    out[:, 2 * width :] = bias[...]


def split3(x):
    hi = x.astype(BF16)
    rest = x - hi.astype(F32)
    mid = rest.astype(BF16)
    low = (rest - mid.astype(F32)).astype(BF16)
    return hi, mid, low


def fwd_kernel(kv, q0, q1, q2, q3, s0, s1, s2, s3, qd, stats):
    rows = q0.shape[0]
    width = (q0.shape[1] - HDIM) // 2
    heads = width // HDIM
    for d, q in enumerate((q0, q1, q2, q3)):
        qd[d * rows : (d + 1) * rows, :] = q[...]
    outs = (s0, s1, s2, s3)
    step = 2 * rows
    for part in range(2):
        here = slice(part * step, (part + 1) * step)
        bias = dot(kv[:, 2 * width :], qd[here, 2 * width :], NT)
        for h in range(heads):
            cols = slice(h * HDIM, (h + 1) * HDIM)
            vcols = slice(width + h * HDIM, width + (h + 1) * HDIM)
            scores = dot(kv[:, cols], qd[here, cols], NT) + bias
            top = jnp.max(scores, axis=0, keepdims=True)
            probs = jnp.exp2((scores - top) * C2)
            total = jnp.sum(probs, axis=0, keepdims=True)
            dprob = dot(kv[:, vcols], qd[here, vcols], NT)
            corr = jnp.sum(probs * dprob, axis=0, keepdims=True)
            acc = dot(kv[:, vcols].T, probs.astype(BF16), NN)
            for i in range(2):
                d = 2 * part + i
                lanes = slice(i * rows, (i + 1) * rows)
                outs[d][cols, :] = acc[:, lanes].astype(BF16)
                for n, stat in enumerate((top, total, corr)):
                    stats[d * 16 + n * heads + h : d * 16 + n * heads + h + 1, :] = stat[:, lanes]
    pieces = split3(stats[...])
    for out in outs:
        for n in range(3):
            out[width + n * 64 : width + (n + 1) * 64, :] = pieces[n]


def merge_kernel(s0, s1, s2, s3, lse, delta, attn_t):
    heads = 3
    width = attn_t.shape[0]
    rows = attn_t.shape[1]
    got = []
    for s in (s0, s1, s2, s3):
        got.append(
            s[width : width + 64, :].astype(F32)
            + s[width + 64 : width + 128, :].astype(F32)
            + s[width + 128 : width + 192, :].astype(F32)
        )
    for b in range(4):
        mine = [got[e][16 * (b ^ e) : 16 * (b ^ e) + 16, :] for e in range(4)]
        tops = [m[0:heads] for m in mine]
        top = jnp.maximum(jnp.maximum(tops[0], tops[1]), jnp.maximum(tops[2], tops[3]))
        ws = [jnp.exp2((t - top) * C2) for t in tops]
        total = sum(w * m[heads : 2 * heads] for w, m in zip(ws, mine))
        corr = sum(w * m[2 * heads : 3 * heads] for w, m in zip(ws, mine))
        lse[8 * b : 8 * b + heads, :] = top * C2 + jnp.log(total) * LOG2E
        delta[8 * b : 8 * b + heads, :] = corr / total
        if b == 0:
            for h in range(heads):
                cols = slice(h * HDIM, (h + 1) * HDIM)
                acc = jnp.zeros((HDIM, rows), F32)
                for w, s in zip(ws, (s0, s1, s2, s3)):
                    acc += s[cols, :].astype(F32) * (w[h : h + 1] / total[h : h + 1])
                attn_t[cols, :] = acc.astype(BF16)


def bwd_kernel(kv, q0, q1, q2, q3, lse, delta, dkv, g0, g1, g2, g3, qd):
    rows = q0.shape[0]
    width = (q0.shape[1] - HDIM) // 2
    heads = width // HDIM
    for d, q in enumerate((q0, q1, q2, q3)):
        qd[d * rows : (d + 1) * rows, :] = q[...]
    outs = (g0, g1, g2, g3)
    step = 2 * rows
    biases = [
        dot(kv[:, 2 * width :], qd[p * step : (p + 1) * step, 2 * width :], NT) for p in range(2)
    ]
    for h in range(heads):
        cols = slice(h * HDIM, (h + 1) * HDIM)
        vcols = slice(width + h * HDIM, width + (h + 1) * HDIM)
        keys_t = kv[:, cols].T
        dkey = None
        dval = None
        for part in range(2):
            here = slice(part * step, (part + 1) * step)
            d = 2 * part
            row = lambda ref: jnp.concatenate(
                [ref[8 * d + h : 8 * d + h + 1, :], ref[8 * d + 8 + h : 8 * d + 9 + h, :]], axis=1
            )
            scores = dot(kv[:, cols], qd[here, cols], NT) + biases[part]
            probs = jnp.exp2(scores * C2 - row(lse))
            dprob = dot(kv[:, vcols], qd[here, vcols], NT)
            dscore = (probs * (dprob - row(delta))).astype(BF16)
            dk = dot(dscore, qd[here, cols], NN)
            dv = dot(probs.astype(BF16), qd[here, vcols], NN)
            dkey = dk if dkey is None else dkey + dk
            dval = dv if dval is None else dval + dv
            dq = dot(keys_t, dscore, NN) * SCALE
            outs[d][cols, :] = dq[:, :rows].astype(BF16)
            outs[d + 1][cols, :] = dq[:, rows:].astype(BF16)
        dkv[:, cols] = (dkey * SCALE).astype(BF16)
        dkv[:, vcols] = dval.astype(BF16)


def dquery_kernel(g0, g1, g2, g3, out):
    acc = g0[...].astype(F32) + g1[...].astype(F32) + g2[...].astype(F32) + g3[...].astype(F32)
    out[...] = acc.T.astype(BF16)


def dgate_kernel(me, *refs):
    blocks = refs[:8]
    tok_step, weight, attn_t, out, w_vmem, sems = refs[8:]
    rows = attn_t.shape[1]
    levels = tok_step.shape[1]
    cols = blocks[0].shape[1]
    copies = []
    for e in range(8):
        at = pl.multiple_of((me[0] ^ e) * cols, cols)
        copy = pltpu.make_async_copy(weight.at[:, pl.ds(at, cols)], w_vmem.at[e], sems.at[e])
        copy.start()
        copies.append(copy)
    attn = attn_t[...].astype(F32).T.astype(BF16)
    steps_t = tok_step[...].astype(F32).T
    for e in range(8):
        copies[e].wait()
        proj = dot(attn, w_vmem[e], NN)
        terms = proj * blocks[e][:rows, :].astype(F32)
        high = terms.astype(BF16)
        low = (terms - high.astype(F32)).astype(BF16)
        hot = steps_t.astype(BF16)
        out[e * levels : (e + 1) * levels, :] = (dot(hot, high, NN) + dot(hot, low, NN)).astype(BF16)


def body(query, key, value, out_weight, gate_table, grad_out, span_ids, span_mask, span_step):
    rows, width = query.shape
    levels, gcols = gate_table.shape
    me = (lax.axis_index("xh") * 4 + lax.axis_index("y")).astype(jnp.int32).reshape(1)
    wide = 2 * width + HDIM
    kv, bias, tok_step, sent = call(
        prep_kernel,
        (shape(rows, wide), shape(rows, HDIM), shape(rows, levels), shape(rows + levels, gcols)),
    )(key, value, query, grad_out, gate_table, span_ids.reshape(1, rows), span_mask,
      span_step.reshape(1, -1))
    kv_all = lax.all_gather(kv, "z", axis=0, tiled=True)
    blocks = [sent] + [swap(sent, HEAD, 8, e) for e in range(1, 8)]

    def weighted(kernel, out_shape, args, flops):
        specs = [pl.BlockSpec(memory_space=pltpu.SMEM)]
        specs += [pl.BlockSpec(memory_space=pltpu.VMEM)] * 9
        specs += [pl.BlockSpec(memory_space=pl.ANY)]
        specs += [pl.BlockSpec(memory_space=pltpu.VMEM)] * (len(args) - 11)
        return pl.pallas_call(
            kernel,
            out_shape=out_shape,
            in_specs=specs,
            out_specs=pl.BlockSpec(memory_space=pltpu.VMEM),
            scratch_shapes=[
                pltpu.VMEM((8, width, gcols), BF16),
                pltpu.SemaphoreType.DMA((8,)),
            ],
            compiler_params=pltpu.CompilerParams(vmem_limit_bytes=VMEM_LIMIT),
            cost_estimate=pl.CostEstimate(
                flops=flops, bytes_accessed=out_weight.size * 2, transcendentals=0
            ),
        )(*args)

    flops = 2 * rows * out_weight.size
    qd = weighted(
        dattn_kernel, shape(rows, wide), (me, *blocks, tok_step, out_weight, query, bias), flops
    )
    qds = [qd] + [swap(qd, FRAME_C, 4, d) for d in range(1, 4)]
    tall = width + 192
    parts = call(
        fwd_kernel,
        tuple(shape(tall, rows) for _ in range(4)),
        scratch=(pltpu.VMEM((4 * rows, wide), BF16), pltpu.VMEM((64, rows), F32)),
        flops=3 * 2 * 8 * rows * 4 * rows * width,
        nbytes=kv_all.size * 2,
    )(kv_all, *qds)
    sums = [parts[0]] + [swap(parts[d], FRAME_C, 4, d) for d in range(1, 4)]
    lse, delta, attn_t = call(
        merge_kernel, (shape(32, rows, F32), shape(32, rows, F32), shape(width, rows))
    )(*sums)
    dkv, g0, g1, g2, g3 = call(
        bwd_kernel,
        (shape(8 * rows, 2 * width),) + tuple(shape(width, rows) for _ in range(4)),
        scratch=(pltpu.VMEM((4 * rows, wide), BF16),),
        flops=5 * 2 * 8 * rows * 4 * rows * width,
        nbytes=kv_all.size * 2,
    )(kv_all, *qds, lse, delta)
    dkv_own = lax.psum_scatter(dkv, "z", scatter_dimension=0, tiled=True)
    back = [g0] + [swap(g, FRAME_C, 4, d) for d, g in ((1, g1), (2, g2), (3, g3))]
    d_query = call(dquery_kernel, shape(rows, width))(*back)
    terms = weighted(
        dgate_kernel,
        shape(8 * levels, gcols),
        (me, *blocks, tok_step, out_weight, attn_t),
        flops,
    )
    for by in (4, 2, 1):
        half = by * levels
        terms = terms[:half].astype(F32) + swap(terms[half:], HEAD, 8, by).astype(F32)
        terms = terms.astype(BF16)
    total = terms.astype(F32)
    for by in (1, 2, 4, 8, 16):
        total = total + swap(total, FRAME, 32, by)
    return (d_query, dkv_own[:, :width], dkv_own[:, width:], total)


def solution(mesh):
    fine = Mesh(mesh.devices.reshape(8, 2, 2, 2, 4), FRAME + HEAD)
    both = P(FRAME, HEAD)
    return jax.shard_map(
        body,
        mesh=fine,
        in_specs=(both, both, both, P(HEAD, None), P(None, HEAD), both, P(FRAME), P(), P()),
        out_specs=(both, both, both, P(None, HEAD)),
        check_vma=False,
    )
```

```python
import functools
import math

import jax
import jax.numpy as jnp
from jax import lax
from jax.experimental import pallas as pl
from jax.experimental.pallas import tpu as pltpu
from jax.sharding import Mesh, PartitionSpec as P

HDIM = 128
BIG = 1e30
SCALE = HDIM ** (-0.5)
LOG2E = math.log2(math.e)
C2 = SCALE * LOG2E
Z = ("zh", "zl")
FRAME = ("zh", "zl", "xl", "core")
HEAD = ("xh", "y")
FRAME_C = ("xl", "core")
NT = (((1,), (1,)), ((), ()))
NN = (((1,), (0,)), ((), ()))
F32 = jnp.float32
BF16 = jnp.bfloat16
MIB = 1024 * 1024
VMEM_LIMIT = 40 * MIB


def dot(a, b, dims):
    return lax.dot_general(a, b, dims, preferred_element_type=F32)


def swap(block, axes, count, by):
    return lax.ppermute(block, axes, [(i, i ^ by) for i in range(count)])


def call(kernel, out_shape, scratch=(), flops=0, nbytes=0, limit=40):
    def run(*args):
        specs = [pl.BlockSpec(memory_space=pltpu.VMEM)] * len(args)
        return pl.pallas_call(
            kernel,
            out_shape=out_shape,
            in_specs=specs,
            out_specs=jax.tree.map(lambda _: pl.BlockSpec(memory_space=pltpu.VMEM), out_shape),
            scratch_shapes=list(scratch),
            compiler_params=pltpu.CompilerParams(vmem_limit_bytes=limit * MIB),
            cost_estimate=pl.CostEstimate(flops=flops, bytes_accessed=nbytes, transcendentals=0),
        )(*args)

    return run


def shape(rows, cols, dtype=BF16):
    return jax.ShapeDtypeStruct((rows, cols), dtype)


def prep_kernel(key, value, query, grad, gate, ids, mask, step, kv, qb, tok_step, sent):
    rows, width = key.shape
    spans = mask.shape[0]
    levels = gate.shape[0]
    hot_t = (lax.broadcasted_iota(jnp.int32, (rows, rows), 0) == ids[...]).astype(F32)
    hot = hot_t.T.astype(BF16)
    kv[:, :width] = key[...]
    kv[:, width : 2 * width] = value[...]
    kv[:, 2 * width :] = hot
    table = jnp.where(mask[...] == 1, 0.0, -BIG).astype(BF16)
    qb[:, :width] = query[...]
    qb[:, width:] = jnp.zeros((rows, HDIM), BF16)
    qb[:, width : width + spans] = dot(hot[:, :spans], table, NN).astype(BF16)
    step_t = (lax.broadcasted_iota(jnp.int32, (levels, spans), 0) == step[...]).astype(BF16)
    tok_step[...] = dot(hot[:, :spans], step_t, NT).astype(BF16)
    sent[:rows, :] = grad[...]
    sent[rows:, :] = gate[...].astype(BF16)


def fetch_weight(me, weight, w_vmem, sems, cols):
    copies = []
    for e in range(8):
        at = pl.multiple_of((me[0] ^ e) * cols, cols)
        copy = pltpu.make_async_copy(weight.at[:, pl.ds(at, cols)], w_vmem.at[e], sems.at[e])
        copy.start()
        copies.append(copy)
    return copies


def by_head(own, y1, y3, y2_near, y2_far):
    tall = y2_near.shape[0]
    low, high = pl.ds(0, tall), pl.ds(tall, tall)
    return [
        own.at[low], y1.at[low], y2_near, y3.at[low],
        own.at[high], y1.at[high], y2_far, y3.at[high],
    ]


def dattn_kernel(me, *refs):
    blocks = by_head(*refs[:5])
    tok_step, weight, out, w_vmem, sems = refs[5:]
    rows, width = out.shape
    copies = fetch_weight(me, weight, w_vmem, sems, blocks[0].shape[1])
    acc = jnp.zeros((rows, width), F32)
    for e in range(8):
        gate_tok = dot(tok_step[...], blocks[e][rows:, :], NN)
        d_proj = (blocks[e][:rows, :].astype(F32) * gate_tok).astype(BF16)
        copies[e].wait()
        acc += dot(d_proj, w_vmem[e], NT)
    out[...] = acc.astype(BF16)


def split3(x):
    hi = x.astype(BF16)
    rest = x - hi.astype(F32)
    mid = rest.astype(BF16)
    low = (rest - mid.astype(F32)).astype(BF16)
    return hi, mid, low


def fwd_kernel(k0, k1, k2, k3, k4, k5, k6, k7, q0, q1, q2, q3, s0, s1, s2, s3, kv, qd, stats):
    rows = q0.shape[0]
    width = q0.shape[1] - HDIM
    heads = width // HDIM
    for i, k in enumerate((k0, k1, k2, k3, k4, k5, k6, k7)):
        kv[i * rows : (i + 1) * rows, :] = k[...]
    for d, q in enumerate((q0, q1, q2, q3)):
        qd[d * rows : (d + 1) * rows, :] = q[...]
    stats[...] = jnp.zeros_like(stats)
    outs = (s0, s1, s2, s3)
    step = 2 * rows
    hot = kv[:, 2 * width :]
    for part in range(2):
        here = slice(part * step, (part + 1) * step)
        bias = dot(hot, qd[here, width:], NT)
        for h in range(heads):
            cols = slice(h * HDIM, (h + 1) * HDIM)
            vcols = slice(width + h * HDIM, width + (h + 1) * HDIM)
            keys = kv[:, cols]
            vals = kv[:, vcols]
            scores = dot(keys, qd[here, cols], NT) + bias
            top = jnp.max(scores, axis=0, keepdims=True)
            probs = jnp.exp2((scores - top) * C2)
            total = jnp.sum(probs, axis=0, keepdims=True)
            acc = dot(vals.T, probs.astype(BF16), NN)
            for i in range(2):
                d = 2 * part + i
                lanes = slice(i * rows, (i + 1) * rows)
                outs[d][cols, :] = acc[:, lanes].astype(BF16)
                stats[d * 8 + h : d * 8 + h + 1, :] = top[:, lanes]
                stats[d * 8 + heads + h : d * 8 + heads + h + 1, :] = total[:, lanes]
    for d, out in enumerate(outs):
        pieces = split3(stats[8 * d : 8 * d + 8, :])
        tail = jnp.concatenate([p.astype(F32) for p in pieces] + [jnp.zeros((8, rows), F32)], axis=0)
        out[width:, :] = tail.astype(BF16)


def merge_kernel(s0, s1, s2, s3, d_attn, attn_t, sent):
    width, rows = attn_t.shape
    heads = width // HDIM
    parts = (s0, s1, s2, s3)
    mine = []
    for s in parts:
        tail = s[width:, :].astype(F32)
        mine.append(tail[0:8] + tail[8:16] + tail[16:24])
    tops = [m[0:heads] for m in mine]
    top = jnp.maximum(jnp.maximum(tops[0], tops[1]), jnp.maximum(tops[2], tops[3]))
    ws = [jnp.exp2((t - top) * C2) for t in tops]
    total = sum(w * m[heads : 2 * heads] for w, m in zip(ws, mine))
    lse = top * C2 + jnp.log(total) * LOG2E
    dattn_t = d_attn[...].astype(F32).T
    deltas = []
    for h in range(heads):
        cols = slice(h * HDIM, (h + 1) * HDIM)
        acc = jnp.zeros((HDIM, rows), F32)
        for w, s in zip(ws, parts):
            acc += s[cols, :].astype(F32) * (w[h : h + 1] / total[h : h + 1])
        rounded = acc.astype(BF16)
        attn_t[cols, :] = rounded
        deltas.append(jnp.sum(rounded.astype(F32) * dattn_t[cols, :], axis=0, keepdims=True))
    stats = jnp.concatenate([lse] + deltas + [jnp.zeros((2, rows), F32)], axis=0)
    pieces = jnp.concatenate([p.astype(F32) for p in split3(stats)], axis=1)
    sent[:rows, :] = d_attn[...]
    sent[rows:, :] = jnp.concatenate([pieces, jnp.zeros_like(pieces)], axis=0).astype(BF16)


def bwd_kernel(count, last, *refs):
    ks = refs[:count]
    qs = refs[count : count + 4]
    owns = refs[count + 4 : count + 8]
    at = count + 8
    if last:
        before = refs[at]
        at += 1
    slots = refs[at : at + count]
    outs = refs[at + count : -4]
    kv, qd, ad, stats = refs[-4:]
    rows = qs[0].shape[0]
    width = qs[0].shape[1] - HDIM
    heads = width // HDIM
    for i, k in enumerate(ks):
        kv[i * rows : (i + 1) * rows, :] = k[...]
    for d, (q, a) in enumerate(zip(qs, owns)):
        lanes = slice(d * rows, (d + 1) * rows)
        qd[lanes, :] = q[...]
        ad[lanes, :] = a[:rows, :]
        tail = a[rows:, :].astype(F32)
        stats[:, lanes] = (tail[0:8, :rows] + tail[0:8, rows : 2 * rows]) + tail[0:8, 2 * rows :]
    step = 2 * rows
    hot = kv[:, 2 * width :]
    biases = [dot(hot, qd[p * step : (p + 1) * step, width:], NT) for p in range(2)]
    for h in range(heads):
        cols = slice(h * HDIM, (h + 1) * HDIM)
        vcols = slice(width + h * HDIM, width + (h + 1) * HDIM)
        keys = kv[:, cols]
        vals = kv[:, vcols]
        keys_t = keys.T
        dkey = None
        dval = None
        for part in range(2):
            here = slice(part * step, (part + 1) * step)
            d = 2 * part
            scores = dot(keys, qd[here, cols], NT) + biases[part]
            probs = jnp.exp2(scores * C2 - stats[h : h + 1, here])
            dprob = dot(vals, ad[here, cols], NT)
            dscore = (probs * (dprob - stats[heads + h : heads + h + 1, here])).astype(BF16)
            dk = dot(dscore, qd[here, cols], NN)
            dv = dot(probs.astype(BF16), ad[here, cols], NN)
            dkey = dk if dkey is None else dkey + dk
            dval = dv if dval is None else dval + dv
            dq = dot(keys_t, dscore, NN)
            if last:
                dq = (dq + before[cols, here]) * SCALE
                low_half = slice(h * HDIM, (h + 1) * HDIM)
                high_half = slice(width + h * HDIM, width + (h + 1) * HDIM)
                outs[part][low_half, :] = dq[:, :rows].astype(BF16)
                outs[part][high_half, :] = dq[:, rows:].astype(BF16)
            else:
                outs[0][cols, here] = dq
        for k, slot in enumerate(slots):
            here = slice(k * rows, (k + 1) * rows)
            slot[:, cols] = (dkey[here] * SCALE).astype(BF16)
            slot[:, vcols] = dval[here].astype(BF16)


def dquery_kernel(here, there, got, out):
    width = here.shape[0] // 2
    acc = here[:width, :].astype(F32) + there[:width, :].astype(F32) + got[...].astype(F32)
    out[...] = acc.T.astype(BF16)


def dgate_kernel(me, *refs):
    blocks = by_head(*refs[:5])
    tok_step, weight, attn_t, out, w_vmem, sems = refs[5:]
    rows = attn_t.shape[1]
    levels = tok_step.shape[1]
    copies = fetch_weight(me, weight, w_vmem, sems, blocks[0].shape[1])
    attn = attn_t[...].astype(F32).T.astype(BF16)
    hot = tok_step[...].astype(F32).T.astype(BF16)
    for e in range(8):
        copies[e].wait()
        proj = dot(attn, w_vmem[e], NN)
        terms = proj * blocks[e][:rows, :].astype(F32)
        high = terms.astype(BF16)
        low = (terms - high.astype(F32)).astype(BF16)
        out[e * levels : (e + 1) * levels, :] = (dot(hot, high, NN) + dot(hot, low, NN)).astype(BF16)


def body(query, key, value, out_weight, gate_table, grad_out, span_ids, span_mask, span_step):
    rows, width = query.shape
    levels, gcols = gate_table.shape
    me = (lax.axis_index("xh") * 4 + lax.axis_index("y")).astype(jnp.int32).reshape(1)
    wide = 2 * width + HDIM
    kv, qb, tok_step, sent = call(
        prep_kernel,
        (shape(rows, wide), shape(rows, width + HDIM), shape(rows, levels),
         shape(rows + levels, gcols)),
        limit=60,
    )(key, value, query, grad_out, gate_table, span_ids.reshape(1, rows), span_mask,
      span_step.reshape(1, -1))
    above = [(z, (z + 1) % 8) for z in range(8)]
    below = [(z, (z - 1) % 8) for z in range(8)]
    tall = rows + levels

    hold = lax.optimization_barrier
    u1, d1 = lax.ppermute(kv, Z, above), lax.ppermute(kv, Z, below)
    gx = swap(sent, "xh", 2, 1)
    qcore = swap(qb, "core", 2, 1)
    u1, d1, qcore = hold((u1, d1, qcore))
    u2, d2 = lax.ppermute(u1, Z, above), lax.ppermute(d1, Z, below)
    u2, d2, gx = hold((u2, d2, gx))
    u3, d3 = lax.ppermute(u2, Z, above), lax.ppermute(d2, Z, below)
    gown = jnp.concatenate([sent, gx], axis=0)
    gy1, gy3 = swap(gown, "y", 4, 1), swap(gown, "y", 4, 3)
    u3, d3 = hold((u3, d3))
    u4 = lax.ppermute(u3, Z, above)
    qxl, qdiag = swap(qb, "xl", 2, 1), swap(qcore, "xl", 2, 1)
    u4, qxl, qdiag, gy1, gy3 = hold((u4, qxl, qdiag, gy1, gy3))
    near, far = swap(gy1[:tall], "y", 4, 3), swap(gy3[tall:], "y", 4, 1)
    kvs = (kv, u1, u2, u3, u4, d1, d2, d3)
    qbs = (qb, qcore, qxl, qdiag)

    def weighted(kernel, out_shape, args, flops):
        specs = [pl.BlockSpec(memory_space=pltpu.SMEM)]
        specs += [pl.BlockSpec(memory_space=pltpu.VMEM)] * 6
        specs += [pl.BlockSpec(memory_space=pl.ANY)]
        specs += [pl.BlockSpec(memory_space=pltpu.VMEM)] * (len(args) - 8)
        return pl.pallas_call(
            kernel,
            out_shape=out_shape,
            in_specs=specs,
            out_specs=pl.BlockSpec(memory_space=pltpu.VMEM),
            scratch_shapes=[
                pltpu.VMEM((8, width, gcols), BF16),
                pltpu.SemaphoreType.DMA((8,)),
            ],
            compiler_params=pltpu.CompilerParams(vmem_limit_bytes=VMEM_LIMIT),
            cost_estimate=pl.CostEstimate(
                flops=flops, bytes_accessed=out_weight.size * 2, transcendentals=0
            ),
        )(*args)

    flops = 2 * rows * out_weight.size
    product = 2 * 8 * rows * 4 * rows * width
    parts = call(
        fwd_kernel,
        tuple(shape(width + 32, rows) for _ in range(4)),
        scratch=(
            pltpu.VMEM((8 * rows, wide), BF16),
            pltpu.VMEM((4 * rows, width + HDIM), BF16),
            pltpu.VMEM((32, rows), F32),
        ),
        flops=2 * product,
        nbytes=8 * kv.size * 2,
    )(*kvs, *qbs)
    *parts, near, far = hold((*parts, near, far))
    gblocks = (gown, gy1, gy3, near, far)
    sums = [parts[0]] + [swap(parts[d], FRAME_C, 4, d) for d in range(1, 4)]
    d_attn = weighted(
        dattn_kernel, shape(rows, width), (me, *gblocks, tok_step, out_weight), flops
    )
    attn_t, own = call(merge_kernel, (shape(width, rows), shape(rows + 16, width)))(*sums, d_attn)
    owns = [own] + [swap(own, FRAME_C, 4, d) for d in range(1, 4)]
    terms = weighted(
        dgate_kernel,
        shape(8 * levels, gcols),
        (me, *gblocks, tok_step, out_weight, attn_t),
        flops,
    )
    terms, *owns = hold((terms, *owns))

    def backward(blocks, extra, out_shape):
        count = len(blocks)
        return call(
            functools.partial(bwd_kernel, count, bool(extra)),
            tuple(shape(rows, 2 * width) for _ in range(count)) + out_shape,
            scratch=(
                pltpu.VMEM((count * rows, wide), BF16),
                pltpu.VMEM((4 * rows, width + HDIM), BF16),
                pltpu.VMEM((4 * rows, width), BF16),
                pltpu.VMEM((8, 4 * rows), F32),
            ),
            flops=5 * product * count // 8,
            nbytes=count * kv.size * 2,
        )(*blocks, *qbs, *owns, *extra)

    def add(*blocks):
        return sum(b.astype(F32) for b in blocks).astype(BF16)

    got = swap(terms[4 * levels :], "xh", 2, 1)
    p4, n3, dq_part = backward((u4, d3), (), (shape(width, 4 * rows, F32),))
    low = lax.ppermute(p4, Z, below)
    high = lax.ppermute(n3, Z, above)
    p0, p1, p2, p3, n1, n2, here, away = backward(
        (kv, u1, u2, u3, d1, d2), (dq_part,), tuple(shape(2 * width, rows) for _ in range(2))
    )
    got, low, high, p3, n2, away = hold((got, low, high, p3, n2, away))

    terms = add(terms[: 4 * levels], got)
    piece = [terms[e * levels : (e + 1) * levels] for e in range(4)]
    low = lax.ppermute(add(low, p3), Z, below)
    high = lax.ppermute(add(high, n2), Z, above)
    got = [swap(piece[e], "y", 4, e) for e in range(1, 4)]
    low, high, *got = hold((low, high, *got))

    total = piece[0].astype(F32) + sum(g.astype(F32) for g in got)
    low = lax.ppermute(add(low, p2), Z, below)
    high = lax.ppermute(add(high, n1), Z, above)
    got = [swap(total, ("zl", "xl"), 4, e) for e in range(1, 4)]
    low, high, *got = hold((low, high, *got))

    total = total + sum(got)
    low = lax.ppermute(add(low, p1), Z, below)
    there = swap(away, "xl", 2, 1)
    got = [swap(total, "zh", 4, e) for e in range(1, 4)]
    low, there, *got = hold((low, there, *got))

    total = total + sum(got)
    total = total + swap(total, "core", 2, 1)
    mate = add(here[width:], there[width:])
    d_query = call(dquery_kernel, shape(rows, width))(here, there, swap(mate, "core", 2, 1))
    dkv = add(p0, low, high)
    return (d_query, dkv[:, :width], dkv[:, width:], total)


def solution(mesh):
    fine = Mesh(mesh.devices.reshape(4, 2, 2, 2, 2, 4), FRAME + HEAD)
    both = P(FRAME, HEAD)
    return jax.shard_map(
        body,
        mesh=fine,
        in_specs=(both, both, both, P(HEAD, None), P(None, HEAD), both, P(FRAME), P(), P()),
        out_specs=(both, both, both, P(None, HEAD)),
        check_vma=False,
    )
```

```python
import functools
import math

import jax
import jax.numpy as jnp
from jax import lax
from jax.experimental import pallas as pl
from jax.experimental.pallas import tpu as pltpu
from jax.sharding import Mesh, PartitionSpec as P

HDIM = 128
BIG = 1e30
SCALE = HDIM ** (-0.5)
LOG2E = math.log2(math.e)
C2 = SCALE * LOG2E
Z = ("zh", "zl")
FRAME = ("zh", "zl", "xl", "core")
HEAD = ("xh", "y")
FRAME_C = ("xl", "core")
NT = (((1,), (1,)), ((), ()))
NN = (((1,), (0,)), ((), ()))
F32 = jnp.float32
BF16 = jnp.bfloat16
MIB = 1024 * 1024


def dot(a, b, dims):
    return lax.dot_general(a, b, dims, preferred_element_type=F32)


def swap(block, axes, count, by):
    return lax.ppermute(block, axes, [(i, i ^ by) for i in range(count)])


def call(kernel, out_shape, scratch=(), flops=0, nbytes=0, limit=40):
    def run(*args):
        specs = [pl.BlockSpec(memory_space=pltpu.VMEM)] * len(args)
        return pl.pallas_call(
            kernel,
            out_shape=out_shape,
            in_specs=specs,
            out_specs=jax.tree.map(lambda _: pl.BlockSpec(memory_space=pltpu.VMEM), out_shape),
            scratch_shapes=list(scratch),
            compiler_params=pltpu.CompilerParams(vmem_limit_bytes=limit * MIB),
            cost_estimate=pl.CostEstimate(flops=flops, bytes_accessed=nbytes, transcendentals=0),
        )(*args)

    return run


def shape(rows, cols, dtype=BF16):
    return jax.ShapeDtypeStruct((rows, cols), dtype)


def prep_kernel(key, value, query, grad, gate, ids, mask, step, kv, qb, tok_step, sent):
    rows, width = key.shape
    spans = mask.shape[0]
    levels = gate.shape[0]
    hot_t = (lax.broadcasted_iota(jnp.int32, (rows, rows), 0) == ids[...]).astype(F32)
    hot = hot_t.T.astype(BF16)
    kv[:, :width] = key[...]
    kv[:, width : 2 * width] = value[...]
    kv[:, 2 * width :] = hot
    table = jnp.where(mask[...] == 1, 0.0, -BIG).astype(BF16)
    qb[:, :width] = query[...]
    qb[:, width:] = jnp.zeros((rows, HDIM), BF16)
    qb[:, width : width + spans] = dot(hot[:, :spans], table, NN).astype(BF16)
    step_t = (lax.broadcasted_iota(jnp.int32, (levels, spans), 0) == step[...]).astype(BF16)
    tok_step[...] = dot(hot[:, :spans], step_t, NT).astype(BF16)
    sent[:rows, :] = grad[...]
    sent[rows:, :] = gate[...].astype(BF16)


def fetch_weight(me, weight, w_vmem, sems, cols):
    copies = []
    for e in range(8):
        at = pl.multiple_of((me[0] ^ e) * cols, cols)
        copy = pltpu.make_async_copy(weight.at[:, pl.ds(at, cols)], w_vmem.at[e], sems.at[e])
        copy.start()
        copies.append(copy)
    return copies


def by_head(own, y1, y3, y2_near, y2_far):
    tall = y2_near.shape[0]
    low, high = pl.ds(0, tall), pl.ds(tall, tall)
    return [
        own.at[low], y1.at[low], y2_near, y3.at[low],
        own.at[high], y1.at[high], y2_far, y3.at[high],
    ]


def dattn_kernel(me, *refs):
    blocks = by_head(*refs[:5])
    tok_step, weight, out, w_vmem, sems = refs[5:]
    rows, width = out.shape
    copies = fetch_weight(me, weight, w_vmem, sems, blocks[0].shape[1])
    acc = jnp.zeros((rows, width), F32)
    for e in range(8):
        gate_tok = dot(tok_step[...], blocks[e][rows:, :], NN)
        d_proj = (blocks[e][:rows, :].astype(F32) * gate_tok).astype(BF16)
        copies[e].wait()
        acc += dot(d_proj, w_vmem[e], NT)
    out[...] = acc.astype(BF16)


def split3(x):
    hi = x.astype(BF16)
    rest = x - hi.astype(F32)
    mid = rest.astype(BF16)
    low = (rest - mid.astype(F32)).astype(BF16)
    return hi, mid, low


def fwd_kernel(k0, k1, k2, k3, k4, k5, k6, k7, q0, q1, q2, q3, s0, s1, s2, s3, kv, qd, stats):
    rows = q0.shape[0]
    width = q0.shape[1] - HDIM
    heads = width // HDIM
    for i, k in enumerate((k0, k1, k2, k3, k4, k5, k6, k7)):
        kv[i * rows : (i + 1) * rows, :] = k[...]
    for d, q in enumerate((q0, q1, q2, q3)):
        qd[d * rows : (d + 1) * rows, :] = q[...]
    stats[...] = jnp.zeros_like(stats)
    outs = (s0, s1, s2, s3)
    step = 2 * rows
    hot = kv[:, 2 * width :]
    for part in range(2):
        here = slice(part * step, (part + 1) * step)
        bias = dot(hot, qd[here, width:], NT)
        for h in range(heads):
            cols = slice(h * HDIM, (h + 1) * HDIM)
            vcols = slice(width + h * HDIM, width + (h + 1) * HDIM)
            keys = kv[:, cols]
            vals = kv[:, vcols]
            scores = dot(keys, qd[here, cols], NT) + bias
            top = jnp.max(scores, axis=0, keepdims=True)
            probs = jnp.exp2((scores - top) * C2)
            total = jnp.sum(probs, axis=0, keepdims=True)
            acc = dot(vals.T, probs.astype(BF16), NN)
            for i in range(2):
                d = 2 * part + i
                lanes = slice(i * rows, (i + 1) * rows)
                outs[d][cols, :] = acc[:, lanes].astype(BF16)
                stats[d * 8 + h : d * 8 + h + 1, :] = top[:, lanes]
                stats[d * 8 + heads + h : d * 8 + heads + h + 1, :] = total[:, lanes]
    for d, out in enumerate(outs):
        pieces = split3(stats[8 * d : 8 * d + 8, :])
        tail = jnp.concatenate([p.astype(F32) for p in pieces] + [jnp.zeros((8, rows), F32)], axis=0)
        out[width:, :] = tail.astype(BF16)


def merge_kernel(s0, s1, s2, s3, d_attn, attn_t, sent):
    width, rows = attn_t.shape
    heads = width // HDIM
    parts = (s0, s1, s2, s3)
    mine = []
    for s in parts:
        tail = s[width:, :].astype(F32)
        mine.append(tail[0:8] + tail[8:16] + tail[16:24])
    tops = [m[0:heads] for m in mine]
    top = jnp.maximum(jnp.maximum(tops[0], tops[1]), jnp.maximum(tops[2], tops[3]))
    ws = [jnp.exp2((t - top) * C2) for t in tops]
    total = sum(w * m[heads : 2 * heads] for w, m in zip(ws, mine))
    lse = top * C2 + jnp.log(total) * LOG2E
    dattn_t = d_attn[...].astype(F32).T
    deltas = []
    for h in range(heads):
        cols = slice(h * HDIM, (h + 1) * HDIM)
        acc = jnp.zeros((HDIM, rows), F32)
        for w, s in zip(ws, parts):
            acc += s[cols, :].astype(F32) * (w[h : h + 1] / total[h : h + 1])
        rounded = acc.astype(BF16)
        attn_t[cols, :] = rounded
        deltas.append(jnp.sum(rounded.astype(F32) * dattn_t[cols, :], axis=0, keepdims=True))
    stats = jnp.concatenate([lse] + deltas + [jnp.zeros((2, rows), F32)], axis=0)
    pieces = jnp.concatenate([p.astype(F32) for p in split3(stats)], axis=1)
    sent[:rows, :] = d_attn[...]
    sent[rows:, :] = jnp.concatenate([pieces, jnp.zeros_like(pieces)], axis=0).astype(BF16)


def bwd_kernel(count, last, *refs):
    ks = refs[:count]
    qs = refs[count : count + 4]
    owns = refs[count + 4 : count + 8]
    at = count + 8
    if last:
        before = refs[at]
        at += 1
    slots = refs[at : at + count]
    outs = refs[at + count : -4]
    kv, qd, ad, stats = refs[-4:]
    rows = qs[0].shape[0]
    width = qs[0].shape[1] - HDIM
    heads = width // HDIM
    for i, k in enumerate(ks):
        kv[i * rows : (i + 1) * rows, :] = k[...]
    for d, (q, a) in enumerate(zip(qs, owns)):
        lanes = slice(d * rows, (d + 1) * rows)
        qd[lanes, :] = q[...]
        ad[lanes, :] = a[:rows, :]
        tail = a[rows:, :].astype(F32)
        stats[:, lanes] = (tail[0:8, :rows] + tail[0:8, rows : 2 * rows]) + tail[0:8, 2 * rows :]
    step = 2 * rows
    hot = kv[:, 2 * width :]
    biases = [dot(hot, qd[p * step : (p + 1) * step, width:], NT) for p in range(2)]
    for h in range(heads):
        cols = slice(h * HDIM, (h + 1) * HDIM)
        vcols = slice(width + h * HDIM, width + (h + 1) * HDIM)
        keys = kv[:, cols]
        vals = kv[:, vcols]
        keys_t = keys.T
        dkey = None
        dval = None
        for part in range(2):
            here = slice(part * step, (part + 1) * step)
            d = 2 * part
            scores = dot(keys, qd[here, cols], NT) + biases[part]
            probs = jnp.exp2(scores * C2 - stats[h : h + 1, here])
            dprob = dot(vals, ad[here, cols], NT)
            dscore = (probs * (dprob - stats[heads + h : heads + h + 1, here])).astype(BF16)
            dk = dot(dscore, qd[here, cols], NN)
            dv = dot(probs.astype(BF16), ad[here, cols], NN)
            dkey = dk if dkey is None else dkey + dk
            dval = dv if dval is None else dval + dv
            dq = dot(keys_t, dscore, NN)
            if last:
                dq = (dq + before[cols, here]) * SCALE
                low_half = slice(h * HDIM, (h + 1) * HDIM)
                high_half = slice(width + h * HDIM, width + (h + 1) * HDIM)
                outs[part][low_half, :] = dq[:, :rows].astype(BF16)
                outs[part][high_half, :] = dq[:, rows:].astype(BF16)
            else:
                outs[0][cols, here] = dq
        for k, slot in enumerate(slots):
            here = slice(k * rows, (k + 1) * rows)
            slot[:, cols] = (dkey[here] * SCALE).astype(BF16)
            slot[:, vcols] = dval[here].astype(BF16)


def dquery_kernel(here, there, got, out):
    width = here.shape[0] // 2
    acc = here[:width, :].astype(F32) + there[:width, :].astype(F32) + got[...].astype(F32)
    out[...] = acc.T.astype(BF16)


def dgate_kernel(me, *refs):
    blocks = by_head(*refs[:5])
    tok_step, weight, attn_t, out, w_vmem, sems = refs[5:]
    rows = attn_t.shape[1]
    levels = tok_step.shape[1]
    copies = fetch_weight(me, weight, w_vmem, sems, blocks[0].shape[1])
    attn = attn_t[...].astype(F32).T.astype(BF16)
    hot = tok_step[...].astype(F32).T.astype(BF16)
    for e in range(8):
        copies[e].wait()
        proj = dot(attn, w_vmem[e], NN)
        terms = proj * blocks[e][:rows, :].astype(F32)
        high = terms.astype(BF16)
        low = (terms - high.astype(F32)).astype(BF16)
        out[e * levels : (e + 1) * levels, :] = (dot(hot, high, NN) + dot(hot, low, NN)).astype(BF16)


def body(query, key, value, out_weight, gate_table, grad_out, span_ids, span_mask, span_step):
    rows, width = query.shape
    levels, gcols = gate_table.shape
    me = (lax.axis_index("xh") * 4 + lax.axis_index("y")).astype(jnp.int32).reshape(1)
    wide = 2 * width + HDIM
    kv, qb, tok_step, sent = call(
        prep_kernel,
        (shape(rows, wide), shape(rows, width + HDIM), shape(rows, levels),
         shape(rows + levels, gcols)),
        limit=60,
    )(key, value, query, grad_out, gate_table, span_ids.reshape(1, rows), span_mask,
      span_step.reshape(1, -1))
    above = [(z, (z + 1) % 8) for z in range(8)]
    below = [(z, (z - 1) % 8) for z in range(8)]
    tall = rows + levels
    hold = lax.optimization_barrier

    u1, d1 = lax.ppermute(kv, Z, above), lax.ppermute(kv, Z, below)
    gx = swap(sent, "xh", 2, 1)
    qcore = swap(qb, "core", 2, 1)
    u1, qcore = hold((u1, qcore))
    d1, gx = hold((d1, gx))
    u2, d2 = lax.ppermute(u1, Z, above), lax.ppermute(d1, Z, below)
    gown = jnp.concatenate([sent, gx], axis=0)
    gy1, gy3 = swap(gown, "y", 4, 1), swap(gown, "y", 4, 3)
    u2, qcore = hold((u2, qcore))
    u3 = lax.ppermute(u2, Z, above)
    qxl, qdiag = swap(qb, "xl", 2, 1), swap(qcore, "xl", 2, 1)
    u3, d2, gy1, gy3, qxl, qdiag = hold((u3, d2, gy1, gy3, qxl, qdiag))
    u4, d3 = lax.ppermute(u3, Z, above), lax.ppermute(d2, Z, below)
    near, far = swap(gy1[:tall], "y", 4, 3), swap(gy3[tall:], "y", 4, 1)
    u4, d3, near, far = hold((u4, d3, near, far))
    kvs = (kv, u1, u2, u3, u4, d1, d2, d3)
    qbs = (qb, qcore, qxl, qdiag)

    def weighted(kernel, out_shape, args, flops):
        specs = [pl.BlockSpec(memory_space=pltpu.SMEM)]
        specs += [pl.BlockSpec(memory_space=pltpu.VMEM)] * 6
        specs += [pl.BlockSpec(memory_space=pl.ANY)]
        specs += [pl.BlockSpec(memory_space=pltpu.VMEM)] * (len(args) - 8)
        return pl.pallas_call(
            kernel,
            out_shape=out_shape,
            in_specs=specs,
            out_specs=pl.BlockSpec(memory_space=pltpu.VMEM),
            scratch_shapes=[
                pltpu.VMEM((8, width, gcols), BF16),
                pltpu.SemaphoreType.DMA((8,)),
            ],
            compiler_params=pltpu.CompilerParams(vmem_limit_bytes=57 * MIB),
            cost_estimate=pl.CostEstimate(
                flops=flops, bytes_accessed=out_weight.size * 2, transcendentals=0
            ),
        )(*args)

    flops = 2 * rows * out_weight.size
    product = 2 * 8 * rows * 4 * rows * width
    parts = call(
        fwd_kernel,
        tuple(shape(width + 32, rows) for _ in range(4)),
        scratch=(
            pltpu.VMEM((8 * rows, wide), BF16),
            pltpu.VMEM((4 * rows, width + HDIM), BF16),
            pltpu.VMEM((32, rows), F32),
        ),
        flops=2 * product,
        nbytes=8 * kv.size * 2,
    )(*kvs, *qbs)
    gblocks = (gown, gy1, gy3, near, far)
    sums = [parts[0]] + [swap(parts[d], FRAME_C, 4, d) for d in range(1, 4)]
    d_attn = weighted(
        dattn_kernel, shape(rows, width), (me, *gblocks, tok_step, out_weight), flops
    )
    attn_t, own = call(merge_kernel, (shape(width, rows), shape(rows + 16, width)))(*sums, d_attn)
    owns = [own] + [swap(own, FRAME_C, 4, d) for d in range(1, 4)]
    terms = weighted(
        dgate_kernel,
        shape(8 * levels, gcols),
        (me, *gblocks, tok_step, out_weight, attn_t),
        flops,
    )
    terms, *owns = hold((terms, *owns))

    def backward(blocks, extra, out_shape):
        count = len(blocks)
        return call(
            functools.partial(bwd_kernel, count, bool(extra)),
            tuple(shape(rows, 2 * width) for _ in range(count)) + out_shape,
            scratch=(
                pltpu.VMEM((count * rows, wide), BF16),
                pltpu.VMEM((4 * rows, width + HDIM), BF16),
                pltpu.VMEM((4 * rows, width), BF16),
                pltpu.VMEM((8, 4 * rows), F32),
            ),
            flops=5 * product * count // 8,
            nbytes=count * kv.size * 2,
        )(*blocks, *qbs, *owns, *extra)

    def add(*blocks):
        return sum(b.astype(F32) for b in blocks).astype(BF16)

    got = swap(terms[4 * levels :], "xh", 2, 1)
    p4, n3, dq_part = backward((u4, d3), (), (shape(width, 4 * rows, F32),))
    low = lax.ppermute(p4, Z, below)
    high = lax.ppermute(n3, Z, above)
    p0, p1, p2, p3, n1, n2, here, away = backward(
        (kv, u1, u2, u3, d1, d2), (dq_part,), tuple(shape(2 * width, rows) for _ in range(2))
    )
    got, low, high, p3, n2, away = hold((got, low, high, p3, n2, away))

    terms = add(terms[: 4 * levels], got)
    piece = [terms[e * levels : (e + 1) * levels] for e in range(4)]
    low = lax.ppermute(add(low, p3), Z, below)
    high = lax.ppermute(add(high, n2), Z, above)
    got = [swap(piece[e], "y", 4, e) for e in range(1, 4)]
    low, high, *got = hold((low, high, *got))

    total = piece[0].astype(F32) + sum(g.astype(F32) for g in got)
    low = lax.ppermute(add(low, p2), Z, below)
    high = lax.ppermute(add(high, n1), Z, above)
    got = [swap(total, ("zl", "xl"), 4, e) for e in range(1, 4)]
    low, high, *got = hold((low, high, *got))

    total = total + sum(got)
    low = lax.ppermute(add(low, p1), Z, below)
    there = swap(away, "xl", 2, 1)
    got = [swap(total, "zh", 4, e) for e in range(1, 4)]
    low, there, *got = hold((low, there, *got))

    total = total + sum(got)
    total = total + swap(total, "core", 2, 1)
    mate = add(here[width:], there[width:])
    d_query = call(dquery_kernel, shape(rows, width))(here, there, swap(mate, "core", 2, 1))
    dkv = add(p0, low, high)
    return (d_query, dkv[:, :width], dkv[:, width:], total)


def solution(mesh):
    fine = Mesh(mesh.devices.reshape(4, 2, 2, 2, 2, 4), FRAME + HEAD)
    both = P(FRAME, HEAD)
    return jax.shard_map(
        body,
        mesh=fine,
        in_specs=(both, both, both, P(HEAD, None), P(None, HEAD), both, P(FRAME), P(), P()),
        out_specs=(both, both, both, P(None, HEAD)),
        check_vma=False,
    )
```

```python
import functools
import math

import jax
import jax.numpy as jnp
from jax import lax
from jax.experimental import pallas as pl
from jax.experimental.pallas import tpu as pltpu
from jax.sharding import Mesh, PartitionSpec as P

HDIM = 128
BIG = 1e30
SCALE = HDIM ** (-0.5)
LOG2E = math.log2(math.e)
C2 = SCALE * LOG2E
Z = ("zh", "zl")
FRAME = ("zh", "zl", "xl", "core")
HEAD = ("xh", "y")
FRAME_C = ("xl", "core")
NT = (((1,), (1,)), ((), ()))
NN = (((1,), (0,)), ((), ()))
F32 = jnp.float32
BF16 = jnp.bfloat16
MIB = 1024 * 1024


def dot(a, b, dims):
    return lax.dot_general(a, b, dims, preferred_element_type=F32)


def swap(block, axes, count, by):
    return lax.ppermute(block, axes, [(i, i ^ by) for i in range(count)])


def call(kernel, out_shape, scratch=(), flops=0, nbytes=0, limit=40, loose=()):
    def run(*args):
        specs = [
            pl.BlockSpec(memory_space=pl.ANY if i in loose else pltpu.VMEM)
            for i in range(len(args))
        ]
        return pl.pallas_call(
            kernel,
            out_shape=out_shape,
            in_specs=specs,
            out_specs=jax.tree.map(lambda _: pl.BlockSpec(memory_space=pltpu.VMEM), out_shape),
            scratch_shapes=list(scratch),
            compiler_params=pltpu.CompilerParams(vmem_limit_bytes=limit * MIB),
            cost_estimate=pl.CostEstimate(flops=flops, bytes_accessed=nbytes, transcendentals=0),
        )(*args)

    return run


def shape(rows, cols, dtype=BF16):
    return jax.ShapeDtypeStruct((rows, cols), dtype)


def prep_kernel(key, value, query, grad, gate, ids, mask, step, kv, qb, tok_step, sent):
    rows, width = key.shape
    spans = mask.shape[0]
    levels = gate.shape[0]
    hot_t = (lax.broadcasted_iota(jnp.int32, (rows, rows), 0) == ids[...]).astype(F32)
    hot = hot_t.T.astype(BF16)
    kv[:, :width] = key[...]
    kv[:, width : 2 * width] = value[...]
    kv[:, 2 * width :] = hot
    table = jnp.where(mask[...] == 1, 0.0, -BIG).astype(BF16)
    qb[:, :width] = query[...]
    qb[:, width:] = jnp.zeros((rows, HDIM), BF16)
    qb[:, width : width + spans] = dot(hot[:, :spans], table, NN).astype(BF16)
    step_t = (lax.broadcasted_iota(jnp.int32, (levels, spans), 0) == step[...]).astype(BF16)
    tok_step[...] = dot(hot[:, :spans], step_t, NT).astype(BF16)
    sent[:rows, :] = grad[...]
    sent[rows:, :] = gate[...].astype(BF16)


def fetch_weight(me, weight, w_vmem, sems, cols):
    copies = []
    for e in range(8):
        at = pl.multiple_of((me[0] ^ e) * cols, cols)
        copy = pltpu.make_async_copy(weight.at[:, pl.ds(at, cols)], w_vmem.at[e], sems.at[e])
        copy.start()
        copies.append(copy)
    return copies


def by_head(own, y1, y3, y2_near, y2_far):
    tall = y2_near.shape[0]
    low, high = pl.ds(0, tall), pl.ds(tall, tall)
    return [
        own.at[low], y1.at[low], y2_near, y3.at[low],
        own.at[high], y1.at[high], y2_far, y3.at[high],
    ]


def dattn_kernel(me, *refs):
    blocks = by_head(*refs[:5])
    tok_step, weight, out, w_vmem, sems = refs[5:]
    rows, width = out.shape
    copies = fetch_weight(me, weight, w_vmem, sems, blocks[0].shape[1])
    acc = jnp.zeros((rows, width), F32)
    for e in range(8):
        gate_tok = dot(tok_step[...], blocks[e][rows:, :], NN)
        d_proj = (blocks[e][:rows, :].astype(F32) * gate_tok).astype(BF16)
        copies[e].wait()
        acc += dot(d_proj, w_vmem[e], NT)
    out[...] = acc.astype(BF16)


def split3(x):
    hi = x.astype(BF16)
    rest = x - hi.astype(F32)
    mid = rest.astype(BF16)
    low = (rest - mid.astype(F32)).astype(BF16)
    return hi, mid, low


def fwd_kernel(k0, k1, k2, k3, k4, k5, k6, k7, q0, q1, q2, q3, s0, s1, s2, s3, kv, qd, stats, sems):
    rows = q0.shape[0]
    width = q0.shape[1] - HDIM
    heads = width // HDIM
    mine = [
        pltpu.make_async_copy(k0, kv.at[pl.ds(0, rows)], sems.at[0]),
        pltpu.make_async_copy(q0, qd.at[pl.ds(0, rows)], sems.at[1]),
    ]
    for copy in mine:
        copy.start()
    for i, k in enumerate((k1, k2, k3, k4, k5, k6, k7)):
        kv[(i + 1) * rows : (i + 2) * rows, :] = k[...]
    for d, q in enumerate((q1, q2, q3)):
        qd[(d + 1) * rows : (d + 2) * rows, :] = q[...]
    stats[...] = jnp.zeros_like(stats)
    for copy in mine:
        copy.wait()
    outs = (s0, s1, s2, s3)
    step = 2 * rows
    hot = kv[:, 2 * width :]
    for part in range(2):
        here = slice(part * step, (part + 1) * step)
        bias = dot(hot, qd[here, width:], NT)
        for h in range(heads):
            cols = slice(h * HDIM, (h + 1) * HDIM)
            vcols = slice(width + h * HDIM, width + (h + 1) * HDIM)
            keys = kv[:, cols]
            vals = kv[:, vcols]
            scores = dot(keys, qd[here, cols], NT) + bias
            top = jnp.max(scores, axis=0, keepdims=True)
            probs = jnp.exp2((scores - top) * C2)
            total = jnp.sum(probs, axis=0, keepdims=True)
            acc = dot(vals.T, probs.astype(BF16), NN)
            for i in range(2):
                d = 2 * part + i
                lanes = slice(i * rows, (i + 1) * rows)
                outs[d][cols, :] = acc[:, lanes].astype(BF16)
                stats[d * 8 + h : d * 8 + h + 1, :] = top[:, lanes]
                stats[d * 8 + heads + h : d * 8 + heads + h + 1, :] = total[:, lanes]
    for d, out in enumerate(outs):
        pieces = split3(stats[8 * d : 8 * d + 8, :])
        tail = jnp.concatenate([p.astype(F32) for p in pieces] + [jnp.zeros((8, rows), F32)], axis=0)
        out[width:, :] = tail.astype(BF16)


def merge_kernel(s0, s1, s2, s3, d_attn, attn_t, sent):
    width, rows = attn_t.shape
    heads = width // HDIM
    parts = (s0, s1, s2, s3)
    mine = []
    for s in parts:
        tail = s[width:, :].astype(F32)
        mine.append(tail[0:8] + tail[8:16] + tail[16:24])
    tops = [m[0:heads] for m in mine]
    top = jnp.maximum(jnp.maximum(tops[0], tops[1]), jnp.maximum(tops[2], tops[3]))
    ws = [jnp.exp2((t - top) * C2) for t in tops]
    total = sum(w * m[heads : 2 * heads] for w, m in zip(ws, mine))
    lse = top * C2 + jnp.log(total) * LOG2E
    dattn_t = d_attn[...].astype(F32).T
    deltas = []
    for h in range(heads):
        cols = slice(h * HDIM, (h + 1) * HDIM)
        acc = jnp.zeros((HDIM, rows), F32)
        for w, s in zip(ws, parts):
            acc += s[cols, :].astype(F32) * (w[h : h + 1] / total[h : h + 1])
        rounded = acc.astype(BF16)
        attn_t[cols, :] = rounded
        deltas.append(jnp.sum(rounded.astype(F32) * dattn_t[cols, :], axis=0, keepdims=True))
    stats = jnp.concatenate([lse] + deltas + [jnp.zeros((2, rows), F32)], axis=0)
    pieces = jnp.concatenate([p.astype(F32) for p in split3(stats)], axis=1)
    sent[:rows, :] = d_attn[...]
    sent[rows:, :] = jnp.concatenate([pieces, jnp.zeros_like(pieces)], axis=0).astype(BF16)


def bwd_kernel(count, last, *refs):
    ks = refs[:count]
    qs = refs[count : count + 4]
    owns = refs[count + 4 : count + 8]
    at = count + 8
    if last:
        before = refs[at]
        at += 1
    slots = refs[at : at + count]
    outs = refs[at + count : -4]
    kv, qd, ad, stats = refs[-4:]
    rows = qs[0].shape[0]
    width = qs[0].shape[1] - HDIM
    heads = width // HDIM
    for i, k in enumerate(ks):
        kv[i * rows : (i + 1) * rows, :] = k[...]
    for d, (q, a) in enumerate(zip(qs, owns)):
        lanes = slice(d * rows, (d + 1) * rows)
        qd[lanes, :] = q[...]
        ad[lanes, :] = a[:rows, :]
        tail = a[rows:, :].astype(F32)
        stats[:, lanes] = (tail[0:8, :rows] + tail[0:8, rows : 2 * rows]) + tail[0:8, 2 * rows :]
    step = 2 * rows
    hot = kv[:, 2 * width :]
    biases = [dot(hot, qd[p * step : (p + 1) * step, width:], NT) for p in range(2)]
    for h in range(heads):
        cols = slice(h * HDIM, (h + 1) * HDIM)
        vcols = slice(width + h * HDIM, width + (h + 1) * HDIM)
        keys = kv[:, cols]
        vals = kv[:, vcols]
        keys_t = keys.T
        dkey = None
        dval = None
        for part in range(2):
            here = slice(part * step, (part + 1) * step)
            d = 2 * part
            scores = dot(keys, qd[here, cols], NT) + biases[part]
            probs = jnp.exp2(scores * C2 - stats[h : h + 1, here])
            dprob = dot(vals, ad[here, cols], NT)
            dscore = (probs * (dprob - stats[heads + h : heads + h + 1, here])).astype(BF16)
            dk = dot(dscore, qd[here, cols], NN)
            dv = dot(probs.astype(BF16), ad[here, cols], NN)
            dkey = dk if dkey is None else dkey + dk
            dval = dv if dval is None else dval + dv
            dq = dot(keys_t, dscore, NN)
            if last:
                dq = (dq + before[cols, here]) * SCALE
                low_half = slice(h * HDIM, (h + 1) * HDIM)
                high_half = slice(width + h * HDIM, width + (h + 1) * HDIM)
                outs[part][low_half, :] = dq[:, :rows].astype(BF16)
                outs[part][high_half, :] = dq[:, rows:].astype(BF16)
            else:
                outs[0][cols, here] = dq
        for k, slot in enumerate(slots):
            here = slice(k * rows, (k + 1) * rows)
            slot[:, cols] = (dkey[here] * SCALE).astype(BF16)
            slot[:, vcols] = dval[here].astype(BF16)


def dquery_kernel(here, there, got, out):
    width = here.shape[0] // 2
    acc = here[:width, :].astype(F32) + there[:width, :].astype(F32) + got[...].astype(F32)
    out[...] = acc.T.astype(BF16)


def dgate_kernel(me, *refs):
    blocks = by_head(*refs[:5])
    tok_step, weight, attn_t, out, w_vmem, sems = refs[5:]
    rows = attn_t.shape[1]
    levels = tok_step.shape[1]
    copies = fetch_weight(me, weight, w_vmem, sems, blocks[0].shape[1])
    attn = attn_t[...].astype(F32).T.astype(BF16)
    hot = tok_step[...].astype(F32).T.astype(BF16)
    for e in range(8):
        copies[e].wait()
        proj = dot(attn, w_vmem[e], NN)
        terms = proj * blocks[e][:rows, :].astype(F32)
        high = terms.astype(BF16)
        low = (terms - high.astype(F32)).astype(BF16)
        out[e * levels : (e + 1) * levels, :] = (dot(hot, high, NN) + dot(hot, low, NN)).astype(BF16)


def body(query, key, value, out_weight, gate_table, grad_out, span_ids, span_mask, span_step):
    rows, width = query.shape
    levels, gcols = gate_table.shape
    me = (lax.axis_index("xh") * 4 + lax.axis_index("y")).astype(jnp.int32).reshape(1)
    wide = 2 * width + HDIM
    kv, qb, tok_step, sent = call(
        prep_kernel,
        (shape(rows, wide), shape(rows, width + HDIM), shape(rows, levels),
         shape(rows + levels, gcols)),
        limit=60,
    )(key, value, query, grad_out, gate_table, span_ids.reshape(1, rows), span_mask,
      span_step.reshape(1, -1))
    above = [(z, (z + 1) % 8) for z in range(8)]
    below = [(z, (z - 1) % 8) for z in range(8)]
    tall = rows + levels
    hold = lax.optimization_barrier

    u1, d1 = lax.ppermute(kv, Z, above), lax.ppermute(kv, Z, below)
    gx = swap(sent, "xh", 2, 1)
    qcore = swap(qb, "core", 2, 1)
    u1, qcore = hold((u1, qcore))
    d1, gx = hold((d1, gx))
    u2, d2 = lax.ppermute(u1, Z, above), lax.ppermute(d1, Z, below)
    gown = jnp.concatenate([sent, gx], axis=0)
    gy1, gy3 = swap(gown, "y", 4, 1), swap(gown, "y", 4, 3)
    u2, qcore = hold((u2, qcore))
    u3 = lax.ppermute(u2, Z, above)
    qxl, qdiag = swap(qb, "xl", 2, 1), swap(qcore, "xl", 2, 1)
    u3, d2, gy1, gy3, qxl, qdiag = hold((u3, d2, gy1, gy3, qxl, qdiag))
    u4, d3 = lax.ppermute(u3, Z, above), lax.ppermute(d2, Z, below)
    near, far = swap(gy1[:tall], "y", 4, 3), swap(gy3[tall:], "y", 4, 1)
    u4, d3 = hold((u4, d3))
    kvs = (kv, u1, u2, u3, u4, d1, d2, d3)
    qbs = (qb, qcore, qxl, qdiag)

    def weighted(kernel, out_shape, args, flops):
        specs = [pl.BlockSpec(memory_space=pltpu.SMEM)]
        specs += [pl.BlockSpec(memory_space=pltpu.VMEM)] * 6
        specs += [pl.BlockSpec(memory_space=pl.ANY)]
        specs += [pl.BlockSpec(memory_space=pltpu.VMEM)] * (len(args) - 8)
        return pl.pallas_call(
            kernel,
            out_shape=out_shape,
            in_specs=specs,
            out_specs=pl.BlockSpec(memory_space=pltpu.VMEM),
            scratch_shapes=[
                pltpu.VMEM((8, width, gcols), BF16),
                pltpu.SemaphoreType.DMA((8,)),
            ],
            compiler_params=pltpu.CompilerParams(vmem_limit_bytes=40 * MIB),
            cost_estimate=pl.CostEstimate(
                flops=flops, bytes_accessed=out_weight.size * 2, transcendentals=0
            ),
        )(*args)

    flops = 2 * rows * out_weight.size
    product = 2 * 8 * rows * 4 * rows * width
    parts = call(
        fwd_kernel,
        tuple(shape(width + 32, rows) for _ in range(4)),
        scratch=(
            pltpu.VMEM((8 * rows, wide), BF16),
            pltpu.VMEM((4 * rows, width + HDIM), BF16),
            pltpu.VMEM((32, rows), F32),
            pltpu.SemaphoreType.DMA((2,)),
        ),
        loose=(0, 8),
        flops=2 * product,
        nbytes=8 * kv.size * 2,
    )(*kvs, *qbs)
    *parts, near, far = hold((*parts, near, far))
    gblocks = (gown, gy1, gy3, near, far)
    sums = [parts[0]] + [swap(parts[d], FRAME_C, 4, d) for d in range(1, 4)]
    d_attn = weighted(
        dattn_kernel, shape(rows, width), (me, *gblocks, tok_step, out_weight), flops
    )
    attn_t, own = call(merge_kernel, (shape(width, rows), shape(rows + 16, width)))(*sums, d_attn)
    owns = [own] + [swap(own, FRAME_C, 4, d) for d in range(1, 4)]
    terms = weighted(
        dgate_kernel,
        shape(8 * levels, gcols),
        (me, *gblocks, tok_step, out_weight, attn_t),
        flops,
    )
    terms, *owns = hold((terms, *owns))

    def backward(blocks, extra, out_shape):
        count = len(blocks)
        return call(
            functools.partial(bwd_kernel, count, bool(extra)),
            tuple(shape(rows, 2 * width) for _ in range(count)) + out_shape,
            scratch=(
                pltpu.VMEM((count * rows, wide), BF16),
                pltpu.VMEM((4 * rows, width + HDIM), BF16),
                pltpu.VMEM((4 * rows, width), BF16),
                pltpu.VMEM((8, 4 * rows), F32),
            ),
            flops=5 * product * count // 8,
            nbytes=count * kv.size * 2,
        )(*blocks, *qbs, *owns, *extra)

    def add(*blocks):
        return sum(b.astype(F32) for b in blocks).astype(BF16)

    got = swap(terms[4 * levels :], "xh", 2, 1)
    p4, n3, dq_part = backward((u4, d3), (), (shape(width, 4 * rows, F32),))
    low = lax.ppermute(p4, Z, below)
    high = lax.ppermute(n3, Z, above)
    p0, p1, p2, p3, n1, n2, here, away = backward(
        (kv, u1, u2, u3, d1, d2), (dq_part,), tuple(shape(2 * width, rows) for _ in range(2))
    )
    got, low, high, p3, n2, away = hold((got, low, high, p3, n2, away))

    terms = add(terms[: 4 * levels], got)
    piece = [terms[e * levels : (e + 1) * levels] for e in range(4)]
    low = lax.ppermute(add(low, p3), Z, below)
    high = lax.ppermute(add(high, n2), Z, above)
    got = [swap(piece[e], "y", 4, e) for e in range(1, 4)]
    low, high, *got = hold((low, high, *got))

    total = piece[0].astype(F32) + sum(g.astype(F32) for g in got)
    low = lax.ppermute(add(low, p2), Z, below)
    high = lax.ppermute(add(high, n1), Z, above)
    got = [swap(total, ("zl", "xl"), 4, e) for e in range(1, 4)]
    low, high, *got = hold((low, high, *got))

    total = total + sum(got)
    low = lax.ppermute(add(low, p1), Z, below)
    there = swap(away, "xl", 2, 1)
    got = [swap(total, "zh", 4, e) for e in range(1, 4)]
    low, there, *got = hold((low, there, *got))

    total = total + sum(got)
    total = total + swap(total, "core", 2, 1)
    mate = add(here[width:], there[width:])
    d_query = call(dquery_kernel, shape(rows, width))(here, there, swap(mate, "core", 2, 1))
    dkv = add(p0, low, high)
    return (d_query, dkv[:, :width], dkv[:, width:], total)


def solution(mesh):
    fine = Mesh(mesh.devices.reshape(4, 2, 2, 2, 2, 4), FRAME + HEAD)
    both = P(FRAME, HEAD)
    return jax.shard_map(
        body,
        mesh=fine,
        in_specs=(both, both, both, P(HEAD, None), P(None, HEAD), both, P(FRAME), P(), P()),
        out_specs=(both, both, both, P(None, HEAD)),
        check_vma=False,
    )
```

```python
import functools
import math

import jax
import jax.numpy as jnp
from jax import lax
from jax.experimental import pallas as pl
from jax.experimental.pallas import tpu as pltpu
from jax.sharding import Mesh, PartitionSpec as P

HDIM = 128
BIG = 1e30
SCALE = HDIM ** (-0.5)
LOG2E = math.log2(math.e)
C2 = SCALE * LOG2E
Z = ("zh", "zl")
FRAME = ("zh", "zl", "xl", "core")
HEAD = ("xh", "y")
FRAME_C = ("xl", "core")
NT = (((1,), (1,)), ((), ()))
NN = (((1,), (0,)), ((), ()))
F32 = jnp.float32
BF16 = jnp.bfloat16
MIB = 1024 * 1024


def dot(a, b, dims):
    return lax.dot_general(a, b, dims, preferred_element_type=F32)


def swap(block, axes, count, by):
    return lax.ppermute(block, axes, [(i, i ^ by) for i in range(count)])


def call(kernel, out_shape, scratch=(), flops=0, nbytes=0, limit=40, loose=()):
    def run(*args):
        specs = [
            pl.BlockSpec(memory_space=pltpu.HBM if i in loose else pltpu.VMEM)
            for i in range(len(args))
        ]
        return pl.pallas_call(
            kernel,
            out_shape=out_shape,
            in_specs=specs,
            out_specs=jax.tree.map(lambda _: pl.BlockSpec(memory_space=pltpu.VMEM), out_shape),
            scratch_shapes=list(scratch),
            compiler_params=pltpu.CompilerParams(vmem_limit_bytes=limit * MIB),
            cost_estimate=pl.CostEstimate(flops=flops, bytes_accessed=nbytes, transcendentals=0),
        )(*args)

    return run


def shape(rows, cols, dtype=BF16):
    return jax.ShapeDtypeStruct((rows, cols), dtype)


def prep_kernel(key, value, query, grad, gate, ids, mask, step, kv, qb, tok_step, sent):
    rows, width = key.shape
    spans = mask.shape[0]
    levels = gate.shape[0]
    hot_t = (lax.broadcasted_iota(jnp.int32, (rows, rows), 0) == ids[...]).astype(F32)
    hot = hot_t.T.astype(BF16)
    kv[:, :width] = key[...]
    kv[:, width : 2 * width] = value[...]
    kv[:, 2 * width :] = hot
    table = jnp.where(mask[...] == 1, 0.0, -BIG).astype(BF16)
    qb[:, :width] = query[...]
    qb[:, width:] = jnp.zeros((rows, HDIM), BF16)
    qb[:, width : width + spans] = dot(hot[:, :spans], table, NN).astype(BF16)
    step_t = (lax.broadcasted_iota(jnp.int32, (levels, spans), 0) == step[...]).astype(BF16)
    tok_step[...] = dot(hot[:, :spans], step_t, NT).astype(BF16)
    sent[:rows, :] = grad[...]
    sent[rows:, :] = gate[...].astype(BF16)


def fetch_weight(me, weight, w_vmem, sems, cols):
    copies = []
    for e in range(8):
        at = pl.multiple_of((me[0] ^ e) * cols, cols)
        copy = pltpu.make_async_copy(weight.at[:, pl.ds(at, cols)], w_vmem.at[e], sems.at[e])
        copy.start()
        copies.append(copy)
    return copies


def by_head(own, y1, y3, y2_near, y2_far):
    tall = y2_near.shape[0]
    low, high = pl.ds(0, tall), pl.ds(tall, tall)
    return [
        own.at[low], y1.at[low], y2_near, y3.at[low],
        own.at[high], y1.at[high], y2_far, y3.at[high],
    ]


def dattn_kernel(me, *refs):
    blocks = by_head(*refs[:5])
    tok_step, weight, out, w_vmem, sems = refs[5:]
    width, rows = out.shape
    copies = fetch_weight(me, weight, w_vmem, sems, blocks[0].shape[1])
    acc = jnp.zeros((width, rows), F32)
    for e in range(8):
        gate_tok = dot(tok_step[...], blocks[e][rows:, :], NN)
        d_proj = (blocks[e][:rows, :].astype(F32) * gate_tok).astype(BF16)
        copies[e].wait()
        acc += dot(w_vmem[e], d_proj, NT)
    out[...] = acc.astype(BF16)


def split3(x):
    hi = x.astype(BF16)
    rest = x - hi.astype(F32)
    mid = rest.astype(BF16)
    low = (rest - mid.astype(F32)).astype(BF16)
    return hi, mid, low


def fwd_kernel(k0, k1, k2, k3, k4, k5, k6, k7, q0, q1, q2, q3, s0, s1, s2, s3, kv, qd, stats, sems):
    rows = q0.shape[0]
    width = q0.shape[1] - HDIM
    heads = width // HDIM
    mine = [
        pltpu.make_async_copy(k0, kv.at[pl.ds(0, rows)], sems.at[0]),
        pltpu.make_async_copy(q0, qd.at[pl.ds(0, rows)], sems.at[1]),
    ]
    for copy in mine:
        copy.start()
    for i, k in enumerate((k1, k2, k3, k4, k5, k6, k7)):
        kv[(i + 1) * rows : (i + 2) * rows, :] = k[...]
    for d, q in enumerate((q1, q2, q3)):
        qd[(d + 1) * rows : (d + 2) * rows, :] = q[...]
    stats[...] = jnp.zeros_like(stats)
    for copy in mine:
        copy.wait()
    outs = (s0, s1, s2, s3)
    step = 2 * rows
    hot = kv[:, 2 * width :]
    for part in range(2):
        here = slice(part * step, (part + 1) * step)
        bias = dot(hot, qd[here, width:], NT)
        for h in range(heads):
            cols = slice(h * HDIM, (h + 1) * HDIM)
            vcols = slice(width + h * HDIM, width + (h + 1) * HDIM)
            keys = kv[:, cols]
            vals = kv[:, vcols]
            scores = dot(keys, qd[here, cols], NT) + bias
            top = jnp.max(scores, axis=0, keepdims=True)
            probs = jnp.exp2((scores - top) * C2)
            total = jnp.sum(probs, axis=0, keepdims=True)
            acc = dot(vals.T, probs.astype(BF16), NN)
            for i in range(2):
                d = 2 * part + i
                lanes = slice(i * rows, (i + 1) * rows)
                outs[d][cols, :] = acc[:, lanes].astype(BF16)
                stats[d * 8 + h : d * 8 + h + 1, :] = top[:, lanes]
                stats[d * 8 + heads + h : d * 8 + heads + h + 1, :] = total[:, lanes]
    for d, out in enumerate(outs):
        pieces = split3(stats[8 * d : 8 * d + 8, :])
        tail = jnp.concatenate([p.astype(F32) for p in pieces] + [jnp.zeros((8, rows), F32)], axis=0)
        out[width:, :] = tail.astype(BF16)


def merge_kernel(s0, s1, s2, s3, d_attn_t, attn_t, sent):
    width, rows = attn_t.shape
    heads = width // HDIM
    parts = (s0, s1, s2, s3)
    mine = []
    for s in parts:
        tail = s[width:, :].astype(F32)
        mine.append(tail[0:8] + tail[8:16] + tail[16:24])
    tops = [m[0:heads] for m in mine]
    top = jnp.maximum(jnp.maximum(tops[0], tops[1]), jnp.maximum(tops[2], tops[3]))
    ws = [jnp.exp2((t - top) * C2) for t in tops]
    total = sum(w * m[heads : 2 * heads] for w, m in zip(ws, mine))
    lse = top * C2 + jnp.log(total) * LOG2E
    dattn_t = d_attn_t[...].astype(F32)
    deltas = []
    for h in range(heads):
        cols = slice(h * HDIM, (h + 1) * HDIM)
        acc = jnp.zeros((HDIM, rows), F32)
        for w, s in zip(ws, parts):
            acc += s[cols, :].astype(F32) * (w[h : h + 1] / total[h : h + 1])
        rounded = acc.astype(BF16)
        attn_t[cols, :] = rounded
        deltas.append(jnp.sum(rounded.astype(F32) * dattn_t[cols, :], axis=0, keepdims=True))
    stats = jnp.concatenate([lse] + deltas + [jnp.zeros((2, rows), F32)], axis=0)
    pieces = jnp.concatenate([p.astype(F32) for p in split3(stats)], axis=1)
    sent[:rows, :] = dattn_t.T.astype(BF16)
    sent[rows:, :] = jnp.concatenate([pieces, jnp.zeros_like(pieces)], axis=0).astype(BF16)


def bwd_kernel(count, last, *refs):
    ks = refs[:count]
    qs = refs[count : count + 4]
    owns = refs[count + 4 : count + 8]
    at = count + 8
    if last:
        before = refs[at]
        at += 1
    slots = refs[at : at + count]
    outs = refs[at + count : -4]
    kv, qd, ad, stats = refs[-4:]
    rows = qs[0].shape[0]
    width = qs[0].shape[1] - HDIM
    heads = width // HDIM
    for i, k in enumerate(ks):
        kv[i * rows : (i + 1) * rows, :] = k[...]
    for d, (q, a) in enumerate(zip(qs, owns)):
        lanes = slice(d * rows, (d + 1) * rows)
        qd[lanes, :] = q[...]
        ad[lanes, :] = a[:rows, :]
        tail = a[rows:, :].astype(F32)
        stats[:, lanes] = (tail[0:8, :rows] + tail[0:8, rows : 2 * rows]) + tail[0:8, 2 * rows :]
    step = 2 * rows
    hot = kv[:, 2 * width :]
    biases = [dot(hot, qd[p * step : (p + 1) * step, width:], NT) for p in range(2)]
    for h in range(heads):
        cols = slice(h * HDIM, (h + 1) * HDIM)
        vcols = slice(width + h * HDIM, width + (h + 1) * HDIM)
        keys = kv[:, cols]
        vals = kv[:, vcols]
        keys_t = keys.T
        dkey = None
        dval = None
        for part in range(2):
            here = slice(part * step, (part + 1) * step)
            d = 2 * part
            scores = dot(keys, qd[here, cols], NT) + biases[part]
            probs = jnp.exp2(scores * C2 - stats[h : h + 1, here])
            dprob = dot(vals, ad[here, cols], NT)
            dscore = (probs * (dprob - stats[heads + h : heads + h + 1, here])).astype(BF16)
            dk = dot(dscore, qd[here, cols], NN)
            dv = dot(probs.astype(BF16), ad[here, cols], NN)
            dkey = dk if dkey is None else dkey + dk
            dval = dv if dval is None else dval + dv
            dq = dot(keys_t, dscore, NN)
            if last:
                dq = (dq + before[cols, here]) * SCALE
                low_half = slice(h * HDIM, (h + 1) * HDIM)
                high_half = slice(width + h * HDIM, width + (h + 1) * HDIM)
                outs[part][low_half, :] = dq[:, :rows].astype(BF16)
                outs[part][high_half, :] = dq[:, rows:].astype(BF16)
            else:
                outs[0][cols, here] = dq
        for k, slot in enumerate(slots):
            here = slice(k * rows, (k + 1) * rows)
            slot[:, cols] = (dkey[here] * SCALE).astype(BF16)
            slot[:, vcols] = dval[here].astype(BF16)


def dquery_kernel(here, there, got, out):
    width = here.shape[0] // 2
    acc = here[:width, :].astype(F32) + there[:width, :].astype(F32) + got[...].astype(F32)
    out[...] = acc.T.astype(BF16)


def dgate_kernel(me, *refs):
    blocks = by_head(*refs[:5])
    tok_step, weight, attn_t, out, w_vmem, sems = refs[5:]
    rows = attn_t.shape[1]
    levels = tok_step.shape[1]
    copies = fetch_weight(me, weight, w_vmem, sems, blocks[0].shape[1])
    attn = attn_t[...].astype(F32).T.astype(BF16)
    hot = tok_step[...].astype(F32).T.astype(BF16)
    for e in range(8):
        copies[e].wait()
        proj = dot(attn, w_vmem[e], NN)
        terms = (proj * blocks[e][:rows, :].astype(F32)).astype(BF16)
        out[e * levels : (e + 1) * levels, :] = dot(hot, terms, NN).astype(BF16)


def body(query, key, value, out_weight, gate_table, grad_out, span_ids, span_mask, span_step):
    rows, width = query.shape
    levels, gcols = gate_table.shape
    me = (lax.axis_index("xh") * 4 + lax.axis_index("y")).astype(jnp.int32).reshape(1)
    wide = 2 * width + HDIM
    kv, qb, tok_step, sent = call(
        prep_kernel,
        (shape(rows, wide), shape(rows, width + HDIM), shape(rows, levels),
         shape(rows + levels, gcols)),
        limit=60,
    )(key, value, query, grad_out, gate_table, span_ids.reshape(1, rows), span_mask,
      span_step.reshape(1, -1))
    above = [(z, (z + 1) % 8) for z in range(8)]
    below = [(z, (z - 1) % 8) for z in range(8)]
    tall = rows + levels
    hold = lax.optimization_barrier

    u1, d1 = lax.ppermute(kv, Z, above), lax.ppermute(kv, Z, below)
    gx = swap(sent, "xh", 2, 1)
    qcore = swap(qb, "core", 2, 1)
    u1, qcore = hold((u1, qcore))
    d1, gx = hold((d1, gx))
    u2, d2 = lax.ppermute(u1, Z, above), lax.ppermute(d1, Z, below)
    gown = jnp.concatenate([sent, gx], axis=0)
    gy1, gy3 = swap(gown, "y", 4, 1), swap(gown, "y", 4, 3)
    u2, qcore = hold((u2, qcore))
    u3 = lax.ppermute(u2, Z, above)
    qxl, qdiag = swap(qb, "xl", 2, 1), swap(qcore, "xl", 2, 1)
    u3, d2, gy1, gy3, qxl, qdiag = hold((u3, d2, gy1, gy3, qxl, qdiag))
    u4, d3 = lax.ppermute(u3, Z, above), lax.ppermute(d2, Z, below)
    near, far = swap(gy1[:tall], "y", 4, 3), swap(gy3[tall:], "y", 4, 1)
    u4, d3 = hold((u4, d3))
    kvs = (kv, u1, u2, u3, u4, d1, d2, d3)
    qbs = (qb, qcore, qxl, qdiag)

    def weighted(kernel, out_shape, args, flops):
        specs = [pl.BlockSpec(memory_space=pltpu.SMEM)]
        specs += [pl.BlockSpec(memory_space=pltpu.VMEM)] * 6
        specs += [pl.BlockSpec(memory_space=pltpu.HBM)]
        specs += [pl.BlockSpec(memory_space=pltpu.VMEM)] * (len(args) - 8)
        return pl.pallas_call(
            kernel,
            out_shape=out_shape,
            in_specs=specs,
            out_specs=pl.BlockSpec(memory_space=pltpu.VMEM),
            scratch_shapes=[
                pltpu.VMEM((8, width, gcols), BF16),
                pltpu.SemaphoreType.DMA((8,)),
            ],
            compiler_params=pltpu.CompilerParams(vmem_limit_bytes=40 * MIB),
            cost_estimate=pl.CostEstimate(
                flops=flops, bytes_accessed=out_weight.size * 2, transcendentals=0
            ),
        )(*args)

    flops = 2 * rows * out_weight.size
    product = 2 * 8 * rows * 4 * rows * width
    parts = call(
        fwd_kernel,
        tuple(shape(width + 32, rows) for _ in range(4)),
        scratch=(
            pltpu.VMEM((8 * rows, wide), BF16),
            pltpu.VMEM((4 * rows, width + HDIM), BF16),
            pltpu.VMEM((32, rows), F32),
            pltpu.SemaphoreType.DMA((2,)),
        ),
        loose=(0, 8),
        flops=2 * product,
        nbytes=8 * kv.size * 2,
    )(*kvs, *qbs)
    *parts, near, far = hold((*parts, near, far))
    gblocks = (gown, gy1, gy3, near, far)
    sums = [parts[0]] + [swap(parts[d], FRAME_C, 4, d) for d in range(1, 4)]
    d_attn = weighted(
        dattn_kernel, shape(width, rows), (me, *gblocks, tok_step, out_weight), flops
    )
    attn_t, own = call(merge_kernel, (shape(width, rows), shape(rows + 16, width)))(*sums, d_attn)
    owns = [own] + [swap(own, FRAME_C, 4, d) for d in range(1, 4)]
    terms = weighted(
        dgate_kernel,
        shape(8 * levels, gcols),
        (me, *gblocks, tok_step, out_weight, attn_t),
        flops,
    )
    terms, *owns = hold((terms, *owns))

    def backward(blocks, extra, out_shape):
        count = len(blocks)
        return call(
            functools.partial(bwd_kernel, count, bool(extra)),
            tuple(shape(rows, 2 * width) for _ in range(count)) + out_shape,
            scratch=(
                pltpu.VMEM((count * rows, wide), BF16),
                pltpu.VMEM((4 * rows, width + HDIM), BF16),
                pltpu.VMEM((4 * rows, width), BF16),
                pltpu.VMEM((8, 4 * rows), F32),
            ),
            flops=5 * product * count // 8,
            nbytes=count * kv.size * 2,
        )(*blocks, *qbs, *owns, *extra)

    def add(*blocks):
        return sum(b.astype(F32) for b in blocks).astype(BF16)

    got = swap(terms[4 * levels :], "xh", 2, 1)
    p4, n3, dq_part = backward((u4, d3), (), (shape(width, 4 * rows, F32),))
    low = lax.ppermute(p4, Z, below)
    high = lax.ppermute(n3, Z, above)
    p0, p1, p2, p3, n1, n2, here, away = backward(
        (kv, u1, u2, u3, d1, d2), (dq_part,), tuple(shape(2 * width, rows) for _ in range(2))
    )
    got, low, high, p3, n2, away = hold((got, low, high, p3, n2, away))

    terms = add(terms[: 4 * levels], got)
    piece = [terms[e * levels : (e + 1) * levels] for e in range(4)]
    low = lax.ppermute(add(low, p3), Z, below)
    high = lax.ppermute(add(high, n2), Z, above)
    got = [swap(piece[e], "y", 4, e) for e in range(1, 4)]
    low, high, *got = hold((low, high, *got))

    total = piece[0].astype(F32) + sum(g.astype(F32) for g in got)
    low = lax.ppermute(add(low, p2), Z, below)
    high = lax.ppermute(add(high, n1), Z, above)
    got = [swap(total, ("zl", "xl"), 4, e) for e in range(1, 4)]
    low, high, *got = hold((low, high, *got))

    total = total + sum(got)
    low = lax.ppermute(add(low, p1), Z, below)
    there = swap(away, "xl", 2, 1)
    got = [swap(total, "zh", 4, e) for e in range(1, 4)]
    low, there, *got = hold((low, there, *got))

    total = total + sum(got)
    total = total + swap(total, "core", 2, 1)
    mate = add(here[width:], there[width:])
    d_query = call(dquery_kernel, shape(rows, width))(here, there, swap(mate, "core", 2, 1))
    dkv = add(p0, low, high)
    return (d_query, dkv[:, :width], dkv[:, width:], total)


def solution(mesh):
    fine = Mesh(mesh.devices.reshape(4, 2, 2, 2, 2, 4), FRAME + HEAD)
    both = P(FRAME, HEAD)
    return jax.shard_map(
        body,
        mesh=fine,
        in_specs=(both, both, both, P(HEAD, None), P(None, HEAD), both, P(FRAME), P(), P()),
        out_specs=(both, both, both, P(None, HEAD)),
        check_vma=False,
    )
```

```python
import functools
import math

import jax
import jax.numpy as jnp
from jax import lax
from jax.experimental import pallas as pl
from jax.experimental.pallas import tpu as pltpu
from jax.sharding import Mesh, PartitionSpec as P

HDIM = 128
BIG = 1e30
SCALE = HDIM ** (-0.5)
LOG2E = math.log2(math.e)
C2 = SCALE * LOG2E
Z = ("zh", "zl")
FRAME = ("zh", "zl", "xl", "core")
HEAD = ("xh", "y")
FRAME_C = ("xl", "core")
NT = (((1,), (1,)), ((), ()))
NN = (((1,), (0,)), ((), ()))
F32 = jnp.float32
BF16 = jnp.bfloat16
MIB = 1024 * 1024


def dot(a, b, dims):
    return lax.dot_general(a, b, dims, preferred_element_type=F32)


def swap(block, axes, count, by):
    return lax.ppermute(block, axes, [(i, i ^ by) for i in range(count)])


def call(kernel, out_shape, scratch=(), flops=0, nbytes=0, limit=40, loose=()):
    def run(*args):
        specs = [
            pl.BlockSpec(memory_space=pl.ANY if i in loose else pltpu.VMEM)
            for i in range(len(args))
        ]
        return pl.pallas_call(
            kernel,
            out_shape=out_shape,
            in_specs=specs,
            out_specs=jax.tree.map(lambda _: pl.BlockSpec(memory_space=pltpu.VMEM), out_shape),
            scratch_shapes=list(scratch),
            compiler_params=pltpu.CompilerParams(vmem_limit_bytes=limit * MIB),
            cost_estimate=pl.CostEstimate(flops=flops, bytes_accessed=nbytes, transcendentals=0),
        )(*args)

    return run


def shape(rows, cols, dtype=BF16):
    return jax.ShapeDtypeStruct((rows, cols), dtype)


def prep_kernel(key, value, query, grad, gate, ids, mask, step, kv, qb, tok_step, sent):
    rows, width = key.shape
    spans = mask.shape[0]
    levels = gate.shape[0]
    hot_t = (lax.broadcasted_iota(jnp.int32, (rows, rows), 0) == ids[...]).astype(F32)
    hot = hot_t.T.astype(BF16)
    kv[:, :width] = key[...]
    kv[:, width : 2 * width] = value[...]
    kv[:, 2 * width :] = hot
    table = jnp.where(mask[...] == 1, 0.0, -BIG).astype(BF16)
    qb[:, :width] = query[...]
    qb[:, width:] = jnp.zeros((rows, HDIM), BF16)
    qb[:, width : width + spans] = dot(hot[:, :spans], table, NN).astype(BF16)
    step_t = (lax.broadcasted_iota(jnp.int32, (levels, spans), 0) == step[...]).astype(BF16)
    tok_step[...] = dot(hot[:, :spans], step_t, NT).astype(BF16)
    sent[:rows, :] = grad[...]
    sent[rows:, :] = gate[...].astype(BF16)


def near_kernel(query, kv, weight, out):
    out[...] = query[...]


def fetch_weight(me, weight, w_vmem, sems, cols):
    copies = []
    for e in range(8):
        at = pl.multiple_of((me[0] ^ e) * cols, cols)
        copy = pltpu.make_async_copy(weight.at[:, pl.ds(at, cols)], w_vmem.at[e], sems.at[e])
        copy.start()
        copies.append(copy)
    return copies


def by_head(own, y1, y3, y2_near, y2_far):
    tall = y2_near.shape[0]
    low, high = pl.ds(0, tall), pl.ds(tall, tall)
    return [
        own.at[low], y1.at[low], y2_near, y3.at[low],
        own.at[high], y1.at[high], y2_far, y3.at[high],
    ]


def dattn_kernel(me, *refs):
    blocks = by_head(*refs[:5])
    tok_step, weight, out, w_vmem, sems = refs[5:]
    rows, width = out.shape
    copies = fetch_weight(me, weight, w_vmem, sems, blocks[0].shape[1])
    acc = jnp.zeros((rows, width), F32)
    for e in range(8):
        gate_tok = dot(tok_step[...], blocks[e][rows:, :], NN)
        d_proj = (blocks[e][:rows, :].astype(F32) * gate_tok).astype(BF16)
        copies[e].wait()
        acc += dot(d_proj, w_vmem[e], NT)
    out[...] = acc.astype(BF16)


def split3(x):
    hi = x.astype(BF16)
    rest = x - hi.astype(F32)
    mid = rest.astype(BF16)
    low = (rest - mid.astype(F32)).astype(BF16)
    return hi, mid, low


def fwd_kernel(k0, k1, k2, k3, k4, k5, k6, k7, q0, q1, q2, q3, s0, s1, s2, s3, kv, qd, stats):
    rows = q0.shape[0]
    width = q0.shape[1] - HDIM
    heads = width // HDIM
    for i, k in enumerate((k0, k1, k2, k3, k4, k5, k6, k7)):
        kv[i * rows : (i + 1) * rows, :] = k[...]
    for d, q in enumerate((q0, q1, q2, q3)):
        qd[d * rows : (d + 1) * rows, :] = q[...]
    stats[...] = jnp.zeros_like(stats)
    outs = (s0, s1, s2, s3)
    step = 2 * rows
    hot = kv[:, 2 * width :]
    for part in range(2):
        here = slice(part * step, (part + 1) * step)
        bias = dot(hot, qd[here, width:], NT)
        for h in range(heads):
            cols = slice(h * HDIM, (h + 1) * HDIM)
            vcols = slice(width + h * HDIM, width + (h + 1) * HDIM)
            keys = kv[:, cols]
            vals = kv[:, vcols]
            scores = dot(keys, qd[here, cols], NT) + bias
            top = jnp.max(scores, axis=0, keepdims=True)
            probs = jnp.exp2((scores - top) * C2)
            total = jnp.sum(probs, axis=0, keepdims=True)
            acc = dot(vals.T, probs.astype(BF16), NN)
            for i in range(2):
                d = 2 * part + i
                lanes = slice(i * rows, (i + 1) * rows)
                outs[d][cols, :] = acc[:, lanes].astype(BF16)
                stats[d * 8 + h : d * 8 + h + 1, :] = top[:, lanes]
                stats[d * 8 + heads + h : d * 8 + heads + h + 1, :] = total[:, lanes]
    for d, out in enumerate(outs):
        pieces = split3(stats[8 * d : 8 * d + 8, :])
        tail = jnp.concatenate([p.astype(F32) for p in pieces] + [jnp.zeros((8, rows), F32)], axis=0)
        out[width:, :] = tail.astype(BF16)


def merge_kernel(s0, s1, s2, s3, d_attn, attn_t, sent):
    width, rows = attn_t.shape
    heads = width // HDIM
    parts = (s0, s1, s2, s3)
    mine = []
    for s in parts:
        tail = s[width:, :].astype(F32)
        mine.append(tail[0:8] + tail[8:16] + tail[16:24])
    tops = [m[0:heads] for m in mine]
    top = jnp.maximum(jnp.maximum(tops[0], tops[1]), jnp.maximum(tops[2], tops[3]))
    ws = [jnp.exp2((t - top) * C2) for t in tops]
    total = sum(w * m[heads : 2 * heads] for w, m in zip(ws, mine))
    lse = top * C2 + jnp.log(total) * LOG2E
    dattn_t = d_attn[...].astype(F32).T
    deltas = []
    for h in range(heads):
        cols = slice(h * HDIM, (h + 1) * HDIM)
        acc = jnp.zeros((HDIM, rows), F32)
        for w, s in zip(ws, parts):
            acc += s[cols, :].astype(F32) * (w[h : h + 1] / total[h : h + 1])
        rounded = acc.astype(BF16)
        attn_t[cols, :] = rounded
        deltas.append(jnp.sum(rounded.astype(F32) * dattn_t[cols, :], axis=0, keepdims=True))
    stats = jnp.concatenate([lse] + deltas + [jnp.zeros((2, rows), F32)], axis=0)
    pieces = jnp.concatenate([p.astype(F32) for p in split3(stats)], axis=1)
    sent[:rows, :] = d_attn[...]
    sent[rows:, :] = jnp.concatenate([pieces, jnp.zeros_like(pieces)], axis=0).astype(BF16)


def bwd_kernel(count, last, *refs):
    ks = refs[:count]
    qs = refs[count : count + 4]
    owns = refs[count + 4 : count + 8]
    at = count + 8
    if last:
        before = refs[at]
        at += 1
    slots = refs[at : at + count]
    outs = refs[at + count : -4]
    kv, qd, ad, stats = refs[-4:]
    rows = qs[0].shape[0]
    width = qs[0].shape[1] - HDIM
    heads = width // HDIM
    for i, k in enumerate(ks):
        kv[i * rows : (i + 1) * rows, :] = k[...]
    for d, (q, a) in enumerate(zip(qs, owns)):
        lanes = slice(d * rows, (d + 1) * rows)
        qd[lanes, :] = q[...]
        ad[lanes, :] = a[:rows, :]
        tail = a[rows:, :].astype(F32)
        stats[:, lanes] = (tail[0:8, :rows] + tail[0:8, rows : 2 * rows]) + tail[0:8, 2 * rows :]
    step = 2 * rows
    hot = kv[:, 2 * width :]
    biases = [dot(hot, qd[p * step : (p + 1) * step, width:], NT) for p in range(2)]
    for h in range(heads):
        cols = slice(h * HDIM, (h + 1) * HDIM)
        vcols = slice(width + h * HDIM, width + (h + 1) * HDIM)
        keys = kv[:, cols]
        vals = kv[:, vcols]
        keys_t = keys.T
        dkey = None
        dval = None
        for part in range(2):
            here = slice(part * step, (part + 1) * step)
            d = 2 * part
            scores = dot(keys, qd[here, cols], NT) + biases[part]
            probs = jnp.exp2(scores * C2 - stats[h : h + 1, here])
            dprob = dot(vals, ad[here, cols], NT)
            dscore = (probs * (dprob - stats[heads + h : heads + h + 1, here])).astype(BF16)
            dk = dot(dscore, qd[here, cols], NN)
            dv = dot(probs.astype(BF16), ad[here, cols], NN)
            dkey = dk if dkey is None else dkey + dk
            dval = dv if dval is None else dval + dv
            dq = dot(keys_t, dscore, NN)
            if last:
                dq = (dq + before[cols, here]) * SCALE
                low_half = slice(h * HDIM, (h + 1) * HDIM)
                high_half = slice(width + h * HDIM, width + (h + 1) * HDIM)
                outs[part][low_half, :] = dq[:, :rows].astype(BF16)
                outs[part][high_half, :] = dq[:, rows:].astype(BF16)
            else:
                outs[0][cols, here] = dq
        for k, slot in enumerate(slots):
            here = slice(k * rows, (k + 1) * rows)
            slot[:, cols] = (dkey[here] * SCALE).astype(BF16)
            slot[:, vcols] = dval[here].astype(BF16)


def dquery_kernel(here, there, got, out):
    width = here.shape[0] // 2
    acc = here[:width, :].astype(F32) + there[:width, :].astype(F32) + got[...].astype(F32)
    out[...] = acc.T.astype(BF16)


def dgate_kernel(me, *refs):
    blocks = by_head(*refs[:5])
    tok_step, weight, attn_t, out, w_vmem, sems = refs[5:]
    rows = attn_t.shape[1]
    levels = tok_step.shape[1]
    copies = fetch_weight(me, weight, w_vmem, sems, blocks[0].shape[1])
    attn = attn_t[...].astype(F32).T.astype(BF16)
    hot = tok_step[...].astype(F32).T.astype(BF16)
    for e in range(8):
        copies[e].wait()
        proj = dot(attn, w_vmem[e], NN)
        terms = (proj * blocks[e][:rows, :].astype(F32)).astype(BF16)
        out[e * levels : (e + 1) * levels, :] = dot(hot, terms, NN).astype(BF16)


def body(query, key, value, out_weight, gate_table, grad_out, span_ids, span_mask, span_step):
    rows, width = query.shape
    levels, gcols = gate_table.shape
    me = (lax.axis_index("xh") * 4 + lax.axis_index("y")).astype(jnp.int32).reshape(1)
    wide = 2 * width + HDIM
    kv, qb, tok_step, sent = call(
        prep_kernel,
        (shape(rows, wide), shape(rows, width + HDIM), shape(rows, levels),
         shape(rows + levels, gcols)),
        limit=60,
    )(key, value, query, grad_out, gate_table, span_ids.reshape(1, rows), span_mask,
      span_step.reshape(1, -1))
    above = [(z, (z + 1) % 8) for z in range(8)]
    below = [(z, (z - 1) % 8) for z in range(8)]
    tall = rows + levels
    hold = lax.optimization_barrier

    u1, d1 = lax.ppermute(kv, Z, above), lax.ppermute(kv, Z, below)
    gx = swap(sent, "xh", 2, 1)
    qcore = swap(qb, "core", 2, 1)
    u1, qcore = hold((u1, qcore))
    d1, gx = hold((d1, gx))
    u2, d2 = lax.ppermute(u1, Z, above), lax.ppermute(d1, Z, below)
    gown = jnp.concatenate([sent, gx], axis=0)
    gy1, gy3 = swap(gown, "y", 4, 1), swap(gown, "y", 4, 3)
    u2, qcore, qb = hold((u2, qcore, qb))
    u3 = lax.ppermute(u2, Z, above)
    qxl, qdiag = swap(qb, "xl", 2, 1), swap(qcore, "xl", 2, 1)
    q_own = call(near_kernel, shape(rows, width + HDIM), loose=(2,), nbytes=out_weight.size)(
        qb, kv, out_weight
    )
    u3, d2, gy1, gy3, qxl, qdiag, q_own = hold((u3, d2, gy1, gy3, qxl, qdiag, q_own))
    u4, d3 = lax.ppermute(u3, Z, above), lax.ppermute(d2, Z, below)
    near, far = swap(gy1[:tall], "y", 4, 3), swap(gy3[tall:], "y", 4, 1)
    u4, d3 = hold((u4, d3))
    kvs = (kv, u1, u2, u3, u4, d1, d2, d3)
    qbs = (q_own, qcore, qxl, qdiag)

    def weighted(kernel, out_shape, args, flops):
        specs = [pl.BlockSpec(memory_space=pltpu.SMEM)]
        specs += [pl.BlockSpec(memory_space=pltpu.VMEM)] * 6
        specs += [pl.BlockSpec(memory_space=pl.ANY)]
        specs += [pl.BlockSpec(memory_space=pltpu.VMEM)] * (len(args) - 8)
        return pl.pallas_call(
            kernel,
            out_shape=out_shape,
            in_specs=specs,
            out_specs=pl.BlockSpec(memory_space=pltpu.VMEM),
            scratch_shapes=[
                pltpu.VMEM((8, width, gcols), BF16),
                pltpu.SemaphoreType.DMA((8,)),
            ],
            compiler_params=pltpu.CompilerParams(vmem_limit_bytes=40 * MIB),
            cost_estimate=pl.CostEstimate(
                flops=flops, bytes_accessed=out_weight.size * 2, transcendentals=0
            ),
        )(*args)

    flops = 2 * rows * out_weight.size
    product = 2 * 8 * rows * 4 * rows * width
    parts = call(
        fwd_kernel,
        tuple(shape(width + 32, rows) for _ in range(4)),
        scratch=(
            pltpu.VMEM((8 * rows, wide), BF16),
            pltpu.VMEM((4 * rows, width + HDIM), BF16),
            pltpu.VMEM((32, rows), F32),
        ),
        flops=2 * product,
        nbytes=8 * kv.size * 2,
    )(*kvs, *qbs)
    *parts, near, far = hold((*parts, near, far))
    gblocks = (gown, gy1, gy3, near, far)
    sums = [parts[0]] + [swap(parts[d], FRAME_C, 4, d) for d in range(1, 4)]
    d_attn = weighted(
        dattn_kernel, shape(rows, width), (me, *gblocks, tok_step, out_weight), flops
    )
    attn_t, own = call(merge_kernel, (shape(width, rows), shape(rows + 16, width)))(*sums, d_attn)
    owns = [own] + [swap(own, FRAME_C, 4, d) for d in range(1, 4)]
    terms = weighted(
        dgate_kernel,
        shape(8 * levels, gcols),
        (me, *gblocks, tok_step, out_weight, attn_t),
        flops,
    )
    terms, *owns = hold((terms, *owns))

    def backward(blocks, extra, out_shape):
        count = len(blocks)
        return call(
            functools.partial(bwd_kernel, count, bool(extra)),
            tuple(shape(rows, 2 * width) for _ in range(count)) + out_shape,
            scratch=(
                pltpu.VMEM((count * rows, wide), BF16),
                pltpu.VMEM((4 * rows, width + HDIM), BF16),
                pltpu.VMEM((4 * rows, width), BF16),
                pltpu.VMEM((8, 4 * rows), F32),
            ),
            flops=5 * product * count // 8,
            nbytes=count * kv.size * 2,
        )(*blocks, *qbs, *owns, *extra)

    def add(*blocks):
        return sum(b.astype(F32) for b in blocks).astype(BF16)

    got = swap(terms[4 * levels :], "xh", 2, 1)
    p4, n3, dq_part = backward((u4, d3), (), (shape(width, 4 * rows, F32),))
    low = lax.ppermute(p4, Z, below)
    high = lax.ppermute(n3, Z, above)
    p0, p1, p2, p3, n1, n2, here, away = backward(
        (kv, u1, u2, u3, d1, d2), (dq_part,), tuple(shape(2 * width, rows) for _ in range(2))
    )
    got, low, high, p3, n2, away = hold((got, low, high, p3, n2, away))

    terms = add(terms[: 4 * levels], got)
    piece = [terms[e * levels : (e + 1) * levels] for e in range(4)]
    low = lax.ppermute(add(low, p3), Z, below)
    high = lax.ppermute(add(high, n2), Z, above)
    got = [swap(piece[e], "y", 4, e) for e in range(1, 4)]
    low, high, *got = hold((low, high, *got))

    total = piece[0].astype(F32) + sum(g.astype(F32) for g in got)
    low = lax.ppermute(add(low, p2), Z, below)
    high = lax.ppermute(add(high, n1), Z, above)
    got = [swap(total, ("zl", "xl"), 4, e) for e in range(1, 4)]
    low, high, *got = hold((low, high, *got))

    total = total + sum(got)
    low = lax.ppermute(add(low, p1), Z, below)
    there = swap(away, "xl", 2, 1)
    got = lax.ppermute(total, Z, [(z, (z + 1 if z % 2 else z - 1) % 8) for z in range(8)])
    there, got = hold((there, got))
    total = total + got
    total = total + lax.ppermute(total, Z, [(z, (z - 3 if z % 2 else z + 3) % 8) for z in range(8)])
    total = total + swap(total, "core", 2, 1)
    mate = add(here[width:], there[width:])
    d_query = call(dquery_kernel, shape(rows, width))(here, there, swap(mate, "core", 2, 1))
    dkv = add(p0, low, high)
    return (d_query, dkv[:, :width], dkv[:, width:], total)


def solution(mesh):
    fine = Mesh(mesh.devices.reshape(4, 2, 2, 2, 2, 4), FRAME + HEAD)
    both = P(FRAME, HEAD)
    return jax.shard_map(
        body,
        mesh=fine,
        in_specs=(both, both, both, P(HEAD, None), P(None, HEAD), both, P(FRAME), P(), P()),
        out_specs=(both, both, both, P(None, HEAD)),
        check_vma=False,
    )
```

```python
import functools
import math

import jax
import jax.numpy as jnp
from jax import lax
from jax.experimental import pallas as pl
from jax.experimental.pallas import tpu as pltpu
from jax.sharding import Mesh, PartitionSpec as P

HDIM = 128
BIG = 1e30
SCALE = HDIM ** (-0.5)
LOG2E = math.log2(math.e)
C2 = SCALE * LOG2E
Z = ("zh", "zl")
FRAME = ("zh", "zl", "xl", "core")
HEAD = ("xh", "y")
FRAME_C = ("xl", "core")
NT = (((1,), (1,)), ((), ()))
NN = (((1,), (0,)), ((), ()))
F32 = jnp.float32
BF16 = jnp.bfloat16
MIB = 1024 * 1024


def dot(a, b, dims):
    return lax.dot_general(a, b, dims, preferred_element_type=F32)


def swap(block, axes, count, by):
    return lax.ppermute(block, axes, [(i, i ^ by) for i in range(count)])


def call(kernel, out_shape, scratch=(), flops=0, nbytes=0, limit=40, loose=()):
    def run(*args):
        specs = [
            pl.BlockSpec(memory_space=pl.ANY if i in loose else pltpu.VMEM)
            for i in range(len(args))
        ]
        return pl.pallas_call(
            kernel,
            out_shape=out_shape,
            in_specs=specs,
            out_specs=jax.tree.map(lambda _: pl.BlockSpec(memory_space=pltpu.VMEM), out_shape),
            scratch_shapes=list(scratch),
            compiler_params=pltpu.CompilerParams(vmem_limit_bytes=limit * MIB),
            cost_estimate=pl.CostEstimate(flops=flops, bytes_accessed=nbytes, transcendentals=0),
        )(*args)

    return run


def shape(rows, cols, dtype=BF16):
    return jax.ShapeDtypeStruct((rows, cols), dtype)


def prep_kernel(key, value, query, grad, gate, ids, mask, step, kv, qb, tok_step, sent):
    rows, width = key.shape
    spans = mask.shape[0]
    levels = gate.shape[0]
    hot_t = (lax.broadcasted_iota(jnp.int32, (rows, rows), 0) == ids[...]).astype(F32)
    hot = hot_t.T.astype(BF16)
    kv[:, :width] = key[...]
    kv[:, width : 2 * width] = value[...]
    kv[:, 2 * width :] = hot
    table = jnp.where(mask[...] == 1, 0.0, -BIG).astype(BF16)
    qb[:, :width] = query[...]
    qb[:, width:] = jnp.zeros((rows, HDIM), BF16)
    qb[:, width : width + spans] = dot(hot[:, :spans], table, NN).astype(BF16)
    step_t = (lax.broadcasted_iota(jnp.int32, (levels, spans), 0) == step[...]).astype(BF16)
    tok_step[...] = dot(hot[:, :spans], step_t, NT).astype(BF16)
    sent[:rows, :] = grad[...]
    sent[rows:, :] = gate[...].astype(BF16)


def near_kernel(query, kv, out):
    out[...] = query[...]


def fetch_weight(me, weight, w_vmem, sems, cols):
    copies = []
    for e in range(8):
        at = pl.multiple_of((me[0] ^ e) * cols, cols)
        copy = pltpu.make_async_copy(weight.at[:, pl.ds(at, cols)], w_vmem.at[e], sems.at[e])
        copy.start()
        copies.append(copy)
    return copies


def by_head(own, y1, y3, y2_near, y2_far):
    tall = y2_near.shape[0]
    low, high = pl.ds(0, tall), pl.ds(tall, tall)
    return [
        own.at[low], y1.at[low], y2_near, y3.at[low],
        own.at[high], y1.at[high], y2_far, y3.at[high],
    ]


def dattn_kernel(me, *refs):
    blocks = by_head(*refs[:5])
    tok_step, weight, out, w_vmem, sems = refs[5:]
    rows, width = out.shape
    copies = fetch_weight(me, weight, w_vmem, sems, blocks[0].shape[1])
    acc = jnp.zeros((rows, width), F32)
    for e in range(8):
        gate_tok = dot(tok_step[...], blocks[e][rows:, :], NN)
        d_proj = (blocks[e][:rows, :].astype(F32) * gate_tok).astype(BF16)
        copies[e].wait()
        acc += dot(d_proj, w_vmem[e], NT)
    out[...] = acc.astype(BF16)


def split3(x):
    hi = x.astype(BF16)
    rest = x - hi.astype(F32)
    mid = rest.astype(BF16)
    low = (rest - mid.astype(F32)).astype(BF16)
    return hi, mid, low


def fwd_kernel(k0, k1, k2, k3, k4, k5, k6, k7, q0, q1, q2, q3, s0, s1, s2, s3, kv, qd, stats):
    rows = q0.shape[0]
    width = q0.shape[1] - HDIM
    heads = width // HDIM
    for i, k in enumerate((k0, k1, k2, k3, k4, k5, k6, k7)):
        kv[i * rows : (i + 1) * rows, :] = k[...]
    for d, q in enumerate((q0, q1, q2, q3)):
        qd[d * rows : (d + 1) * rows, :] = q[...]
    stats[...] = jnp.zeros_like(stats)
    outs = (s0, s1, s2, s3)
    step = 2 * rows
    hot = kv[:, 2 * width :]
    for part in range(2):
        here = slice(part * step, (part + 1) * step)
        bias = dot(hot, qd[here, width:], NT)
        for h in range(heads):
            cols = slice(h * HDIM, (h + 1) * HDIM)
            vcols = slice(width + h * HDIM, width + (h + 1) * HDIM)
            keys = kv[:, cols]
            vals = kv[:, vcols]
            scores = dot(keys, qd[here, cols], NT) + bias
            top = jnp.max(scores, axis=0, keepdims=True)
            probs = jnp.exp2((scores - top) * C2)
            total = jnp.sum(probs, axis=0, keepdims=True)
            acc = dot(vals.T, probs.astype(BF16), NN)
            for i in range(2):
                d = 2 * part + i
                lanes = slice(i * rows, (i + 1) * rows)
                outs[d][cols, :] = acc[:, lanes].astype(BF16)
                stats[d * 8 + h : d * 8 + h + 1, :] = top[:, lanes]
                stats[d * 8 + heads + h : d * 8 + heads + h + 1, :] = total[:, lanes]
    for d, out in enumerate(outs):
        pieces = split3(stats[8 * d : 8 * d + 8, :])
        tail = jnp.concatenate([p.astype(F32) for p in pieces] + [jnp.zeros((8, rows), F32)], axis=0)
        out[width:, :] = tail.astype(BF16)


def merge_kernel(s0, s1, s2, s3, d_attn, attn_t, sent):
    width, rows = attn_t.shape
    heads = width // HDIM
    parts = (s0, s1, s2, s3)
    mine = []
    for s in parts:
        tail = s[width:, :].astype(F32)
        mine.append(tail[0:8] + tail[8:16] + tail[16:24])
    tops = [m[0:heads] for m in mine]
    top = jnp.maximum(jnp.maximum(tops[0], tops[1]), jnp.maximum(tops[2], tops[3]))
    ws = [jnp.exp2((t - top) * C2) for t in tops]
    total = sum(w * m[heads : 2 * heads] for w, m in zip(ws, mine))
    lse = top * C2 + jnp.log(total) * LOG2E
    dattn_t = d_attn[...].astype(F32).T
    deltas = []
    for h in range(heads):
        cols = slice(h * HDIM, (h + 1) * HDIM)
        acc = jnp.zeros((HDIM, rows), F32)
        for w, s in zip(ws, parts):
            acc += s[cols, :].astype(F32) * (w[h : h + 1] / total[h : h + 1])
        rounded = acc.astype(BF16)
        attn_t[cols, :] = rounded
        deltas.append(jnp.sum(rounded.astype(F32) * dattn_t[cols, :], axis=0, keepdims=True))
    stats = jnp.concatenate([lse] + deltas + [jnp.zeros((2, rows), F32)], axis=0)
    pieces = jnp.concatenate([p.astype(F32) for p in split3(stats)], axis=1)
    sent[:rows, :] = d_attn[...]
    sent[rows:, :] = jnp.concatenate([pieces, jnp.zeros_like(pieces)], axis=0).astype(BF16)


def bwd_kernel(count, last, *refs):
    ks = refs[:count]
    qs = refs[count : count + 4]
    owns = refs[count + 4 : count + 8]
    at = count + 8
    if last:
        before = refs[at]
        at += 1
    slots = refs[at : at + count]
    outs = refs[at + count : -4]
    kv, qd, ad, stats = refs[-4:]
    rows = qs[0].shape[0]
    width = qs[0].shape[1] - HDIM
    heads = width // HDIM
    for i, k in enumerate(ks):
        kv[i * rows : (i + 1) * rows, :] = k[...]
    for d, (q, a) in enumerate(zip(qs, owns)):
        lanes = slice(d * rows, (d + 1) * rows)
        qd[lanes, :] = q[...]
        ad[lanes, :] = a[:rows, :]
        tail = a[rows:, :].astype(F32)
        stats[:, lanes] = (tail[0:8, :rows] + tail[0:8, rows : 2 * rows]) + tail[0:8, 2 * rows :]
    step = 2 * rows
    hot = kv[:, 2 * width :]
    biases = [dot(hot, qd[p * step : (p + 1) * step, width:], NT) for p in range(2)]
    for h in range(heads):
        cols = slice(h * HDIM, (h + 1) * HDIM)
        vcols = slice(width + h * HDIM, width + (h + 1) * HDIM)
        keys = kv[:, cols]
        vals = kv[:, vcols]
        keys_t = keys.T
        dkey = None
        dval = None
        for part in range(2):
            here = slice(part * step, (part + 1) * step)
            d = 2 * part
            scores = dot(keys, qd[here, cols], NT) + biases[part]
            probs = jnp.exp2(scores * C2 - stats[h : h + 1, here])
            dprob = dot(vals, ad[here, cols], NT)
            dscore = (probs * (dprob - stats[heads + h : heads + h + 1, here])).astype(BF16)
            dk = dot(dscore, qd[here, cols], NN)
            dv = dot(probs.astype(BF16), ad[here, cols], NN)
            dkey = dk if dkey is None else dkey + dk
            dval = dv if dval is None else dval + dv
            dq = dot(keys_t, dscore, NN)
            if last:
                dq = (dq + before[cols, here]) * SCALE
                low_half = slice(h * HDIM, (h + 1) * HDIM)
                high_half = slice(width + h * HDIM, width + (h + 1) * HDIM)
                outs[part][low_half, :] = dq[:, :rows].astype(BF16)
                outs[part][high_half, :] = dq[:, rows:].astype(BF16)
            else:
                outs[0][cols, here] = dq
        for k, slot in enumerate(slots):
            here = slice(k * rows, (k + 1) * rows)
            slot[:, cols] = (dkey[here] * SCALE).astype(BF16)
            slot[:, vcols] = dval[here].astype(BF16)


def dquery_kernel(here, there, got, out):
    width = here.shape[0] // 2
    acc = here[:width, :].astype(F32) + there[:width, :].astype(F32) + got[...].astype(F32)
    out[...] = acc.T.astype(BF16)


def dgate_kernel(me, *refs):
    blocks = by_head(*refs[:5])
    tok_step, weight, attn_t, out, w_vmem, sems = refs[5:]
    rows = attn_t.shape[1]
    levels = tok_step.shape[1]
    copies = fetch_weight(me, weight, w_vmem, sems, blocks[0].shape[1])
    attn = attn_t[...].astype(F32).T.astype(BF16)
    hot = tok_step[...].astype(F32).T.astype(BF16)
    for e in range(8):
        copies[e].wait()
        proj = dot(attn, w_vmem[e], NN)
        terms = (proj * blocks[e][:rows, :].astype(F32)).astype(BF16)
        out[e * levels : (e + 1) * levels, :] = dot(hot, terms, NN).astype(BF16)


def body(query, key, value, out_weight, gate_table, grad_out, span_ids, span_mask, span_step):
    rows, width = query.shape
    levels, gcols = gate_table.shape
    me = (lax.axis_index("xh") * 4 + lax.axis_index("y")).astype(jnp.int32).reshape(1)
    wide = 2 * width + HDIM
    kv, qb, tok_step, sent = call(
        prep_kernel,
        (shape(rows, wide), shape(rows, width + HDIM), shape(rows, levels),
         shape(rows + levels, gcols)),
        limit=60,
    )(key, value, query, grad_out, gate_table, span_ids.reshape(1, rows), span_mask,
      span_step.reshape(1, -1))
    above = [(z, (z + 1) % 8) for z in range(8)]
    below = [(z, (z - 1) % 8) for z in range(8)]
    tall = rows + levels
    hold = lax.optimization_barrier

    u1, d1 = lax.ppermute(kv, Z, above), lax.ppermute(kv, Z, below)
    gx = swap(sent, "xh", 2, 1)
    qcore = swap(qb, "core", 2, 1)
    u1, qcore = hold((u1, qcore))
    d1, gx = hold((d1, gx))
    u2, d2 = lax.ppermute(u1, Z, above), lax.ppermute(d1, Z, below)
    gown = jnp.concatenate([sent, gx], axis=0)
    gy1, gy3 = swap(gown, "y", 4, 1), swap(gown, "y", 4, 3)
    u2, qcore, qb = hold((u2, qcore, qb))
    u3 = lax.ppermute(u2, Z, above)
    qxl, qdiag = swap(qb, "xl", 2, 1), swap(qcore, "xl", 2, 1)
    u3, d2, gy1, gy3, qxl, qdiag, qb, kv = hold((u3, d2, gy1, gy3, qxl, qdiag, qb, kv))
    u4, d3 = lax.ppermute(u3, Z, above), lax.ppermute(d2, Z, below)
    near, far = swap(gy1[:tall], "y", 4, 3), swap(gy3[tall:], "y", 4, 1)
    q_own = call(near_kernel, shape(rows, width + HDIM))(qb, kv)
    u4, d3, q_own = hold((u4, d3, q_own))
    kvs = (kv, u1, u2, u3, u4, d1, d2, d3)
    qbs = (q_own, qcore, qxl, qdiag)

    def weighted(kernel, out_shape, args, flops):
        specs = [pl.BlockSpec(memory_space=pltpu.SMEM)]
        specs += [pl.BlockSpec(memory_space=pltpu.VMEM)] * 6
        specs += [pl.BlockSpec(memory_space=pl.ANY)]
        specs += [pl.BlockSpec(memory_space=pltpu.VMEM)] * (len(args) - 8)
        return pl.pallas_call(
            kernel,
            out_shape=out_shape,
            in_specs=specs,
            out_specs=pl.BlockSpec(memory_space=pltpu.VMEM),
            scratch_shapes=[
                pltpu.VMEM((8, width, gcols), BF16),
                pltpu.SemaphoreType.DMA((8,)),
            ],
            compiler_params=pltpu.CompilerParams(vmem_limit_bytes=40 * MIB),
            cost_estimate=pl.CostEstimate(
                flops=flops, bytes_accessed=out_weight.size * 2, transcendentals=0
            ),
        )(*args)

    flops = 2 * rows * out_weight.size
    product = 2 * 8 * rows * 4 * rows * width
    parts = call(
        fwd_kernel,
        tuple(shape(width + 32, rows) for _ in range(4)),
        scratch=(
            pltpu.VMEM((8 * rows, wide), BF16),
            pltpu.VMEM((4 * rows, width + HDIM), BF16),
            pltpu.VMEM((32, rows), F32),
        ),
        flops=2 * product,
        nbytes=8 * kv.size * 2,
    )(*kvs, *qbs)
    *parts, near, far = hold((*parts, near, far))
    gblocks = (gown, gy1, gy3, near, far)
    sums = [parts[0]] + [swap(parts[d], FRAME_C, 4, d) for d in range(1, 4)]
    d_attn = weighted(
        dattn_kernel, shape(rows, width), (me, *gblocks, tok_step, out_weight), flops
    )
    attn_t, own = call(merge_kernel, (shape(width, rows), shape(rows + 16, width)))(*sums, d_attn)
    owns = [own] + [swap(own, FRAME_C, 4, d) for d in range(1, 4)]
    terms = weighted(
        dgate_kernel,
        shape(8 * levels, gcols),
        (me, *gblocks, tok_step, out_weight, attn_t),
        flops,
    )
    terms, *owns = hold((terms, *owns))

    def backward(blocks, extra, out_shape):
        count = len(blocks)
        return call(
            functools.partial(bwd_kernel, count, bool(extra)),
            tuple(shape(rows, 2 * width) for _ in range(count)) + out_shape,
            scratch=(
                pltpu.VMEM((count * rows, wide), BF16),
                pltpu.VMEM((4 * rows, width + HDIM), BF16),
                pltpu.VMEM((4 * rows, width), BF16),
                pltpu.VMEM((8, 4 * rows), F32),
            ),
            flops=5 * product * count // 8,
            nbytes=count * kv.size * 2,
        )(*blocks, *qbs, *owns, *extra)

    def add(*blocks):
        return sum(b.astype(F32) for b in blocks).astype(BF16)

    terms = add(terms, swap(terms, "core", 2, 1))
    got = swap(terms[4 * levels :], "xh", 2, 1)
    p4, n3, dq_part = backward((u4, d3), (), (shape(width, 4 * rows, F32),))
    low = lax.ppermute(p4, Z, below)
    high = lax.ppermute(n3, Z, above)
    p0, p1, p2, p3, n1, n2, here, away = backward(
        (kv, u1, u2, u3, d1, d2), (dq_part,), tuple(shape(2 * width, rows) for _ in range(2))
    )
    got, low, high, p3, n2, away = hold((got, low, high, p3, n2, away))

    terms = add(terms[: 4 * levels], got)
    piece = [terms[e * levels : (e + 1) * levels] for e in range(4)]
    low = lax.ppermute(add(low, p3), Z, below)
    high = lax.ppermute(add(high, n2), Z, above)
    got = [swap(piece[e], "y", 4, e) for e in range(1, 4)]
    low, high, *got = hold((low, high, *got))

    total = piece[0].astype(F32) + sum(g.astype(F32) for g in got)
    low = lax.ppermute(add(low, p2), Z, below)
    high = lax.ppermute(add(high, n1), Z, above)
    got = [swap(total, ("zl", "xl"), 4, e) for e in range(1, 4)]
    low, high, *got = hold((low, high, *got))

    total = total + sum(got)
    low = lax.ppermute(add(low, p1), Z, below)
    there = swap(away, "xl", 2, 1)
    got = lax.ppermute(total, Z, [(z, (z + 1 if z % 2 else z - 1) % 8) for z in range(8)])
    there, got = hold((there, got))
    total = total + got
    got = lax.ppermute(total, Z, [(z, (z - 3 if z % 2 else z + 3) % 8) for z in range(8)])
    mate = add(here[width:], there[width:])
    d_query = call(dquery_kernel, shape(rows, width))(here, there, swap(mate, "core", 2, 1))
    dkv = add(p0, low, high)
    got, d_query, dkv = hold((got, d_query, dkv))
    total = total + got
    return (d_query, dkv[:, :width], dkv[:, width:], total)


def solution(mesh):
    fine = Mesh(mesh.devices.reshape(4, 2, 2, 2, 2, 4), FRAME + HEAD)
    both = P(FRAME, HEAD)
    return jax.shard_map(
        body,
        mesh=fine,
        in_specs=(both, both, both, P(HEAD, None), P(None, HEAD), both, P(FRAME), P(), P()),
        out_specs=(both, both, both, P(None, HEAD)),
        check_vma=False,
    )
```

```python
import functools
import math

import jax
import jax.numpy as jnp
from jax import lax
from jax.experimental import pallas as pl
from jax.experimental.pallas import tpu as pltpu
from jax.sharding import Mesh, PartitionSpec as P

HDIM = 128
BIG = 1e30
SCALE = HDIM ** (-0.5)
LOG2E = math.log2(math.e)
C2 = SCALE * LOG2E
Z = ("zh", "zl")
FRAME = ("zh", "zl", "xl", "core")
HEAD = ("xh", "y")
FRAME_C = ("xl", "core")
NT = (((1,), (1,)), ((), ()))
NN = (((1,), (0,)), ((), ()))
F32 = jnp.float32
BF16 = jnp.bfloat16
MIB = 1024 * 1024


def dot(a, b, dims):
    return lax.dot_general(a, b, dims, preferred_element_type=F32)


def swap(block, axes, count, by):
    return lax.ppermute(block, axes, [(i, i ^ by) for i in range(count)])


def call(kernel, out_shape, scratch=(), flops=0, nbytes=0, limit=24):
    def run(*args):
        specs = [pl.BlockSpec(memory_space=pltpu.VMEM)] * len(args)
        return pl.pallas_call(
            kernel,
            out_shape=out_shape,
            in_specs=specs,
            out_specs=jax.tree.map(lambda _: pl.BlockSpec(memory_space=pltpu.VMEM), out_shape),
            scratch_shapes=list(scratch),
            compiler_params=pltpu.CompilerParams(vmem_limit_bytes=limit * MIB),
            cost_estimate=pl.CostEstimate(flops=flops, bytes_accessed=nbytes, transcendentals=0),
        )(*args)

    return run


def shape(rows, cols, dtype=BF16):
    return jax.ShapeDtypeStruct((rows, cols), dtype)


def prep_kernel(key, value, query, grad, gate, ids, mask, step, kv, qb, tok_step, sent):
    rows, width = key.shape
    spans = mask.shape[0]
    levels = gate.shape[0]
    hot_t = (lax.broadcasted_iota(jnp.int32, (rows, rows), 0) == ids[...]).astype(F32)
    hot = hot_t.T.astype(BF16)
    kv[:, :width] = key[...]
    kv[:, width : 2 * width] = value[...]
    kv[:, 2 * width :] = hot
    table = jnp.where(mask[...] == 1, 0.0, -BIG).astype(BF16)
    qb[:, :width] = query[...]
    qb[:, width:] = jnp.zeros((rows, HDIM), BF16)
    qb[:, width : width + spans] = dot(hot[:, :spans], table, NN).astype(BF16)
    step_t = (lax.broadcasted_iota(jnp.int32, (levels, spans), 0) == step[...]).astype(BF16)
    tok_step[...] = dot(hot[:, :spans], step_t, NT).astype(BF16)
    sent[:rows, :] = grad[...]
    sent[rows:, :] = gate[...].astype(BF16)


def fetch_weight(me, weight, w_vmem, sems, cols):
    copies = []
    for e in range(8):
        at = pl.multiple_of((me[0] ^ e) * cols, cols)
        copy = pltpu.make_async_copy(weight.at[:, pl.ds(at, cols)], w_vmem.at[e], sems.at[e])
        copy.start()
        copies.append(copy)
    return copies


def by_head(own, y1, y3, y2_near, y2_far):
    tall = y2_near.shape[0]
    low, high = pl.ds(0, tall), pl.ds(tall, tall)
    return [
        own.at[low], y1.at[low], y2_near, y3.at[low],
        own.at[high], y1.at[high], y2_far, y3.at[high],
    ]


def dattn_kernel(me, *refs):
    blocks = by_head(*refs[:5])
    tok_step, weight, out, w_vmem, sems = refs[5:]
    rows, width = out.shape
    copies = fetch_weight(me, weight, w_vmem, sems, blocks[0].shape[1])
    acc = jnp.zeros((rows, width), F32)
    for e in range(8):
        gate_tok = dot(tok_step[...], blocks[e][rows:, :], NN)
        d_proj = (blocks[e][:rows, :].astype(F32) * gate_tok).astype(BF16)
        copies[e].wait()
        acc += dot(d_proj, w_vmem[e], NT)
    out[...] = acc.astype(BF16)


def split3(x):
    hi = x.astype(BF16)
    rest = x - hi.astype(F32)
    mid = rest.astype(BF16)
    low = (rest - mid.astype(F32)).astype(BF16)
    return hi, mid, low


def fwd_kernel(k0, k1, k2, k3, k4, k5, k6, k7, here, there, s0, s1, s2, s3, kv, qd, stats):
    rows = k0.shape[0]
    width = here.shape[1] - HDIM
    heads = width // HDIM
    for i, k in enumerate((k0, k1, k2, k3, k4, k5, k6, k7)):
        kv[i * rows : (i + 1) * rows, :] = k[...]
    qd[: 2 * rows, :] = here[...]
    qd[2 * rows :, :] = there[...]
    stats[...] = jnp.zeros_like(stats)
    outs = (s0, s1, s2, s3)
    step = 2 * rows
    hot = kv[:, 2 * width :]
    for part in range(2):
        here = slice(part * step, (part + 1) * step)
        bias = dot(hot, qd[here, width:], NT)
        for h in range(heads):
            cols = slice(h * HDIM, (h + 1) * HDIM)
            vcols = slice(width + h * HDIM, width + (h + 1) * HDIM)
            keys = kv[:, cols]
            vals = kv[:, vcols]
            scores = dot(keys, qd[here, cols], NT) + bias
            top = jnp.max(scores, axis=0, keepdims=True)
            probs = jnp.exp2((scores - top) * C2)
            total = jnp.sum(probs, axis=0, keepdims=True)
            acc = dot(vals.T, probs.astype(BF16), NN)
            for i in range(2):
                d = 2 * part + i
                lanes = slice(i * rows, (i + 1) * rows)
                outs[d][cols, :] = acc[:, lanes].astype(BF16)
                stats[d * 8 + h : d * 8 + h + 1, :] = top[:, lanes]
                stats[d * 8 + heads + h : d * 8 + heads + h + 1, :] = total[:, lanes]
    for d, out in enumerate(outs):
        pieces = split3(stats[8 * d : 8 * d + 8, :])
        tail = jnp.concatenate([p.astype(F32) for p in pieces] + [jnp.zeros((8, rows), F32)], axis=0)
        out[width:, :] = tail.astype(BF16)


def merge_kernel(s0, s1, s2, s3, d_attn, attn_t, sent):
    width, rows = attn_t.shape
    heads = width // HDIM
    parts = (s0, s1, s2, s3)
    mine = []
    for s in parts:
        tail = s[width:, :].astype(F32)
        mine.append(tail[0:8] + tail[8:16] + tail[16:24])
    tops = [m[0:heads] for m in mine]
    top = jnp.maximum(jnp.maximum(tops[0], tops[1]), jnp.maximum(tops[2], tops[3]))
    ws = [jnp.exp2((t - top) * C2) for t in tops]
    total = sum(w * m[heads : 2 * heads] for w, m in zip(ws, mine))
    lse = top * C2 + jnp.log(total) * LOG2E
    dattn_t = d_attn[...].astype(F32).T
    deltas = []
    for h in range(heads):
        cols = slice(h * HDIM, (h + 1) * HDIM)
        acc = jnp.zeros((HDIM, rows), F32)
        for w, s in zip(ws, parts):
            acc += s[cols, :].astype(F32) * (w[h : h + 1] / total[h : h + 1])
        rounded = acc.astype(BF16)
        attn_t[cols, :] = rounded
        deltas.append(jnp.sum(rounded.astype(F32) * dattn_t[cols, :], axis=0, keepdims=True))
    stats = jnp.concatenate([lse] + deltas + [jnp.zeros((2, rows), F32)], axis=0)
    pieces = jnp.concatenate([p.astype(F32) for p in split3(stats)], axis=1)
    sent[:rows, :] = d_attn[...]
    sent[rows:, :] = jnp.concatenate([pieces, jnp.zeros_like(pieces)], axis=0).astype(BF16)


def bwd_kernel(count, last, *refs):
    ks = refs[:count]
    here, there = refs[count : count + 2]
    owns = refs[count + 2 : count + 6]
    at = count + 6
    if last:
        before = refs[at]
        at += 1
    slots = refs[at : at + count]
    outs = refs[at + count : -4]
    kv, qd, ad, stats = refs[-4:]
    rows = ks[0].shape[0]
    width = here.shape[1] - HDIM
    heads = width // HDIM
    for i, k in enumerate(ks):
        kv[i * rows : (i + 1) * rows, :] = k[...]
    qd[: 2 * rows, :] = here[...]
    qd[2 * rows :, :] = there[...]
    for d, a in enumerate(owns):
        lanes = slice(d * rows, (d + 1) * rows)
        ad[lanes, :] = a[:rows, :]
        tail = a[rows:, :].astype(F32)
        stats[:, lanes] = (tail[0:8, :rows] + tail[0:8, rows : 2 * rows]) + tail[0:8, 2 * rows :]
    step = 2 * rows
    hot = kv[:, 2 * width :]
    biases = [dot(hot, qd[p * step : (p + 1) * step, width:], NT) for p in range(2)]
    for h in range(heads):
        cols = slice(h * HDIM, (h + 1) * HDIM)
        vcols = slice(width + h * HDIM, width + (h + 1) * HDIM)
        keys = kv[:, cols]
        vals = kv[:, vcols]
        keys_t = keys.T
        dkey = None
        dval = None
        for part in range(2):
            here = slice(part * step, (part + 1) * step)
            d = 2 * part
            scores = dot(keys, qd[here, cols], NT) + biases[part]
            probs = jnp.exp2(scores * C2 - stats[h : h + 1, here])
            dprob = dot(vals, ad[here, cols], NT)
            dscore = (probs * (dprob - stats[heads + h : heads + h + 1, here])).astype(BF16)
            dk = dot(dscore, qd[here, cols], NN)
            dv = dot(probs.astype(BF16), ad[here, cols], NN)
            dkey = dk if dkey is None else dkey + dk
            dval = dv if dval is None else dval + dv
            dq = dot(keys_t, dscore, NN)
            if last:
                dq = (dq + before[cols, here]) * SCALE
                low_half = slice(h * HDIM, (h + 1) * HDIM)
                high_half = slice(width + h * HDIM, width + (h + 1) * HDIM)
                outs[part][low_half, :] = dq[:, :rows].astype(BF16)
                outs[part][high_half, :] = dq[:, rows:].astype(BF16)
            else:
                outs[0][cols, here] = dq
        for k, slot in enumerate(slots):
            here = slice(k * rows, (k + 1) * rows)
            slot[:, cols] = (dkey[here] * SCALE).astype(BF16)
            slot[:, vcols] = dval[here].astype(BF16)


def dquery_kernel(here, there, got, out):
    width = here.shape[0] // 2
    acc = here[:width, :].astype(F32) + there[:width, :].astype(F32) + got[...].astype(F32)
    out[...] = acc.T.astype(BF16)


def dgate_kernel(me, *refs):
    blocks = by_head(*refs[:5])
    tok_step, weight, attn_t, out, w_vmem, sems = refs[5:]
    rows = attn_t.shape[1]
    levels = tok_step.shape[1]
    copies = fetch_weight(me, weight, w_vmem, sems, blocks[0].shape[1])
    attn = attn_t[...].astype(F32).T.astype(BF16)
    hot = tok_step[...].astype(F32).T.astype(BF16)
    for e in range(8):
        copies[e].wait()
        proj = dot(attn, w_vmem[e], NN)
        terms = (proj * blocks[e][:rows, :].astype(F32)).astype(BF16)
        out[e * levels : (e + 1) * levels, :] = dot(hot, terms, NN).astype(BF16)


def body(query, key, value, out_weight, gate_table, grad_out, span_ids, span_mask, span_step):
    rows, width = query.shape
    levels, gcols = gate_table.shape
    me = (lax.axis_index("xh") * 4 + lax.axis_index("y")).astype(jnp.int32).reshape(1)
    wide = 2 * width + HDIM
    kv, qb, tok_step, sent = call(
        prep_kernel,
        (shape(rows, wide), shape(rows, width + HDIM), shape(rows, levels),
         shape(rows + levels, gcols)),
        limit=60,
    )(key, value, query, grad_out, gate_table, span_ids.reshape(1, rows), span_mask,
      span_step.reshape(1, -1))
    above = [(z, (z + 1) % 8) for z in range(8)]
    below = [(z, (z - 1) % 8) for z in range(8)]
    tall = rows + levels
    hold = lax.optimization_barrier

    u1, d1 = lax.ppermute(kv, Z, above), lax.ppermute(kv, Z, below)
    gx = swap(sent, "xh", 2, 1)
    qcore = swap(qb, "core", 2, 1)
    u1, qcore = hold((u1, qcore))
    d1, gx = hold((d1, gx))
    u2, d2 = lax.ppermute(u1, Z, above), lax.ppermute(d1, Z, below)
    gown = jnp.concatenate([sent, gx], axis=0)
    gy1, gy3 = swap(gown, "y", 4, 1), swap(gown, "y", 4, 3)
    u2, qcore = hold((u2, qcore))
    u3 = lax.ppermute(u2, Z, above)
    qhere = jnp.concatenate([qb, qcore], axis=0)
    qthere = swap(qhere, "xl", 2, 1)
    u3, d2, gy1, gy3, qthere = hold((u3, d2, gy1, gy3, qthere))
    u4, d3 = lax.ppermute(u3, Z, above), lax.ppermute(d2, Z, below)
    near, far = swap(gy1[:tall], "y", 4, 3), swap(gy3[tall:], "y", 4, 1)
    u4, d3 = hold((u4, d3))
    kvs = (kv, u1, u2, u3, u4, d1, d2, d3)
    qbs = (qhere, qthere)

    def weighted(kernel, out_shape, args, flops):
        specs = [pl.BlockSpec(memory_space=pltpu.SMEM)]
        specs += [pl.BlockSpec(memory_space=pltpu.VMEM)] * 6
        specs += [pl.BlockSpec(memory_space=pl.ANY)]
        specs += [pl.BlockSpec(memory_space=pltpu.VMEM)] * (len(args) - 8)
        return pl.pallas_call(
            kernel,
            out_shape=out_shape,
            in_specs=specs,
            out_specs=pl.BlockSpec(memory_space=pltpu.VMEM),
            scratch_shapes=[
                pltpu.VMEM((8, width, gcols), BF16),
                pltpu.SemaphoreType.DMA((8,)),
            ],
            compiler_params=pltpu.CompilerParams(vmem_limit_bytes=24 * MIB),
            cost_estimate=pl.CostEstimate(
                flops=flops, bytes_accessed=out_weight.size * 2, transcendentals=0
            ),
        )(*args)

    flops = 2 * rows * out_weight.size
    product = 2 * 8 * rows * 4 * rows * width
    parts = call(
        fwd_kernel,
        tuple(shape(width + 32, rows) for _ in range(4)),
        scratch=(
            pltpu.VMEM((8 * rows, wide), BF16),
            pltpu.VMEM((4 * rows, width + HDIM), BF16),
            pltpu.VMEM((32, rows), F32),
        ),
        flops=2 * product,
        nbytes=8 * kv.size * 2,
    )(*kvs, *qbs)
    *parts, near, far = hold((*parts, near, far))
    gblocks = (gown, gy1, gy3, near, far)
    sums = [parts[0]] + [swap(parts[d], FRAME_C, 4, d) for d in range(1, 4)]
    d_attn = weighted(
        dattn_kernel, shape(rows, width), (me, *gblocks, tok_step, out_weight), flops
    )
    attn_t, own = call(merge_kernel, (shape(width, rows), shape(rows + 16, width)))(*sums, d_attn)
    owns = [own] + [swap(own, FRAME_C, 4, d) for d in range(1, 4)]
    terms = weighted(
        dgate_kernel,
        shape(8 * levels, gcols),
        (me, *gblocks, tok_step, out_weight, attn_t),
        flops,
    )
    terms, *owns = hold((terms, *owns))

    def backward(blocks, extra, out_shape):
        count = len(blocks)
        return call(
            functools.partial(bwd_kernel, count, bool(extra)),
            tuple(shape(rows, 2 * width) for _ in range(count)) + out_shape,
            scratch=(
                pltpu.VMEM((count * rows, wide), BF16),
                pltpu.VMEM((4 * rows, width + HDIM), BF16),
                pltpu.VMEM((4 * rows, width), BF16),
                pltpu.VMEM((8, 4 * rows), F32),
            ),
            flops=5 * product * count // 8,
            nbytes=count * kv.size * 2,
        )(*blocks, *qbs, *owns, *extra)

    def add(*blocks):
        return sum(b.astype(F32) for b in blocks).astype(BF16)

    terms = add(terms, swap(terms, "core", 2, 1))
    got = swap(terms[4 * levels :], "xh", 2, 1)
    p4, n3, dq_part = backward((u4, d3), (), (shape(width, 4 * rows, F32),))
    low = lax.ppermute(p4, Z, below)
    high = lax.ppermute(n3, Z, above)
    p0, p1, p2, p3, n1, n2, here, away = backward(
        (kv, u1, u2, u3, d1, d2), (dq_part,), tuple(shape(2 * width, rows) for _ in range(2))
    )
    got, low, high, p3, n2, away = hold((got, low, high, p3, n2, away))

    terms = add(terms[: 4 * levels], got)
    piece = [terms[e * levels : (e + 1) * levels] for e in range(4)]
    low = lax.ppermute(add(low, p3), Z, below)
    high = lax.ppermute(add(high, n2), Z, above)
    got = [swap(piece[e], "y", 4, e) for e in range(1, 4)]
    low, high, *got = hold((low, high, *got))

    total = piece[0].astype(F32) + sum(g.astype(F32) for g in got)
    low = lax.ppermute(add(low, p2), Z, below)
    high = lax.ppermute(add(high, n1), Z, above)
    got = [swap(total, ("zl", "xl"), 4, e) for e in range(1, 4)]
    low, high, *got = hold((low, high, *got))

    total = total + sum(got)
    low = lax.ppermute(add(low, p1), Z, below)
    there = swap(away, "xl", 2, 1)
    got = lax.ppermute(total, Z, [(z, (z + 1 if z % 2 else z - 1) % 8) for z in range(8)])
    there, got = hold((there, got))
    total = total + got
    got = lax.ppermute(total, Z, [(z, (z - 3 if z % 2 else z + 3) % 8) for z in range(8)])
    mate = add(here[width:], there[width:])
    d_query = call(dquery_kernel, shape(rows, width))(here, there, swap(mate, "core", 2, 1))
    dkv = add(p0, low, high)
    got, d_query, dkv = hold((got, d_query, dkv))
    total = total + got
    return (d_query, dkv[:, :width], dkv[:, width:], total)


def solution(mesh):
    fine = Mesh(mesh.devices.reshape(4, 2, 2, 2, 2, 4), FRAME + HEAD)
    both = P(FRAME, HEAD)
    return jax.shard_map(
        body,
        mesh=fine,
        in_specs=(both, both, both, P(HEAD, None), P(None, HEAD), both, P(FRAME), P(), P()),
        out_specs=(both, both, both, P(None, HEAD)),
        check_vma=False,
    )
```

```python
import functools
import math

import jax
import jax.numpy as jnp
from jax import lax
from jax.experimental import pallas as pl
from jax.experimental.pallas import tpu as pltpu
from jax.sharding import Mesh, PartitionSpec as P

HDIM = 128
BIG = 1e30
SCALE = HDIM ** (-0.5)
LOG2E = math.log2(math.e)
C2 = SCALE * LOG2E
Z = ("zh", "zl")
FRAME = ("zh", "zl", "xl", "core")
HEAD = ("xh", "y")
FRAME_C = ("xl", "core")
NT = (((1,), (1,)), ((), ()))
NN = (((1,), (0,)), ((), ()))
F32 = jnp.float32
BF16 = jnp.bfloat16
MIB = 1024 * 1024


def dot(a, b, dims):
    return lax.dot_general(a, b, dims, preferred_element_type=F32)


def swap(block, axes, count, by):
    return lax.ppermute(block, axes, [(i, i ^ by) for i in range(count)])


def call(kernel, out_shape, scratch=(), flops=0, nbytes=0, limit=24):
    def run(*args):
        specs = [pl.BlockSpec(memory_space=pltpu.VMEM)] * len(args)
        return pl.pallas_call(
            kernel,
            out_shape=out_shape,
            in_specs=specs,
            out_specs=jax.tree.map(lambda _: pl.BlockSpec(memory_space=pltpu.VMEM), out_shape),
            scratch_shapes=list(scratch),
            compiler_params=pltpu.CompilerParams(vmem_limit_bytes=limit * MIB),
            cost_estimate=pl.CostEstimate(flops=flops, bytes_accessed=nbytes, transcendentals=0),
        )(*args)

    return run


def shape(rows, cols, dtype=BF16):
    return jax.ShapeDtypeStruct((rows, cols), dtype)


def prep_kernel(key, value, query, grad, gate, ids, mask, step, kv, qb, tok_step, sent):
    rows, width = key.shape
    spans = mask.shape[0]
    levels = gate.shape[0]
    hot_t = (lax.broadcasted_iota(jnp.int32, (rows, rows), 0) == ids[...]).astype(F32)
    hot = hot_t.T.astype(BF16)
    kv[:, :width] = key[...]
    kv[:, width : 2 * width] = value[...]
    kv[:, 2 * width :] = hot
    table = jnp.where(mask[...] == 1, 0.0, -BIG).astype(BF16)
    qb[:, :width] = query[...]
    qb[:, width:] = jnp.zeros((rows, HDIM), BF16)
    qb[:, width : width + spans] = dot(hot[:, :spans], table, NN).astype(BF16)
    step_t = (lax.broadcasted_iota(jnp.int32, (levels, spans), 0) == step[...]).astype(BF16)
    tok_step[...] = dot(hot[:, :spans], step_t, NT).astype(BF16)
    sent[:rows, :] = grad[...]
    sent[rows:, :] = gate[...].astype(BF16)


def fetch_weight(me, weight, w_vmem, sems, cols):
    copies = []
    for e in range(8):
        at = pl.multiple_of((me[0] ^ e) * cols, cols)
        copy = pltpu.make_async_copy(weight.at[:, pl.ds(at, cols)], w_vmem.at[e], sems.at[e])
        copy.start()
        copies.append(copy)
    return copies


def by_head(own, y1, y3, y2_near, y2_far):
    tall = y2_near.shape[0]
    low, high = pl.ds(0, tall), pl.ds(tall, tall)
    return [
        own.at[low], y1.at[low], y2_near, y3.at[low],
        own.at[high], y1.at[high], y2_far, y3.at[high],
    ]


def dattn_kernel(me, *refs):
    blocks = by_head(*refs[:5])
    tok_step, weight, out, w_vmem, sems = refs[5:]
    rows, width = out.shape
    copies = fetch_weight(me, weight, w_vmem, sems, blocks[0].shape[1])
    acc = jnp.zeros((rows, width), F32)
    for e in range(8):
        gate_tok = dot(tok_step[...], blocks[e][rows:, :], NN)
        d_proj = (blocks[e][:rows, :].astype(F32) * gate_tok).astype(BF16)
        copies[e].wait()
        acc += dot(d_proj, w_vmem[e], NT)
    out[...] = acc.astype(BF16)


def split3(x):
    hi = x.astype(BF16)
    rest = x - hi.astype(F32)
    mid = rest.astype(BF16)
    low = (rest - mid.astype(F32)).astype(BF16)
    return hi, mid, low


def fwd_kernel(k0, k1, k2, k3, k4, k5, k6, k7, here, there, s0, s1, s2, s3, kv, qd, stats):
    rows = k0.shape[0]
    width = here.shape[1] - HDIM
    heads = width // HDIM
    for i, k in enumerate((k0, k1, k2, k3, k4, k5, k6, k7)):
        kv[i * rows : (i + 1) * rows, :] = k[...]
    qd[: 2 * rows, :] = here[...]
    qd[2 * rows :, :] = there[...]
    stats[...] = jnp.zeros_like(stats)
    outs = (s0, s1, s2, s3)
    step = 2 * rows
    hot = kv[:, 2 * width :]
    for part in range(2):
        here = slice(part * step, (part + 1) * step)
        bias = dot(hot, qd[here, width:], NT)
        for h in range(heads):
            cols = slice(h * HDIM, (h + 1) * HDIM)
            vcols = slice(width + h * HDIM, width + (h + 1) * HDIM)
            keys = kv[:, cols]
            vals = kv[:, vcols]
            scores = dot(keys, qd[here, cols], NT) + bias
            top = jnp.max(scores, axis=0, keepdims=True)
            probs = jnp.exp2((scores - top) * C2)
            total = jnp.sum(probs, axis=0, keepdims=True)
            acc = dot(vals.T, probs.astype(BF16), NN)
            for i in range(2):
                d = 2 * part + i
                lanes = slice(i * rows, (i + 1) * rows)
                outs[d][cols, :] = acc[:, lanes].astype(BF16)
                stats[d * 8 + h : d * 8 + h + 1, :] = top[:, lanes]
                stats[d * 8 + heads + h : d * 8 + heads + h + 1, :] = total[:, lanes]
    for d, out in enumerate(outs):
        pieces = split3(stats[8 * d : 8 * d + 8, :])
        tail = jnp.concatenate([p.astype(F32) for p in pieces] + [jnp.zeros((8, rows), F32)], axis=0)
        out[width:, :] = tail.astype(BF16)


def merge_kernel(s0, s1, s2, s3, d_attn, attn_t, sent):
    width, rows = attn_t.shape
    heads = width // HDIM
    parts = (s0, s1, s2, s3)
    mine = []
    for s in parts:
        tail = s[width:, :].astype(F32)
        mine.append(tail[0:8] + tail[8:16] + tail[16:24])
    tops = [m[0:heads] for m in mine]
    top = jnp.maximum(jnp.maximum(tops[0], tops[1]), jnp.maximum(tops[2], tops[3]))
    ws = [jnp.exp2((t - top) * C2) for t in tops]
    total = sum(w * m[heads : 2 * heads] for w, m in zip(ws, mine))
    lse = top * C2 + jnp.log(total) * LOG2E
    dattn_t = d_attn[...].astype(F32).T
    deltas = []
    for h in range(heads):
        cols = slice(h * HDIM, (h + 1) * HDIM)
        acc = jnp.zeros((HDIM, rows), F32)
        for w, s in zip(ws, parts):
            acc += s[cols, :].astype(F32) * (w[h : h + 1] / total[h : h + 1])
        rounded = acc.astype(BF16)
        attn_t[cols, :] = rounded
        deltas.append(jnp.sum(rounded.astype(F32) * dattn_t[cols, :], axis=0, keepdims=True))
    stats = jnp.concatenate([lse] + deltas + [jnp.zeros((2, rows), F32)], axis=0)
    pieces = jnp.concatenate([p.astype(F32) for p in split3(stats)], axis=1)
    sent[:rows, :] = d_attn[...]
    sent[rows:, :] = jnp.concatenate([pieces, jnp.zeros_like(pieces)], axis=0).astype(BF16)


def bwd_kernel(count, last, *refs):
    ks = refs[:count]
    here, there = refs[count : count + 2]
    owns = refs[count + 2 : count + 6]
    at = count + 6
    if last:
        before = refs[at]
        at += 1
    slots = refs[at : at + count]
    outs = refs[at + count : -4]
    kv, qd, ad, stats = refs[-4:]
    rows = ks[0].shape[0]
    width = here.shape[1] - HDIM
    heads = width // HDIM
    for i, k in enumerate(ks):
        kv[i * rows : (i + 1) * rows, :] = k[...]
    qd[: 2 * rows, :] = here[...]
    qd[2 * rows :, :] = there[...]
    for d, a in enumerate(owns):
        lanes = slice(d * rows, (d + 1) * rows)
        ad[lanes, :] = a[:rows, :]
        tail = a[rows:, :].astype(F32)
        stats[:, lanes] = (tail[0:8, :rows] + tail[0:8, rows : 2 * rows]) + tail[0:8, 2 * rows :]
    step = 2 * rows
    hot = kv[:, 2 * width :]
    biases = [dot(hot, qd[p * step : (p + 1) * step, width:], NT) for p in range(2)]
    for h in range(heads):
        cols = slice(h * HDIM, (h + 1) * HDIM)
        vcols = slice(width + h * HDIM, width + (h + 1) * HDIM)
        keys = kv[:, cols]
        vals = kv[:, vcols]
        keys_t = keys.T
        dkey = None
        dval = None
        for part in range(2):
            here = slice(part * step, (part + 1) * step)
            d = 2 * part
            scores = dot(keys, qd[here, cols], NT) + biases[part]
            probs = jnp.exp2(scores * C2 - stats[h : h + 1, here])
            dprob = dot(vals, ad[here, cols], NT)
            dscore = (probs * (dprob - stats[heads + h : heads + h + 1, here])).astype(BF16)
            dk = dot(dscore, qd[here, cols], NN)
            dv = dot(probs.astype(BF16), ad[here, cols], NN)
            dkey = dk if dkey is None else dkey + dk
            dval = dv if dval is None else dval + dv
            dq = dot(keys_t, dscore, NN)
            if last:
                dq = (dq + before[cols, here]) * SCALE
                low_half = slice(h * HDIM, (h + 1) * HDIM)
                high_half = slice(width + h * HDIM, width + (h + 1) * HDIM)
                outs[part][low_half, :] = dq[:, :rows].astype(BF16)
                outs[part][high_half, :] = dq[:, rows:].astype(BF16)
            else:
                outs[0][cols, here] = dq
        for k, slot in enumerate(slots):
            here = slice(k * rows, (k + 1) * rows)
            slot[:, cols] = (dkey[here] * SCALE).astype(BF16)
            slot[:, vcols] = dval[here].astype(BF16)


def dquery_kernel(here, there, got, out):
    width = here.shape[0] // 2
    acc = here[:width, :].astype(F32) + there[:width, :].astype(F32) + got[...].astype(F32)
    out[...] = acc.T.astype(BF16)


def dgate_kernel(me, *refs):
    blocks = by_head(*refs[:5])
    tok_step, weight, attn_t, out, w_vmem, sems = refs[5:]
    rows = attn_t.shape[1]
    levels = tok_step.shape[1]
    copies = fetch_weight(me, weight, w_vmem, sems, blocks[0].shape[1])
    attn = attn_t[...].astype(F32).T.astype(BF16)
    hot = tok_step[...].astype(F32).T.astype(BF16)
    for e in range(8):
        copies[e].wait()
        proj = dot(attn, w_vmem[e], NN)
        terms = (proj * blocks[e][:rows, :].astype(F32)).astype(BF16)
        out[e * levels : (e + 1) * levels, :] = dot(hot, terms, NN).astype(BF16)


def body(query, key, value, out_weight, gate_table, grad_out, span_ids, span_mask, span_step):
    rows, width = query.shape
    levels, gcols = gate_table.shape
    me = (lax.axis_index("xh") * 4 + lax.axis_index("y")).astype(jnp.int32).reshape(1)
    wide = 2 * width + HDIM
    kv, qb, tok_step, sent = call(
        prep_kernel,
        (shape(rows, wide), shape(rows, width + HDIM), shape(rows, levels),
         shape(rows + levels, gcols)),
        limit=60,
    )(key, value, query, grad_out, gate_table, span_ids.reshape(1, rows), span_mask,
      span_step.reshape(1, -1))
    above = [(z, (z + 1) % 8) for z in range(8)]
    below = [(z, (z - 1) % 8) for z in range(8)]
    tall = rows + levels
    hold = lax.optimization_barrier

    u1, d1 = lax.ppermute(kv, Z, above), lax.ppermute(kv, Z, below)
    gx = swap(sent, "xh", 2, 1)
    qcore = swap(qb, "core", 2, 1)
    u1, qcore = hold((u1, qcore))
    d1, gx = hold((d1, gx))
    u2, d2 = lax.ppermute(u1, Z, above), lax.ppermute(d1, Z, below)
    gown = jnp.concatenate([sent, gx], axis=0)
    gy1, gy3 = swap(gown, "y", 4, 1), swap(gown, "y", 4, 3)
    u2, qcore = hold((u2, qcore))
    u3 = lax.ppermute(u2, Z, above)
    qhere = jnp.concatenate([qb, qcore], axis=0)
    qthere = swap(qhere, "xl", 2, 1)
    u3, d2 = hold((u3, d2))
    u4, d3 = lax.ppermute(u3, Z, above), lax.ppermute(d2, Z, below)
    near, far = swap(gy1[:tall], "y", 4, 3), swap(gy3[tall:], "y", 4, 1)
    u4, d3, near, far, qthere = hold((u4, d3, near, far, qthere))
    kvs = (kv, u1, u2, u3, u4, d1, d2, d3)
    qbs = (qhere, qthere)

    def weighted(kernel, out_shape, args, flops):
        specs = [pl.BlockSpec(memory_space=pltpu.SMEM)]
        specs += [pl.BlockSpec(memory_space=pltpu.VMEM)] * 6
        specs += [pl.BlockSpec(memory_space=pl.ANY)]
        specs += [pl.BlockSpec(memory_space=pltpu.VMEM)] * (len(args) - 8)
        return pl.pallas_call(
            kernel,
            out_shape=out_shape,
            in_specs=specs,
            out_specs=pl.BlockSpec(memory_space=pltpu.VMEM),
            scratch_shapes=[
                pltpu.VMEM((8, width, gcols), BF16),
                pltpu.SemaphoreType.DMA((8,)),
            ],
            compiler_params=pltpu.CompilerParams(vmem_limit_bytes=24 * MIB),
            cost_estimate=pl.CostEstimate(
                flops=flops, bytes_accessed=out_weight.size * 2, transcendentals=0
            ),
        )(*args)

    flops = 2 * rows * out_weight.size
    product = 2 * 8 * rows * 4 * rows * width
    parts = call(
        fwd_kernel,
        tuple(shape(width + 32, rows) for _ in range(4)),
        scratch=(
            pltpu.VMEM((8 * rows, wide), BF16),
            pltpu.VMEM((4 * rows, width + HDIM), BF16),
            pltpu.VMEM((32, rows), F32),
        ),
        flops=2 * product,
        nbytes=8 * kv.size * 2,
    )(*kvs, *qbs)
    gblocks = (gown, gy1, gy3, near, far)
    sums = [parts[0]] + [swap(parts[d], FRAME_C, 4, d) for d in range(1, 4)]
    d_attn = weighted(
        dattn_kernel, shape(rows, width), (me, *gblocks, tok_step, out_weight), flops
    )
    attn_t, own = call(merge_kernel, (shape(width, rows), shape(rows + 16, width)))(*sums, d_attn)
    owns = [own] + [swap(own, FRAME_C, 4, d) for d in range(1, 4)]
    terms = weighted(
        dgate_kernel,
        shape(8 * levels, gcols),
        (me, *gblocks, tok_step, out_weight, attn_t),
        flops,
    )
    terms, *owns = hold((terms, *owns))

    def backward(blocks, extra, out_shape):
        count = len(blocks)
        return call(
            functools.partial(bwd_kernel, count, bool(extra)),
            tuple(shape(rows, 2 * width) for _ in range(count)) + out_shape,
            scratch=(
                pltpu.VMEM((count * rows, wide), BF16),
                pltpu.VMEM((4 * rows, width + HDIM), BF16),
                pltpu.VMEM((4 * rows, width), BF16),
                pltpu.VMEM((8, 4 * rows), F32),
            ),
            flops=5 * product * count // 8,
            nbytes=count * kv.size * 2,
        )(*blocks, *qbs, *owns, *extra)

    def add(*blocks):
        return sum(b.astype(F32) for b in blocks).astype(BF16)

    terms = add(terms, swap(terms, "core", 2, 1))
    got = swap(terms[4 * levels :], "xh", 2, 1)
    p4, n3, dq_part = backward((u4, d3), (), (shape(width, 4 * rows, F32),))
    low = lax.ppermute(p4, Z, below)
    high = lax.ppermute(n3, Z, above)
    p0, p1, p2, p3, n1, n2, here, away = backward(
        (kv, u1, u2, u3, d1, d2), (dq_part,), tuple(shape(2 * width, rows) for _ in range(2))
    )
    got, low, high, p3, n2, away = hold((got, low, high, p3, n2, away))

    terms = add(terms[: 4 * levels], got)
    piece = [terms[e * levels : (e + 1) * levels] for e in range(4)]
    low = lax.ppermute(add(low, p3), Z, below)
    high = lax.ppermute(add(high, n2), Z, above)
    got = [swap(piece[e], "y", 4, e) for e in range(1, 4)]
    low, high, *got = hold((low, high, *got))

    total = piece[0].astype(F32) + sum(g.astype(F32) for g in got)
    low = lax.ppermute(add(low, p2), Z, below)
    high = lax.ppermute(add(high, n1), Z, above)
    got = [swap(total, ("zl", "xl"), 4, e) for e in range(1, 4)]
    low, high, *got = hold((low, high, *got))

    total = total + sum(got)
    low = lax.ppermute(add(low, p1), Z, below)
    there = swap(away, "xl", 2, 1)
    got = lax.ppermute(total, Z, [(z, (z + 1 if z % 2 else z - 1) % 8) for z in range(8)])
    there, got = hold((there, got))
    total = total + got
    got = lax.ppermute(total, Z, [(z, (z - 3 if z % 2 else z + 3) % 8) for z in range(8)])
    mate = add(here[width:], there[width:])
    d_query = call(dquery_kernel, shape(rows, width))(here, there, swap(mate, "core", 2, 1))
    dkv = add(p0, low, high)
    got, d_query, dkv = hold((got, d_query, dkv))
    total = total + got
    return (d_query, dkv[:, :width], dkv[:, width:], total)


def solution(mesh):
    fine = Mesh(mesh.devices.reshape(4, 2, 2, 2, 2, 4), FRAME + HEAD)
    both = P(FRAME, HEAD)
    return jax.shard_map(
        body,
        mesh=fine,
        in_specs=(both, both, both, P(HEAD, None), P(None, HEAD), both, P(FRAME), P(), P()),
        out_specs=(both, both, both, P(None, HEAD)),
        check_vma=False,
    )
```

```python
import functools
import math

import jax
import jax.numpy as jnp
from jax import lax
from jax.experimental import pallas as pl
from jax.experimental.pallas import tpu as pltpu
from jax.sharding import Mesh, PartitionSpec as P

HDIM = 128
BIG = 1e30
SCALE = HDIM ** (-0.5)
LOG2E = math.log2(math.e)
C2 = SCALE * LOG2E
Z = ("zh", "zl")
FRAME = ("zh", "zl", "xl", "core")
HEAD = ("xh", "y")
FRAME_C = ("xl", "core")
NT = (((1,), (1,)), ((), ()))
NN = (((1,), (0,)), ((), ()))
F32 = jnp.float32
BF16 = jnp.bfloat16
MIB = 1024 * 1024


def dot(a, b, dims):
    return lax.dot_general(a, b, dims, preferred_element_type=F32)


def swap(block, axes, count, by):
    return lax.ppermute(block, axes, [(i, i ^ by) for i in range(count)])


def call(kernel, out_shape, scratch=(), flops=0, nbytes=0, limit=24):
    def run(*args):
        specs = [pl.BlockSpec(memory_space=pltpu.VMEM)] * len(args)
        return pl.pallas_call(
            kernel,
            out_shape=out_shape,
            in_specs=specs,
            out_specs=jax.tree.map(lambda _: pl.BlockSpec(memory_space=pltpu.VMEM), out_shape),
            scratch_shapes=list(scratch),
            compiler_params=pltpu.CompilerParams(vmem_limit_bytes=limit * MIB),
            cost_estimate=pl.CostEstimate(flops=flops, bytes_accessed=nbytes, transcendentals=0),
        )(*args)

    return run


def shape(rows, cols, dtype=BF16):
    return jax.ShapeDtypeStruct((rows, cols), dtype)


def prep_kernel(key, value, query, grad, gate, ids, mask, step, kv, qb, tok_step, sent):
    rows, width = key.shape
    spans = mask.shape[0]
    levels = gate.shape[0]
    hot_t = (lax.broadcasted_iota(jnp.int32, (rows, rows), 0) == ids[...]).astype(F32)
    hot = hot_t.T.astype(BF16)
    kv[:, :width] = key[...]
    kv[:, width : 2 * width] = value[...]
    kv[:, 2 * width :] = hot
    table = jnp.where(mask[...] == 1, 0.0, -BIG).astype(BF16)
    qb[:, :width] = query[...]
    qb[:, width:] = jnp.zeros((rows, HDIM), BF16)
    qb[:, width : width + spans] = dot(hot[:, :spans], table, NN).astype(BF16)
    step_t = (lax.broadcasted_iota(jnp.int32, (levels, spans), 0) == step[...]).astype(BF16)
    tok_step[...] = dot(hot[:, :spans], step_t, NT).astype(BF16)
    sent[:rows, :] = grad[...]
    sent[rows:, :] = gate[...].astype(BF16)


def fetch_weight(me, weight, w_vmem, sems, cols):
    copies = []
    for e in range(8):
        at = pl.multiple_of((me[0] ^ e) * cols, cols)
        copy = pltpu.make_async_copy(weight.at[:, pl.ds(at, cols)], w_vmem.at[e], sems.at[e])
        copy.start()
        copies.append(copy)
    return copies


def by_head(own, y1, y3, y2_near, y2_far):
    tall = y2_near.shape[0]
    low, high = pl.ds(0, tall), pl.ds(tall, tall)
    return [
        own.at[low], y1.at[low], y2_near, y3.at[low],
        own.at[high], y1.at[high], y2_far, y3.at[high],
    ]


def dattn_kernel(me, *refs):
    blocks = by_head(*refs[:5])
    tok_step, weight, out, w_vmem, sems = refs[5:]
    rows, width = out.shape
    copies = fetch_weight(me, weight, w_vmem, sems, blocks[0].shape[1])
    acc = jnp.zeros((rows, width), F32)
    for e in range(8):
        gate_tok = dot(tok_step[...], blocks[e][rows:, :], NN)
        d_proj = (blocks[e][:rows, :].astype(F32) * gate_tok).astype(BF16)
        copies[e].wait()
        acc += dot(d_proj, w_vmem[e], NT)
    out[...] = acc.astype(BF16)


def split3(x):
    hi = x.astype(BF16)
    rest = x - hi.astype(F32)
    mid = rest.astype(BF16)
    low = (rest - mid.astype(F32)).astype(BF16)
    return hi, mid, low


def fwd_kernel(k0, k1, k2, k3, k4, k5, k6, k7, here, there, s0, s1, s2, s3, kv, qd, stats):
    rows = k0.shape[0]
    width = here.shape[1] - HDIM
    heads = width // HDIM
    for i, k in enumerate((k0, k1, k2, k3, k4, k5, k6, k7)):
        kv[i * rows : (i + 1) * rows, :] = k[...]
    qd[: 2 * rows, :] = here[...]
    qd[2 * rows :, :] = there[...]
    stats[...] = jnp.zeros_like(stats)
    outs = (s0, s1, s2, s3)
    step = 2 * rows
    hot = kv[:, 2 * width :]
    for part in range(2):
        here = slice(part * step, (part + 1) * step)
        bias = dot(hot, qd[here, width:], NT)
        for h in range(heads):
            cols = slice(h * HDIM, (h + 1) * HDIM)
            vcols = slice(width + h * HDIM, width + (h + 1) * HDIM)
            keys = kv[:, cols]
            vals = kv[:, vcols]
            scores = dot(keys, qd[here, cols], NT) + bias
            top = jnp.max(scores, axis=0, keepdims=True)
            probs = jnp.exp2((scores - top) * C2)
            total = jnp.sum(probs, axis=0, keepdims=True)
            acc = dot(vals.T, probs.astype(BF16), NN)
            for i in range(2):
                d = 2 * part + i
                lanes = slice(i * rows, (i + 1) * rows)
                outs[d][cols, :] = acc[:, lanes].astype(BF16)
                stats[d * 8 + h : d * 8 + h + 1, :] = top[:, lanes]
                stats[d * 8 + heads + h : d * 8 + heads + h + 1, :] = total[:, lanes]
    for d, out in enumerate(outs):
        pieces = split3(stats[8 * d : 8 * d + 8, :])
        tail = jnp.concatenate([p.astype(F32) for p in pieces] + [jnp.zeros((8, rows), F32)], axis=0)
        out[width:, :] = tail.astype(BF16)


def merge_kernel(s0, s1, s2, s3, d_attn, attn_t, sent):
    width, rows = attn_t.shape
    heads = width // HDIM
    parts = (s0, s1, s2, s3)
    mine = []
    for s in parts:
        tail = s[width:, :].astype(F32)
        mine.append(tail[0:8] + tail[8:16] + tail[16:24])
    tops = [m[0:heads] for m in mine]
    top = jnp.maximum(jnp.maximum(tops[0], tops[1]), jnp.maximum(tops[2], tops[3]))
    ws = [jnp.exp2((t - top) * C2) for t in tops]
    total = sum(w * m[heads : 2 * heads] for w, m in zip(ws, mine))
    lse = top * C2 + jnp.log(total) * LOG2E
    dattn_t = d_attn[...].astype(F32).T
    deltas = []
    for h in range(heads):
        cols = slice(h * HDIM, (h + 1) * HDIM)
        acc = jnp.zeros((HDIM, rows), F32)
        for w, s in zip(ws, parts):
            acc += s[cols, :].astype(F32) * (w[h : h + 1] / total[h : h + 1])
        rounded = acc.astype(BF16)
        attn_t[cols, :] = rounded
        deltas.append(jnp.sum(rounded.astype(F32) * dattn_t[cols, :], axis=0, keepdims=True))
    stats = jnp.concatenate([lse] + deltas + [jnp.zeros((2, rows), F32)], axis=0)
    pieces = jnp.concatenate([p.astype(F32) for p in split3(stats)], axis=1)
    sent[:rows, :] = d_attn[...]
    sent[rows:, :] = jnp.concatenate([pieces, jnp.zeros_like(pieces)], axis=0).astype(BF16)


def bwd_kernel(count, last, *refs):
    ks = refs[:count]
    here, there = refs[count : count + 2]
    owns = refs[count + 2 : count + 6]
    at = count + 6
    if last:
        before = refs[at]
        at += 1
    slots = refs[at : at + count]
    outs = refs[at + count : -4]
    kv, qd, ad, stats = refs[-4:]
    rows = ks[0].shape[0]
    width = here.shape[1] - HDIM
    heads = width // HDIM
    for i, k in enumerate(ks):
        kv[i * rows : (i + 1) * rows, :] = k[...]
    qd[: 2 * rows, :] = here[...]
    qd[2 * rows :, :] = there[...]
    for d, a in enumerate(owns):
        lanes = slice(d * rows, (d + 1) * rows)
        ad[lanes, :] = a[:rows, :]
        tail = a[rows:, :].astype(F32)
        stats[:, lanes] = (tail[0:8, :rows] + tail[0:8, rows : 2 * rows]) + tail[0:8, 2 * rows :]
    step = 2 * rows
    hot = kv[:, 2 * width :]
    biases = [dot(hot, qd[p * step : (p + 1) * step, width:], NT) for p in range(2)]
    for h in range(heads):
        cols = slice(h * HDIM, (h + 1) * HDIM)
        vcols = slice(width + h * HDIM, width + (h + 1) * HDIM)
        keys = kv[:, cols]
        vals = kv[:, vcols]
        keys_t = keys.T
        dkey = None
        dval = None
        for part in range(2):
            here = slice(part * step, (part + 1) * step)
            d = 2 * part
            scores = dot(keys, qd[here, cols], NT) + biases[part]
            probs = jnp.exp2(scores * C2 - stats[h : h + 1, here])
            dprob = dot(vals, ad[here, cols], NT)
            dscore = (probs * (dprob - stats[heads + h : heads + h + 1, here])).astype(BF16)
            dk = dot(dscore, qd[here, cols], NN)
            dv = dot(probs.astype(BF16), ad[here, cols], NN)
            dkey = dk if dkey is None else dkey + dk
            dval = dv if dval is None else dval + dv
            dq = dot(keys_t, dscore, NN)
            if last:
                dq = (dq + before[cols, here]) * SCALE
                low_half = slice(h * HDIM, (h + 1) * HDIM)
                high_half = slice(width + h * HDIM, width + (h + 1) * HDIM)
                outs[part][low_half, :] = dq[:, :rows].astype(BF16)
                outs[part][high_half, :] = dq[:, rows:].astype(BF16)
            else:
                outs[0][cols, here] = dq
        for k, slot in enumerate(slots):
            here = slice(k * rows, (k + 1) * rows)
            slot[:, cols] = (dkey[here] * SCALE).astype(BF16)
            slot[:, vcols] = dval[here].astype(BF16)


def dquery_kernel(here, there, got, out):
    width = here.shape[0] // 2
    acc = here[:width, :].astype(F32) + there[:width, :].astype(F32) + got[...].astype(F32)
    out[...] = acc.T.astype(BF16)


def dgate_kernel(me, *refs):
    blocks = by_head(*refs[:5])
    tok_step, weight, attn_t, out, w_vmem, sems = refs[5:]
    rows = attn_t.shape[1]
    levels = tok_step.shape[1]
    copies = fetch_weight(me, weight, w_vmem, sems, blocks[0].shape[1])
    attn = attn_t[...].astype(F32).T.astype(BF16)
    hot = tok_step[...].astype(F32).T.astype(BF16)
    for e in range(8):
        copies[e].wait()
        proj = dot(attn, w_vmem[e], NN)
        terms = (proj * blocks[e][:rows, :].astype(F32)).astype(BF16)
        out[e * levels : (e + 1) * levels, :] = dot(hot, terms, NN).astype(BF16)


def body(query, key, value, out_weight, gate_table, grad_out, span_ids, span_mask, span_step):
    rows, width = query.shape
    levels, gcols = gate_table.shape
    me = (lax.axis_index("xh") * 4 + lax.axis_index("y")).astype(jnp.int32).reshape(1)
    wide = 2 * width + HDIM
    kv, qb, tok_step, sent = call(
        prep_kernel,
        (shape(rows, wide), shape(rows, width + HDIM), shape(rows, levels),
         shape(rows + levels, gcols)),
        limit=60,
    )(key, value, query, grad_out, gate_table, span_ids.reshape(1, rows), span_mask,
      span_step.reshape(1, -1))
    above = [(z, (z + 1) % 8) for z in range(8)]
    below = [(z, (z - 1) % 8) for z in range(8)]
    tall = rows + levels
    hold = lax.optimization_barrier

    u1, d1 = lax.ppermute(kv, Z, above), lax.ppermute(kv, Z, below)
    gx = swap(sent, "xh", 2, 1)
    qcore = swap(qb, "core", 2, 1)
    u1, qcore = hold((u1, qcore))
    d1, gx = hold((d1, gx))
    u2, d2 = lax.ppermute(u1, Z, above), lax.ppermute(d1, Z, below)
    gown = jnp.concatenate([sent, gx], axis=0)
    gy1, gy3 = swap(gown, "y", 4, 1), swap(gown, "y", 4, 3)
    u2, qcore = hold((u2, qcore))
    u3 = lax.ppermute(u2, Z, above)
    qhere = jnp.concatenate([qb, qcore], axis=0)
    qthere = swap(qhere, "xl", 2, 1)
    u3, d2, gy1, gy3 = hold((u3, d2, gy1, gy3))
    u4, d3 = lax.ppermute(u3, Z, above), lax.ppermute(d2, Z, below)
    near, far = swap(gy1[:tall], "y", 4, 3), swap(gy3[tall:], "y", 4, 1)
    u4, d3, qthere = hold((u4, d3, qthere))
    kvs = (kv, u1, u2, u3, u4, d1, d2, d3)
    qbs = (qhere, qthere)

    def weighted(kernel, out_shape, args, flops):
        specs = [pl.BlockSpec(memory_space=pltpu.SMEM)]
        specs += [pl.BlockSpec(memory_space=pltpu.VMEM)] * 6
        specs += [pl.BlockSpec(memory_space=pl.ANY)]
        specs += [pl.BlockSpec(memory_space=pltpu.VMEM)] * (len(args) - 8)
        return pl.pallas_call(
            kernel,
            out_shape=out_shape,
            in_specs=specs,
            out_specs=pl.BlockSpec(memory_space=pltpu.VMEM),
            scratch_shapes=[
                pltpu.VMEM((8, width, gcols), BF16),
                pltpu.SemaphoreType.DMA((8,)),
            ],
            compiler_params=pltpu.CompilerParams(vmem_limit_bytes=24 * MIB),
            cost_estimate=pl.CostEstimate(
                flops=flops, bytes_accessed=out_weight.size * 2, transcendentals=0
            ),
        )(*args)

    flops = 2 * rows * out_weight.size
    product = 2 * 8 * rows * 4 * rows * width
    parts = call(
        fwd_kernel,
        tuple(shape(width + 32, rows) for _ in range(4)),
        scratch=(
            pltpu.VMEM((8 * rows, wide), BF16),
            pltpu.VMEM((4 * rows, width + HDIM), BF16),
            pltpu.VMEM((32, rows), F32),
        ),
        flops=2 * product,
        nbytes=8 * kv.size * 2,
    )(*kvs, *qbs)
    *parts, near, far = hold((*parts, near, far))
    gblocks = (gown, gy1, gy3, near, far)
    sums = [parts[0]] + [swap(parts[d], FRAME_C, 4, d) for d in range(1, 4)]
    d_attn = weighted(
        dattn_kernel, shape(rows, width), (me, *gblocks, tok_step, out_weight), flops
    )
    attn_t, own = call(merge_kernel, (shape(width, rows), shape(rows + 16, width)))(*sums, d_attn)
    owns = [own] + [swap(own, FRAME_C, 4, d) for d in range(1, 4)]
    terms = weighted(
        dgate_kernel,
        shape(8 * levels, gcols),
        (me, *gblocks, tok_step, out_weight, attn_t),
        flops,
    )
    terms, *owns = hold((terms, *owns))

    def backward(blocks, extra, out_shape):
        count = len(blocks)
        return call(
            functools.partial(bwd_kernel, count, bool(extra)),
            tuple(shape(rows, 2 * width) for _ in range(count)) + out_shape,
            scratch=(
                pltpu.VMEM((count * rows, wide), BF16),
                pltpu.VMEM((4 * rows, width + HDIM), BF16),
                pltpu.VMEM((4 * rows, width), BF16),
                pltpu.VMEM((8, 4 * rows), F32),
            ),
            flops=5 * product * count // 8,
            nbytes=count * kv.size * 2,
        )(*blocks, *qbs, *owns, *extra)

    def add(*blocks):
        return sum(b.astype(F32) for b in blocks).astype(BF16)

    terms = add(terms, swap(terms, "core", 2, 1))
    got = swap(terms[4 * levels :], "xh", 2, 1)
    p4, n3, dq_part = backward((u4, d3), (), (shape(width, 4 * rows, F32),))
    low = lax.ppermute(p4, Z, below)
    high = lax.ppermute(n3, Z, above)
    p0, p1, p2, p3, n1, n2, here, away = backward(
        (kv, u1, u2, u3, d1, d2), (dq_part,), tuple(shape(2 * width, rows) for _ in range(2))
    )
    got, low, high, p3, n2, away = hold((got, low, high, p3, n2, away))

    terms = add(terms[: 4 * levels], got)
    piece = [terms[e * levels : (e + 1) * levels] for e in range(4)]
    low = lax.ppermute(add(low, p3), Z, below)
    high = lax.ppermute(add(high, n2), Z, above)
    got = [swap(piece[e], "y", 4, e) for e in range(1, 4)]
    low, high, *got = hold((low, high, *got))

    total = piece[0].astype(F32) + sum(g.astype(F32) for g in got)
    low = lax.ppermute(add(low, p2), Z, below)
    high = lax.ppermute(add(high, n1), Z, above)
    got = [swap(total, ("zl", "xl"), 4, e) for e in range(1, 4)]
    low, high, *got = hold((low, high, *got))

    total = total + sum(got)
    low = lax.ppermute(add(low, p1), Z, below)
    there = swap(away, "xl", 2, 1)
    got = lax.ppermute(total, Z, [(z, (z + 1 if z % 2 else z - 1) % 8) for z in range(8)])
    there, got = hold((there, got))
    total = total + got
    got = lax.ppermute(total, Z, [(z, (z - 3 if z % 2 else z + 3) % 8) for z in range(8)])
    mate = add(here[width:], there[width:])
    d_query = call(dquery_kernel, shape(rows, width))(here, there, swap(mate, "core", 2, 1))
    dkv = add(p0, low, high)
    got, d_query, dkv = hold((got, d_query, dkv))
    total = total + got
    return (d_query, dkv[:, :width], dkv[:, width:], total)


def solution(mesh):
    fine = Mesh(mesh.devices.reshape(4, 2, 2, 2, 2, 4), FRAME + HEAD)
    both = P(FRAME, HEAD)
    return jax.shard_map(
        body,
        mesh=fine,
        in_specs=(both, both, both, P(HEAD, None), P(None, HEAD), both, P(FRAME), P(), P()),
        out_specs=(both, both, both, P(None, HEAD)),
        check_vma=False,
    )
```

```python
import functools
import math

import jax
import jax.numpy as jnp
from jax import lax
from jax.experimental import pallas as pl
from jax.experimental.pallas import tpu as pltpu
from jax.sharding import Mesh, PartitionSpec as P

HDIM = 128
BIG = 1e30
SCALE = HDIM ** (-0.5)
LOG2E = math.log2(math.e)
C2 = SCALE * LOG2E
Z = ("zh", "zl")
FRAME = ("zh", "zl", "xl", "core")
HEAD = ("xh", "y")
FRAME_C = ("xl", "core")
NT = (((1,), (1,)), ((), ()))
NN = (((1,), (0,)), ((), ()))
F32 = jnp.float32
BF16 = jnp.bfloat16
MIB = 1024 * 1024


def dot(a, b, dims):
    return lax.dot_general(a, b, dims, preferred_element_type=F32)


def swap(block, axes, count, by):
    return lax.ppermute(block, axes, [(i, i ^ by) for i in range(count)])


def call(kernel, out_shape, scratch=(), flops=0, nbytes=0, limit=24):
    def run(*args):
        specs = [pl.BlockSpec(memory_space=pltpu.VMEM)] * len(args)
        return pl.pallas_call(
            kernel,
            out_shape=out_shape,
            in_specs=specs,
            out_specs=jax.tree.map(lambda _: pl.BlockSpec(memory_space=pltpu.VMEM), out_shape),
            scratch_shapes=list(scratch),
            compiler_params=pltpu.CompilerParams(vmem_limit_bytes=limit * MIB),
            cost_estimate=pl.CostEstimate(flops=flops, bytes_accessed=nbytes, transcendentals=0),
        )(*args)

    return run


def shape(rows, cols, dtype=BF16):
    return jax.ShapeDtypeStruct((rows, cols), dtype)


def prep_kernel(key, value, query, grad, gate, ids, mask, step, kv, qb, tok_step, sent):
    rows, width = key.shape
    spans = mask.shape[0]
    levels = gate.shape[0]
    hot_t = (lax.broadcasted_iota(jnp.int32, (rows, rows), 0) == ids[...]).astype(F32)
    hot = hot_t.T.astype(BF16)
    kv[:, :width] = key[...]
    kv[:, width : 2 * width] = value[...]
    kv[:, 2 * width :] = hot
    table = jnp.where(mask[...] == 1, 0.0, -BIG).astype(BF16)
    qb[:, :width] = query[...]
    qb[:, width:] = jnp.zeros((rows, HDIM), BF16)
    qb[:, width : width + spans] = dot(hot[:, :spans], table, NN).astype(BF16)
    step_t = (lax.broadcasted_iota(jnp.int32, (levels, spans), 0) == step[...]).astype(BF16)
    tok_step[...] = dot(hot[:, :spans], step_t, NT).astype(BF16)
    sent[:rows, :] = grad[...]
    sent[rows:, :] = gate[...].astype(BF16)


def fetch_weight(me, weight, w_vmem, sems, cols):
    copies = []
    for e in range(8):
        at = pl.multiple_of((me[0] ^ e) * cols, cols)
        copy = pltpu.make_async_copy(weight.at[:, pl.ds(at, cols)], w_vmem.at[e], sems.at[e])
        copy.start()
        copies.append(copy)
    return copies


def by_head(own, y1, y3, y2_near, y2_far):
    tall = y2_near.shape[0]
    low, high = pl.ds(0, tall), pl.ds(tall, tall)
    return [
        own.at[low], y1.at[low], y2_near, y3.at[low],
        own.at[high], y1.at[high], y2_far, y3.at[high],
    ]


def dattn_kernel(me, *refs):
    blocks = by_head(*refs[:5])
    tok_step, weight, out, w_vmem, sems = refs[5:]
    rows, width = out.shape
    copies = fetch_weight(me, weight, w_vmem, sems, blocks[0].shape[1])
    acc = jnp.zeros((rows, width), F32)
    for e in range(8):
        gate_tok = dot(tok_step[...], blocks[e][rows:, :], NN)
        d_proj = (blocks[e][:rows, :].astype(F32) * gate_tok).astype(BF16)
        copies[e].wait()
        acc += dot(d_proj, w_vmem[e], NT)
    out[...] = acc.astype(BF16)


def split3(x):
    hi = x.astype(BF16)
    rest = x - hi.astype(F32)
    mid = rest.astype(BF16)
    low = (rest - mid.astype(F32)).astype(BF16)
    return hi, mid, low


def fwd_kernel(k0, k1, k2, k3, k4, k5, k6, k7, here, there, s0, s1, s2, s3, kv, qd, stats):
    rows = k0.shape[0]
    width = here.shape[1] - HDIM
    heads = width // HDIM
    for i, k in enumerate((k0, k1, k2, k3, k4, k5, k6, k7)):
        kv[i * rows : (i + 1) * rows, :] = k[...]
    qd[: 2 * rows, :] = here[...]
    qd[2 * rows :, :] = there[...]
    stats[...] = jnp.zeros_like(stats)
    outs = (s0, s1, s2, s3)
    step = 2 * rows
    hot = kv[:, 2 * width :]
    for part in range(2):
        here = slice(part * step, (part + 1) * step)
        bias = dot(hot, qd[here, width:], NT)
        for h in range(heads):
            cols = slice(h * HDIM, (h + 1) * HDIM)
            vcols = slice(width + h * HDIM, width + (h + 1) * HDIM)
            keys = kv[:, cols]
            vals = kv[:, vcols]
            scores = dot(keys, qd[here, cols], NT) + bias
            top = jnp.max(scores, axis=0, keepdims=True)
            probs = jnp.exp2((scores - top) * C2)
            total = jnp.sum(probs, axis=0, keepdims=True)
            acc = dot(vals.T, probs.astype(BF16), NN)
            for i in range(2):
                d = 2 * part + i
                lanes = slice(i * rows, (i + 1) * rows)
                outs[d][cols, :] = acc[:, lanes].astype(BF16)
                stats[d * 8 + h : d * 8 + h + 1, :] = top[:, lanes]
                stats[d * 8 + heads + h : d * 8 + heads + h + 1, :] = total[:, lanes]
    for d, out in enumerate(outs):
        pieces = split3(stats[8 * d : 8 * d + 8, :])
        tail = jnp.concatenate([p.astype(F32) for p in pieces] + [jnp.zeros((8, rows), F32)], axis=0)
        out[width:, :] = tail.astype(BF16)


def merge_kernel(s0, s1, s2, s3, d_attn, attn_t, sent):
    width, rows = attn_t.shape
    heads = width // HDIM
    parts = (s0, s1, s2, s3)
    mine = []
    for s in parts:
        tail = s[width:, :].astype(F32)
        mine.append(tail[0:8] + tail[8:16] + tail[16:24])
    tops = [m[0:heads] for m in mine]
    top = jnp.maximum(jnp.maximum(tops[0], tops[1]), jnp.maximum(tops[2], tops[3]))
    ws = [jnp.exp2((t - top) * C2) for t in tops]
    total = sum(w * m[heads : 2 * heads] for w, m in zip(ws, mine))
    lse = top * C2 + jnp.log(total) * LOG2E
    dattn_t = d_attn[...].astype(F32).T
    deltas = []
    for h in range(heads):
        cols = slice(h * HDIM, (h + 1) * HDIM)
        acc = jnp.zeros((HDIM, rows), F32)
        for w, s in zip(ws, parts):
            acc += s[cols, :].astype(F32) * (w[h : h + 1] / total[h : h + 1])
        rounded = acc.astype(BF16)
        attn_t[cols, :] = rounded
        deltas.append(jnp.sum(rounded.astype(F32) * dattn_t[cols, :], axis=0, keepdims=True))
    stats = jnp.concatenate([lse] + deltas + [jnp.zeros((2, rows), F32)], axis=0)
    pieces = jnp.concatenate([p.astype(F32) for p in split3(stats)], axis=1)
    sent[:rows, :] = d_attn[...]
    sent[rows:, :] = jnp.concatenate([pieces, jnp.zeros_like(pieces)], axis=0).astype(BF16)


def bwd_kernel(count, last, *refs):
    ks = refs[:count]
    here, there = refs[count : count + 2]
    owns = refs[count + 2 : count + 6]
    at = count + 6
    if last:
        before = refs[at]
        at += 1
    slots = refs[at : at + count]
    outs = refs[at + count : -4]
    kv, qd, ad, stats = refs[-4:]
    rows = ks[0].shape[0]
    width = here.shape[1] - HDIM
    heads = width // HDIM
    for i, k in enumerate(ks):
        kv[i * rows : (i + 1) * rows, :] = k[...]
    qd[: 2 * rows, :] = here[...]
    qd[2 * rows :, :] = there[...]
    for d, a in enumerate(owns):
        lanes = slice(d * rows, (d + 1) * rows)
        ad[lanes, :] = a[:rows, :]
        tail = a[rows:, :].astype(F32)
        stats[:, lanes] = (tail[0:8, :rows] + tail[0:8, rows : 2 * rows]) + tail[0:8, 2 * rows :]
    step = 2 * rows
    hot = kv[:, 2 * width :]
    biases = [dot(hot, qd[p * step : (p + 1) * step, width:], NT) for p in range(2)]
    for h in range(heads):
        cols = slice(h * HDIM, (h + 1) * HDIM)
        vcols = slice(width + h * HDIM, width + (h + 1) * HDIM)
        keys = kv[:, cols]
        vals = kv[:, vcols]
        keys_t = keys.T
        dkey = None
        dval = None
        for part in range(2):
            here = slice(part * step, (part + 1) * step)
            d = 2 * part
            scores = dot(keys, qd[here, cols], NT) + biases[part]
            probs = jnp.exp2(scores * C2 - stats[h : h + 1, here])
            dprob = dot(vals, ad[here, cols], NT)
            dscore = (probs * (dprob - stats[heads + h : heads + h + 1, here])).astype(BF16)
            dk = dot(dscore, qd[here, cols], NN)
            dv = dot(probs.astype(BF16), ad[here, cols], NN)
            dkey = dk if dkey is None else dkey + dk
            dval = dv if dval is None else dval + dv
            dq = dot(keys_t, dscore, NN)
            if last:
                dq = (dq + before[cols, here]) * SCALE
                low_half = slice(h * HDIM, (h + 1) * HDIM)
                high_half = slice(width + h * HDIM, width + (h + 1) * HDIM)
                outs[part][low_half, :] = dq[:, :rows].astype(BF16)
                outs[part][high_half, :] = dq[:, rows:].astype(BF16)
            else:
                outs[0][cols, here] = dq
        for k, slot in enumerate(slots):
            here = slice(k * rows, (k + 1) * rows)
            slot[:, cols] = (dkey[here] * SCALE).astype(BF16)
            slot[:, vcols] = dval[here].astype(BF16)


def dquery_kernel(here, there, got, out):
    width = here.shape[0] // 2
    acc = here[:width, :].astype(F32) + there[:width, :].astype(F32) + got[...].astype(F32)
    out[...] = acc.T.astype(BF16)


def dgate_kernel(me, *refs):
    blocks = by_head(*refs[:5])
    tok_step, weight, attn_t, out, w_vmem, sems = refs[5:]
    rows = attn_t.shape[1]
    levels = tok_step.shape[1]
    copies = fetch_weight(me, weight, w_vmem, sems, blocks[0].shape[1])
    attn = attn_t[...].astype(F32).T.astype(BF16)
    hot = tok_step[...].astype(F32).T.astype(BF16)
    for e in range(8):
        copies[e].wait()
        proj = dot(attn, w_vmem[e], NN)
        terms = (proj * blocks[e][:rows, :].astype(F32)).astype(BF16)
        out[e * levels : (e + 1) * levels, :] = dot(hot, terms, NN).astype(BF16)


def body(query, key, value, out_weight, gate_table, grad_out, span_ids, span_mask, span_step):
    rows, width = query.shape
    levels, gcols = gate_table.shape
    me = (lax.axis_index("xh") * 4 + lax.axis_index("y")).astype(jnp.int32).reshape(1)
    wide = 2 * width + HDIM
    kv, qb, tok_step, sent = call(
        prep_kernel,
        (shape(rows, wide), shape(rows, width + HDIM), shape(rows, levels),
         shape(rows + levels, gcols)),
        limit=60,
    )(key, value, query, grad_out, gate_table, span_ids.reshape(1, rows), span_mask,
      span_step.reshape(1, -1))
    above = [(z, (z + 1) % 8) for z in range(8)]
    below = [(z, (z - 1) % 8) for z in range(8)]
    tall = rows + levels
    hold = lax.optimization_barrier

    u1, d1 = lax.ppermute(kv, Z, above), lax.ppermute(kv, Z, below)
    gx = swap(sent, "xh", 2, 1)
    qcore = swap(qb, "core", 2, 1)
    u1, qcore = hold((u1, qcore))
    d1, gx = hold((d1, gx))
    u2, d2 = lax.ppermute(u1, Z, above), lax.ppermute(d1, Z, below)
    gown = jnp.concatenate([sent, gx], axis=0)
    gy1, gy3 = swap(gown, "y", 4, 1), swap(gown, "y", 4, 3)
    u2, qcore = hold((u2, qcore))
    u3 = lax.ppermute(u2, Z, above)
    qhere = jnp.concatenate([qb, qcore], axis=0)
    qthere = swap(qhere, "xl", 2, 1)
    u3, d2, gy1, gy3, kv = hold((u3, d2, gy1, gy3, kv))
    u4, d3 = lax.ppermute(u3, Z, above), lax.ppermute(d2, Z, below)
    near, far = swap(gy1[:tall], "y", 4, 3), swap(gy3[tall:], "y", 4, 1)
    kv = jnp.minimum(kv, jnp.asarray(BIG, BF16))
    u4, d3, qthere, kv = hold((u4, d3, qthere, kv))
    kvs = (kv, u1, u2, u3, u4, d1, d2, d3)
    qbs = (qhere, qthere)

    def weighted(kernel, out_shape, args, flops):
        specs = [pl.BlockSpec(memory_space=pltpu.SMEM)]
        specs += [pl.BlockSpec(memory_space=pltpu.VMEM)] * 6
        specs += [pl.BlockSpec(memory_space=pl.ANY)]
        specs += [pl.BlockSpec(memory_space=pltpu.VMEM)] * (len(args) - 8)
        return pl.pallas_call(
            kernel,
            out_shape=out_shape,
            in_specs=specs,
            out_specs=pl.BlockSpec(memory_space=pltpu.VMEM),
            scratch_shapes=[
                pltpu.VMEM((8, width, gcols), BF16),
                pltpu.SemaphoreType.DMA((8,)),
            ],
            compiler_params=pltpu.CompilerParams(vmem_limit_bytes=24 * MIB),
            cost_estimate=pl.CostEstimate(
                flops=flops, bytes_accessed=out_weight.size * 2, transcendentals=0
            ),
        )(*args)

    flops = 2 * rows * out_weight.size
    product = 2 * 8 * rows * 4 * rows * width
    parts = call(
        fwd_kernel,
        tuple(shape(width + 32, rows) for _ in range(4)),
        scratch=(
            pltpu.VMEM((8 * rows, wide), BF16),
            pltpu.VMEM((4 * rows, width + HDIM), BF16),
            pltpu.VMEM((32, rows), F32),
        ),
        flops=2 * product,
        nbytes=8 * kv.size * 2,
    )(*kvs, *qbs)
    *parts, near, far = hold((*parts, near, far))
    gblocks = (gown, gy1, gy3, near, far)
    sums = [parts[0]] + [swap(parts[d], FRAME_C, 4, d) for d in range(1, 4)]
    d_attn = weighted(
        dattn_kernel, shape(rows, width), (me, *gblocks, tok_step, out_weight), flops
    )
    attn_t, own = call(merge_kernel, (shape(width, rows), shape(rows + 16, width)))(*sums, d_attn)
    owns = [own] + [swap(own, FRAME_C, 4, d) for d in range(1, 4)]
    terms = weighted(
        dgate_kernel,
        shape(8 * levels, gcols),
        (me, *gblocks, tok_step, out_weight, attn_t),
        flops,
    )
    terms, *owns = hold((terms, *owns))

    def backward(blocks, extra, out_shape):
        count = len(blocks)
        return call(
            functools.partial(bwd_kernel, count, bool(extra)),
            tuple(shape(rows, 2 * width) for _ in range(count)) + out_shape,
            scratch=(
                pltpu.VMEM((count * rows, wide), BF16),
                pltpu.VMEM((4 * rows, width + HDIM), BF16),
                pltpu.VMEM((4 * rows, width), BF16),
                pltpu.VMEM((8, 4 * rows), F32),
            ),
            flops=5 * product * count // 8,
            nbytes=count * kv.size * 2,
        )(*blocks, *qbs, *owns, *extra)

    def add(*blocks):
        return sum(b.astype(F32) for b in blocks).astype(BF16)

    terms = add(terms, swap(terms, "core", 2, 1))
    got = swap(terms[4 * levels :], "xh", 2, 1)
    p4, n3, dq_part = backward((u4, d3), (), (shape(width, 4 * rows, F32),))
    low = lax.ppermute(p4, Z, below)
    high = lax.ppermute(n3, Z, above)
    p0, p1, p2, p3, n1, n2, here, away = backward(
        (kv, u1, u2, u3, d1, d2), (dq_part,), tuple(shape(2 * width, rows) for _ in range(2))
    )
    got, low, high, p3, n2, away = hold((got, low, high, p3, n2, away))

    terms = add(terms[: 4 * levels], got)
    piece = [terms[e * levels : (e + 1) * levels] for e in range(4)]
    low = lax.ppermute(add(low, p3), Z, below)
    high = lax.ppermute(add(high, n2), Z, above)
    got = [swap(piece[e], "y", 4, e) for e in range(1, 4)]
    low, high, *got = hold((low, high, *got))

    total = piece[0].astype(F32) + sum(g.astype(F32) for g in got)
    low = lax.ppermute(add(low, p2), Z, below)
    high = lax.ppermute(add(high, n1), Z, above)
    got = [swap(total, ("zl", "xl"), 4, e) for e in range(1, 4)]
    low, high, *got = hold((low, high, *got))

    total = total + sum(got)
    low = lax.ppermute(add(low, p1), Z, below)
    there = swap(away, "xl", 2, 1)
    got = lax.ppermute(total, Z, [(z, (z + 1 if z % 2 else z - 1) % 8) for z in range(8)])
    there, got = hold((there, got))
    total = total + got
    got = lax.ppermute(total, Z, [(z, (z - 3 if z % 2 else z + 3) % 8) for z in range(8)])
    mate = add(here[width:], there[width:])
    d_query = call(dquery_kernel, shape(rows, width))(here, there, swap(mate, "core", 2, 1))
    dkv = add(p0, low, high)
    got, d_query, dkv = hold((got, d_query, dkv))
    total = total + got
    return (d_query, dkv[:, :width], dkv[:, width:], total)


def solution(mesh):
    fine = Mesh(mesh.devices.reshape(4, 2, 2, 2, 2, 4), FRAME + HEAD)
    both = P(FRAME, HEAD)
    return jax.shard_map(
        body,
        mesh=fine,
        in_specs=(both, both, both, P(HEAD, None), P(None, HEAD), both, P(FRAME), P(), P()),
        out_specs=(both, both, both, P(None, HEAD)),
        check_vma=False,
    )
```
